32 devices in a mesh: user: 4 (over z), cand: 8 (over y, x, core).
Axes of the slice: x: 2, y: 2, z: 4, core: 2. Of those that a mesh axis runs over, the one named last changes fastest.
Arguments:
- cand_x: bfloat16 [16384, 1024], P(('user', 'cand')), may hold values from -6 to 6
- cand_user: int32 [16384, 1], P(('user', 'cand')), may hold values from 0 to 7; in each aligned block of 512 rows (0 to 511, 512 to 1023, ...) at most 128 rows name the same one
- visible: int32 [16384], P(('user', 'cand')), may hold values from 1 to 8
- hist_len: int32 [8], P('cand'), may hold values from 1 to 1024
- kv_cache: bfloat16 [8, 1024, 2048], P('cand', 'user'), may hold values from -6 to 6
- w_in: bfloat16 [1024, 2048], replicated, may hold values from -0.1875 to 0.1875
- w_out: bfloat16 [1024, 1024], replicated, may hold values from -0.1875 to 0.1875
- ln_gain: float32 [1024], replicated, may hold values from 0.1 to 1.9
Outputs:
- scored: bfloat16 [16384, 1024], P(('user', 'cand'))
The draws below stay inside these ranges and needn't reach their ends.
Inputs may be any that keep to these rules, and one draw needn't show every extreme that they name: `cand_user`: among the 512 candidates of one device no user is named more than 128 times, a bound that some block reaches.
All inputs are finite; a program needn't handle non-finite values.
Results may differ from the reference program's by a relative error of at most 0.0055.
Values may be sent and summed in bfloat16 or wider, within the bound.
No kernel may reach another device: no remote copies, remote signals or barrier semaphores. Data moves between devices by JAX's collectives and lax.ppermute only.
A program may use at most 128 MiB of HBM per device.

```python
import math
import jax
import jax.numpy as jnp
import numpy as np
from jax import lax

D = 1024
HEADS = 8
BLK = 128
CAND_DEV = 512
HIST = 1024
HB = 8
USERS = 8
CANDS = 16384
CAP = 128


def place_ends(array, key, least, largest):
    place = [jax.random.randint(jax.random.fold_in(key, axis), (), 0, length) for axis, length in enumerate(array.shape)]
    longest = array.shape.index(max(array.shape))
    next_to = place[:longest] + [(place[longest] + 1) % array.shape[longest]] + place[longest + 1:]
    return array.at[tuple(place)].set(least).at[tuple(next_to)].set(largest)


def levels(rng, extent, cuts, least, largest):
    def one(dim, shards_of):
        draws = jax.random.uniform(jax.random.fold_in(jax.random.fold_in(rng, 6), dim), (shards_of,), jnp.float32, least / len(cuts), largest / len(cuts))
        return jnp.repeat(jnp.exp(draws), extent[dim] // shards_of).reshape((-1,) + (1,) * (len(extent) - dim - 1))

    factor_of = one(*cuts[0])
    for cut in cuts[1:]:
        factor_of = factor_of * one(*cut)
    return factor_of


def deal_out(own_key, own, number, rows, count, top, reach, slope):
    order = jax.random.permutation(own_key, count)
    crowded, ordinary = shares(count, rows * top, reach, slope, True), shares(count, rows * top, reach, slope, False)
    places = jnp.arange(count)

    def named(lengths, turn):
        used = int((lengths > 0).sum())
        fixed = max(1, used // 4)
        shifted = fixed + (places - fixed + turn * (used - fixed)) % max(1, count - fixed)
        return jnp.zeros((count,), jnp.int32).at[order[jnp.where(places < fixed, places, shifted)]].set(jnp.asarray(lengths, jnp.int32))

    lengths = jnp.where(number % 4 == 0, named(crowded, number // 4), named(ordinary, number - number // 4 - 1))
    mixed = jax.random.permutation(jax.random.fold_in(own, 3), count)
    source_of, sink = mixed[0:count // 2 * 2:2], mixed[1:count // 2 * 2:2]
    slack = jnp.minimum(lengths[source_of] - 1, reach - lengths[sink]) // 2
    slack = jnp.where((source_of == order[0]) | (sink == order[0]) | (lengths[sink] == 0), 0, jnp.maximum(slack, 0))
    shifted = jax.random.randint(jax.random.fold_in(own, 4), (count // 2,), 0, 1 << 20) % (slack + 1)
    lengths = lengths.at[source_of].add(-shifted).at[sink].add(shifted)
    items = jnp.searchsorted(jnp.cumsum(lengths), jnp.arange(rows * top), side="right").astype(jnp.int32)
    table = items.reshape(top, rows).T
    table = table[jax.random.permutation(jax.random.fold_in(own, 1), rows)]
    turn = jax.random.randint(jax.random.fold_in(own, 2), (rows, 1), 0, top)
    return jnp.take_along_axis(table, (jnp.arange(top)[None, :] + turn) % top, axis=1)


def shares(amount, total, most, skew, full):
    loads = [(1 << 20) // math.isqrt(grade ** skew) + 1 for grade in range(1, amount + 1)]
    largest = most if full else min(most, max(-(-total // amount), total * loads[0] // sum(loads)))
    least = 1 if total - largest >= amount - 1 else 0
    given, spare = [largest] + [least] * (amount - 1), total - largest - least * (amount - 1)
    while spare > 0:
        free = [i for i in range(1, amount) if given[i] < largest] or [i for i in range(1, amount) if given[i] < most]
        whole, remaining = sum([loads[i] for i in free]), spare
        for i in free:
            extra = min(most - given[i], max(1, remaining * loads[i] // whole), spare)
            given[i] = given[i] + extra
            spare = spare - extra
    return np.array(given)


def normal_values(key, shape, scale, most, pieces=(), held_as=jnp.bfloat16):
    gain = levels(key, shape, pieces, -0.22, 0.18) if pieces else 1.0
    values = jax.random.normal(key, shape, jnp.float32) * scale * gain
    return jnp.minimum(jnp.maximum(values, -most), most).astype(held_as)


def setup_inputs(seed: int = 0) -> dict:
    arg_keys = jax.random.split(jax.random.key(seed), 9)
    cand_x = normal_values(arg_keys[0], (CANDS, D), 1.0, 6.0, ((0, 32),))
    cand_user_keys = jax.random.split(jax.random.fold_in(arg_keys[1], 1), CANDS // CAND_DEV)
    cand_user_turns = jax.random.permutation(jax.random.fold_in(arg_keys[1], 3), CANDS // CAND_DEV)
    cand_user = jax.vmap(lambda own, number: deal_out(jax.random.fold_in(arg_keys[1], 2), own, number, CAND_DEV, USERS, 1, CAP, 2))(cand_user_keys, cand_user_turns).reshape((CANDS, 1))
    visible = place_ends(jax.random.randint(arg_keys[2], (CANDS,), 1, HB + 1), jax.random.fold_in(arg_keys[2], 1), 1, HB).astype(jnp.int32)
    hist_len = place_ends(jax.random.randint(arg_keys[3], (USERS,), 1, HIST + 1), jax.random.fold_in(arg_keys[3], 1), 1, HIST).astype(jnp.int32)
    kv_cache = normal_values(arg_keys[4], (USERS, HIST, 2 * D), 1.0, 6.0, ((0, 8), (1, 4)))
    w_in = normal_values(arg_keys[5], (D, 2 * D), D ** -0.5, 0.1875)
    w_out = normal_values(arg_keys[6], (D, D), D ** -0.5, 0.1875)
    ln_gain = jnp.clip(1.0 + 0.18 * jax.random.normal(arg_keys[7], (D,), jnp.float32), 0.1, 1.9)
    return dict(cand_x=cand_x, cand_user=cand_user, visible=visible, hist_len=hist_len, kv_cache=kv_cache, w_in=w_in, w_out=w_out, ln_gain=ln_gain)


def reference(cand_x, cand_user, visible, hist_len, kv_cache, w_in, w_out, ln_gain):
    width = cand_x.shape[1]
    head_size = width // HEADS
    scale = 1.0 / math.sqrt(head_size)
    hidden = jax.nn.silu(jnp.dot(cand_x, w_in, preferred_element_type=jnp.float32))
    queries = hidden[:, :width].astype(jnp.bfloat16)
    gate = hidden[:, width:].astype(jnp.bfloat16)
    owner = cand_user[:, 0].astype(jnp.int32)
    order = jnp.argsort(owner, stable=True).astype(jnp.int32)
    sorted_rows = queries[order]
    sorted_owner = owner[order]
    sorted_vis = visible[order]
    block_rows = min(512, CANDS)
    positions = jnp.arange(HIST, dtype=jnp.int32).astype(jnp.float32)

    def one_block(packed):
        rows_part, owner_part, vis_part = packed
        query_heads = rows_part.astype(jnp.float32).reshape(block_rows, HEADS, head_size)

        def per_user(user_id, partial_value):
            history = lax.dynamic_index_in_dim(kv_cache, user_id, 0, keepdims=False)
            keys = history[:, :width].astype(jnp.float32).reshape(HIST, HEADS, head_size)
            values = history[:, width:].astype(jnp.float32).reshape(HIST, HEADS, head_size)
            limit = jnp.minimum(hist_len[user_id].astype(jnp.float32), BLK * vis_part.astype(jnp.float32))
            limit = jnp.where(owner_part == user_id, limit, jnp.float32(0.0))
            scores = jnp.einsum('bhd,nhd->hbn', query_heads, keys)
            visible_mask = (positions[None, :] < limit[:, None]).astype(jnp.float32)
            weights = (jax.nn.silu(scores * scale) * visible_mask[None]).astype(jnp.bfloat16)
            weights = lax.optimization_barrier(weights).astype(jnp.float32)
            mixed = jnp.einsum('hbn,nhd->bhd', weights, values)
            return partial_value + mixed.reshape(block_rows, width)
        first_user = owner_part[0].astype(jnp.int32)
        last_user = owner_part[block_rows - 1].astype(jnp.int32) + 1
        return lax.fori_loop(first_user, last_user, per_user, jnp.zeros((block_rows, width), jnp.float32))
    blocks = lax.map(one_block, (sorted_rows.reshape(-1, block_rows, width), sorted_owner.reshape(-1, block_rows), sorted_vis.reshape(-1, block_rows)))
    attn_sorted = blocks.reshape(CANDS, width)
    attn = jnp.zeros_like(attn_sorted).at[order].set(attn_sorted)
    mean_row = lax.optimization_barrier(jnp.mean(attn, axis=1, keepdims=True))
    centered = attn - mean_row
    variance = lax.optimization_barrier(jnp.mean(centered * centered, axis=1, keepdims=True))
    normed = (centered * lax.rsqrt(variance + 1e-06) * ln_gain.astype(jnp.float32)).astype(jnp.bfloat16)
    mixed_rows = (normed.astype(jnp.float32) * gate.astype(jnp.float32)).astype(jnp.bfloat16)
    projected = jnp.dot(mixed_rows, w_out, preferred_element_type=jnp.float32)
    return (cand_x.astype(jnp.float32) + projected).astype(jnp.bfloat16)
```

```python
import functools
import math

import jax
import jax.numpy as jnp
from jax import lax
from jax.experimental import pallas as pl
from jax.experimental.pallas import tpu as pltpu
from jax.sharding import PartitionSpec as P

HEADS = 8
BLK = 128
GROUPS = (2, 2, 2, 2)
norm_eps = 1e-06
F32 = jnp.float32
BF16 = jnp.bfloat16
VMEM_BYTES = 40 * 1024 * 1024


def params():
    return pltpu.CompilerParams(vmem_limit_bytes=VMEM_BYTES)


def cost(flops, nbytes, transcendentals=0):
    return pl.CostEstimate(
        flops=int(flops), bytes_accessed=int(nbytes), transcendentals=int(transcendentals)
    )


def silu(v):
    half = 0.5 * v
    return half * jnp.tanh(half) + half


def earlier_mask(rows):
    first = lax.broadcasted_iota(jnp.int32, (rows, rows), 0)
    second = lax.broadcasted_iota(jnp.int32, (rows, rows), 1)
    return (first < second).astype(BF16)


def slot_row(owner_row, columns, capacity):
    rows = owner_row.shape[1]
    users = lax.broadcasted_iota(jnp.int32, (columns, rows), 0)
    mine = users == owner_row
    before = jnp.dot(mine.astype(BF16), earlier_mask(rows), preferred_element_type=F32)
    rank = jnp.sum(jnp.where(mine, before, 0.0), axis=0, keepdims=True)
    return owner_row.astype(F32) * capacity + rank


def query_kernel(columns, capacity, owner_ref, x_ref, w_ref, send_ref, place):
    rows = x_ref.shape[0]
    slots = send_ref.shape[0]

    @pl.when(pl.program_id(0) == 0)
    def _():
        slot = slot_row(owner_ref[...], columns, capacity).astype(jnp.int32)
        index = lax.broadcasted_iota(jnp.int32, (slots, rows), 0)
        place[...] = (index == slot).astype(BF16)

    queries = silu(jnp.dot(x_ref[...], w_ref[...], preferred_element_type=F32)).astype(BF16)
    send_ref[...] = jnp.dot(place[...], queries, preferred_element_type=F32).astype(BF16)


def project_queries(owner_row, cand_x, w_in, columns, capacity):
    rows, width = cand_x.shape
    slots = columns * capacity
    tile = min(256, width)
    return pl.pallas_call(
        functools.partial(query_kernel, columns, capacity),
        grid=(width // tile,),
        in_specs=[
            pl.BlockSpec((1, rows), lambda i: (0, 0)),
            pl.BlockSpec((rows, width), lambda i: (0, 0)),
            pl.BlockSpec((width, tile), lambda i: (0, i)),
        ],
        out_specs=pl.BlockSpec((slots, tile), lambda i: (0, i)),
        out_shape=jax.ShapeDtypeStruct((slots, width), BF16),
        scratch_shapes=[pltpu.VMEM((slots, rows), BF16)],
        compiler_params=params(),
        cost_estimate=cost(
            2 * rows * width * width + 2 * slots * rows * width,
            2 * (rows * width + width * width + slots * width),
            rows * width,
        ),
        name="project_queries",
    )(owner_row, cand_x, w_in)


def gate_kernel(columns, capacity, owner_ref, x_ref, w_ref, gate_ref, slot_ref):
    @pl.when(pl.program_id(0) == 0)
    def _():
        slot = slot_row(owner_ref[...], columns, capacity)
        slot_ref[...] = jnp.broadcast_to(slot, (BLK, slot.shape[1])).T.astype(jnp.int32)

    hidden = jnp.dot(x_ref[...], w_ref[...], preferred_element_type=F32)
    gate_ref[...] = silu(hidden).astype(BF16)


def project_gate(owner_row, cand_x, w_in, columns, capacity):
    rows, width = cand_x.shape
    tile = min(256, width)
    first = width // tile
    return pl.pallas_call(
        functools.partial(gate_kernel, columns, capacity),
        grid=(first,),
        in_specs=[
            pl.BlockSpec((1, rows), lambda i: (0, 0)),
            pl.BlockSpec((rows, width), lambda i: (0, 0)),
            pl.BlockSpec((width, tile), lambda i: (0, first + i)),
        ],
        out_specs=[
            pl.BlockSpec((rows, tile), lambda i: (0, i)),
            pl.BlockSpec((rows, BLK), lambda i: (0, 0)),
        ],
        out_shape=[
            jax.ShapeDtypeStruct((rows, width), BF16),
            jax.ShapeDtypeStruct((rows, BLK), jnp.int32),
        ],
        compiler_params=params(),
        cost_estimate=cost(
            2 * rows * width * width, 2 * (2 * rows * width + width * width), rows * width
        ),
        name="project_gate",
    )(owner_row, cand_x, w_in)


def limits_kernel(capacity, scalars_ref, owner_ref, visible_ref, limit_ref):
    user, length = scalars_ref[0], scalars_ref[1]
    sources, rows = owner_ref.shape
    mine = owner_ref[...] == user
    rank = jnp.dot(mine.astype(BF16), earlier_mask(rows), preferred_element_type=F32)
    slot = jnp.where(mine, rank, -1.0).astype(jnp.int32)
    index = lax.broadcasted_iota(jnp.int32, (capacity, rows), 0)
    seen = visible_ref[...].astype(F32).astype(BF16)
    for source in range(sources):
        pick = (index == slot[source : source + 1, :]).astype(BF16)
        spread = jnp.broadcast_to(seen[source : source + 1, :], (BLK, rows))
        blocks = lax.dot_general(pick, spread, (((1,), (1,)), ((), ())), preferred_element_type=F32)
        limit_ref[source * capacity : (source + 1) * capacity, :] = jnp.minimum(
            blocks.astype(jnp.int32) * BLK, length
        )


def slot_limits(user, length, owners, seen, capacity):
    sources, rows = owners.shape
    slots = sources * capacity
    scalars = jnp.stack([user, length]).astype(jnp.int32)
    return pl.pallas_call(
        functools.partial(limits_kernel, capacity),
        in_specs=[
            pl.BlockSpec(memory_space=pltpu.SMEM),
            pl.BlockSpec(memory_space=pltpu.VMEM),
            pl.BlockSpec(memory_space=pltpu.VMEM),
        ],
        out_specs=pl.BlockSpec(memory_space=pltpu.VMEM),
        out_shape=jax.ShapeDtypeStruct((slots, BLK), jnp.int32),
        compiler_params=params(),
        cost_estimate=cost(2 * slots * rows * BLK, 4 * (slots * BLK + 2 * sources * rows)),
        name="slot_limits",
    )(scalars, owners, seen)


def attend_kernel(heads, size, shard_ref, query_ref, limit_ref, *refs):
    pieces, out_ref = refs[:-1], refs[-1]
    half_scale = 0.5 / math.sqrt(size)
    rows = query_ref.shape[0]
    keys = pieces[0].shape[0]
    wide = heads * size
    lane = lax.broadcasted_iota(jnp.int32, (1, BLK), 1)
    totals = [None] * heads
    for number, piece in enumerate(pieces):
        left = limit_ref[...] - shard_ref[number] * keys
        open_ = jnp.concatenate(
            [lane + start < left for start in range(0, keys, BLK)], axis=1
        )
        for head in range(heads):
            lo, hi = head * size, (head + 1) * size
            scores = lax.dot_general(
                query_ref[:, lo:hi],
                piece[:, lo:hi],
                (((1,), (1,)), ((), ())),
                preferred_element_type=F32,
            )
            half = scores * half_scale
            weights = jnp.where(open_, half * jnp.tanh(half) + half, 0.0).astype(BF16)
            part = jnp.dot(weights, piece[:, wide + lo : wide + hi], preferred_element_type=F32)
            totals[head] = part if totals[head] is None else totals[head] + part
    for head in range(heads):
        out_ref[:, head * size : (head + 1) * size] = totals[head].astype(BF16)


def attend(shards, queries, limits, pieces, first, heads, size):
    slots = queries.shape[0]
    keys = pieces[0].shape[0]
    tile = min(256, slots)
    wide = heads * size
    count = len(pieces)
    return pl.pallas_call(
        functools.partial(attend_kernel, heads, size),
        grid=(slots // tile,),
        in_specs=[
            pl.BlockSpec(memory_space=pltpu.SMEM),
            pl.BlockSpec((tile, wide), lambda i: (i, first // heads)),
            pl.BlockSpec((tile, BLK), lambda i: (i, 0)),
        ]
        + [pl.BlockSpec((keys, 2 * wide), lambda i: (0, 0))] * count,
        out_specs=pl.BlockSpec((tile, wide), lambda i: (i, 0)),
        out_shape=jax.ShapeDtypeStruct((slots, wide), BF16),
        compiler_params=params(),
        cost_estimate=cost(
            4 * slots * keys * count * wide,
            2 * (2 * slots * wide + count * keys * 2 * wide),
            slots * keys * count * heads,
        ),
        name="attend",
    )(shards, queries, limits, *pieces)


def finish_kernel(slot_ref, x_ref, gate_ref, gain_ref, w_ref, *refs):
    returned, out_ref = refs[:-1], refs[-1]
    rows, width = x_ref.shape
    slots = returned[0].shape[0]
    lane = lax.broadcasted_iota(jnp.int32, (1, BLK), 1)
    slot = slot_ref[...]
    place = jnp.concatenate(
        [(lane + start == slot).astype(BF16) for start in range(0, slots, BLK)], axis=1
    )
    attn = jnp.concatenate(
        [jnp.dot(place, part[...], preferred_element_type=F32) for part in returned], axis=1
    )
    centered = attn - jnp.mean(attn, axis=1, keepdims=True)
    variance = jnp.mean(centered * centered, axis=1, keepdims=True)
    normed = (centered * lax.rsqrt(variance + norm_eps) * gain_ref[...]).astype(BF16)
    mixed = (normed.astype(F32) * gate_ref[...].astype(F32)).astype(BF16)
    projected = jnp.dot(mixed, w_ref[...], preferred_element_type=F32)
    out_ref[...] = (x_ref[...].astype(F32) + projected).astype(BF16)


def finish(slot, cand_x, gate, ln_gain, w_out, returned):
    rows, width = cand_x.shape
    slots = returned[0].shape[0]
    tile = min(256, rows)
    return pl.pallas_call(
        finish_kernel,
        grid=(rows // tile,),
        in_specs=[
            pl.BlockSpec((tile, BLK), lambda i: (i, 0)),
            pl.BlockSpec((tile, width), lambda i: (i, 0)),
            pl.BlockSpec((tile, width), lambda i: (i, 0)),
            pl.BlockSpec((1, width), lambda i: (0, 0)),
            pl.BlockSpec((width, width), lambda i: (0, 0)),
        ]
        + [pl.BlockSpec((slots, part.shape[1]), lambda i: (0, 0)) for part in returned],
        out_specs=pl.BlockSpec((tile, width), lambda i: (i, 0)),
        out_shape=jax.ShapeDtypeStruct((rows, width), BF16),
        compiler_params=params(),
        cost_estimate=cost(
            2 * rows * width * (width + slots), 2 * (3 * rows * width + width * width + slots * width)
        ),
        name="finish",
    )(slot, cand_x, gate, ln_gain.reshape(1, width), w_out, *returned)


def swap(array, bit, count):
    return lax.ppermute(array, "user", [(i, i ^ bit) for i in range(count)])


def gather_segments(own, count):
    held = {0: own}
    bit = count // 2
    while bit:
        for key in sorted(held):
            held[key | bit] = swap(held[key], bit, count)
        bit //= 2
    return [held[key] for key in range(count)]


def per_device(cand_x, cand_user, visible, hist_len, kv_cache, w_in, w_out, ln_gain):
    rows, width = cand_x.shape
    columns = lax.axis_size("cand")
    count = lax.axis_size("user")
    size = width // HEADS
    capacity = 2 * rows // columns
    slots = columns * capacity
    kv = kv_cache[0]
    owner_row = cand_user.reshape(1, rows)

    heads_of = []
    first = 0
    for heads in GROUPS:
        heads_of.append((first, heads))
        first += heads

    pieces = []
    for number, (first, heads) in enumerate(heads_of):
        lo, hi = first * size, (first + heads) * size
        own = jnp.concatenate([kv[:, lo:hi], kv[:, width + lo : width + hi]], axis=1)
        if number >= 2:
            own, _ = lax.optimization_barrier((own, pieces[number - 2][count // 2]))
        pieces.append(gather_segments(own, count))

    packed = owner_row * 64 + visible.reshape(1, rows)
    packed = lax.all_gather(packed, "cand", axis=0, tiled=True)
    owners, seen = packed // 64, packed % 64

    send = project_queries(owner_row, cand_x, w_in, columns, capacity)
    got = lax.all_to_all(
        send.reshape(columns, capacity, width), "cand", split_axis=0, concat_axis=0, tiled=True
    ).reshape(slots, width)
    gate, slot = project_gate(owner_row, cand_x, w_in, columns, capacity)
    limits = slot_limits(lax.axis_index("cand"), hist_len[0], owners, seen, capacity)
    shards = lax.axis_index("user").astype(jnp.int32) ^ jnp.arange(count, dtype=jnp.int32)

    returned = []
    for (first, heads), segments in zip(heads_of, pieces):
        wide = heads * size
        attn = attend(shards, got, limits, segments, first, heads, size)
        back = lax.all_to_all(
            attn.reshape(columns, capacity, wide), "cand", split_axis=0, concat_axis=0, tiled=True
        )
        returned.append(back.reshape(slots, wide))
    return finish(slot, cand_x, gate, ln_gain, w_out, returned)


def solution(mesh):
    in_specs = (
        P(("user", "cand"), None),
        P(("user", "cand"), None),
        P(("user", "cand")),
        P("cand"),
        P("cand", "user", None),
        P(),
        P(),
        P(),
    )
    out_specs = P(("user", "cand"), None)
    return jax.shard_map(
        per_device, mesh=mesh, in_specs=in_specs, out_specs=out_specs, check_vma=False
    )
```

```python
import functools
import math

import jax
import jax.numpy as jnp
from jax import lax
from jax.experimental import pallas as pl
from jax.experimental.pallas import tpu as pltpu
from jax.sharding import PartitionSpec as P

HEADS = 8
BLK = 128
GROUPS = (2, 2, 2, 2)
norm_eps = 1e-06
F32 = jnp.float32
BF16 = jnp.bfloat16
MIB = 1024 * 1024
GATE_COST = 12.0


def params(mib):
    return pltpu.CompilerParams(vmem_limit_bytes=mib * MIB)


def cost(flops, nbytes, transcendentals=0):
    return pl.CostEstimate(
        flops=int(flops), bytes_accessed=int(nbytes), transcendentals=int(transcendentals)
    )


def silu(v):
    half = 0.5 * v
    return half * jnp.tanh(half) + half


def earlier_mask(rows):
    first = lax.broadcasted_iota(jnp.int32, (rows, rows), 0)
    second = lax.broadcasted_iota(jnp.int32, (rows, rows), 1)
    return (first < second).astype(BF16)


def slot_row(owner_row, columns, capacity):
    rows = owner_row.shape[1]
    users = lax.broadcasted_iota(jnp.int32, (columns, rows), 0)
    mine = users == owner_row
    before = jnp.dot(mine.astype(BF16), earlier_mask(rows), preferred_element_type=F32)
    rank = jnp.sum(jnp.where(mine, before, 0.0), axis=0, keepdims=True)
    return owner_row.astype(F32) * capacity + rank


def query_kernel(columns, capacity, last, owner_ref, visible_ref, x_ref, w_ref, send_ref, place):
    rows = x_ref.shape[0]
    slots, tile = send_ref.shape

    @pl.when(pl.program_id(0) == 0)
    def _():
        slot = slot_row(owner_ref[...], columns, capacity).astype(jnp.int32)
        index = lax.broadcasted_iota(jnp.int32, (slots, rows), 0)
        place[...] = (index == slot).astype(BF16)

    @pl.when(pl.program_id(0) < last)
    def _():
        queries = silu(jnp.dot(x_ref[...], w_ref[...], preferred_element_type=F32)).astype(BF16)
        send_ref[...] = jnp.dot(place[...], queries, preferred_element_type=F32).astype(BF16)

    @pl.when(pl.program_id(0) == last)
    def _():
        seen = jnp.broadcast_to(visible_ref[...].astype(F32), (tile, rows)).astype(BF16)
        spread = lax.dot_general(
            place[...], seen, (((1,), (1,)), ((), ())), preferred_element_type=F32
        )
        send_ref[...] = spread.astype(BF16)


def project_queries(owner_row, visible_row, cand_x, w_in, columns, capacity):
    rows, width = cand_x.shape
    slots = columns * capacity
    tile = BLK
    last = width // tile
    return pl.pallas_call(
        functools.partial(query_kernel, columns, capacity, last),
        grid=(last + 1,),
        in_specs=[
            pl.BlockSpec((1, rows), lambda i: (0, 0)),
            pl.BlockSpec((1, rows), lambda i: (0, 0)),
            pl.BlockSpec((rows, width), lambda i: (0, 0)),
            pl.BlockSpec((width, tile), lambda i: (0, i)),
        ],
        out_specs=pl.BlockSpec((slots, tile), lambda i: (0, i)),
        out_shape=jax.ShapeDtypeStruct((slots, width + tile), BF16),
        scratch_shapes=[pltpu.VMEM((slots, rows), BF16)],
        compiler_params=params(60),
        cost_estimate=cost(
            2 * rows * width * width + 2 * slots * rows * width,
            2 * (rows * width + width * width + slots * width),
            rows * width,
        ),
        name="project_queries",
    )(owner_row, visible_row, cand_x, w_in)


def gate_kernel(columns, capacity, _first, _second, owner_ref, x_ref, w_ref, gate_ref, slot_ref):

    @pl.when(pl.program_id(0) == 0)
    def _():
        slot = slot_row(owner_ref[...], columns, capacity)
        slot_ref[...] = jnp.broadcast_to(slot, (BLK, slot.shape[1])).T.astype(jnp.int32)

    hidden = jnp.dot(x_ref[...], w_ref[...], preferred_element_type=F32)
    gate_ref[...] = silu(hidden).astype(BF16)


def project_gate(after, owner_row, cand_x, w_in, columns, capacity):
    rows, width = cand_x.shape
    tile = min(256, width)
    first = width // tile
    return pl.pallas_call(
        functools.partial(gate_kernel, columns, capacity),
        grid=(first,),
        in_specs=[
            pl.BlockSpec(memory_space=pl.ANY),
            pl.BlockSpec(memory_space=pl.ANY),
            pl.BlockSpec((1, rows), lambda i: (0, 0)),
            pl.BlockSpec((rows, width), lambda i: (0, 0)),
            pl.BlockSpec((width, tile), lambda i: (0, first + i)),
        ],
        out_specs=[
            pl.BlockSpec((rows, tile), lambda i: (0, i)),
            pl.BlockSpec((rows, BLK), lambda i: (0, 0)),
        ],
        out_shape=[
            jax.ShapeDtypeStruct((rows, width), BF16),
            jax.ShapeDtypeStruct((rows, BLK), jnp.int32),
        ],
        compiler_params=params(60),
        cost_estimate=cost(GATE_COST * 1e9, 2 * (2 * rows * width + width * width), rows * width),
        name="project_gate",
    )(*after, owner_row, cand_x, w_in)


def attend_kernel(heads, size, whole, behind, place_ref, *refs):
    seen_ref, refs = refs[behind], refs[behind + 1 :]
    out_ref = refs[-1]
    queries, refs = refs[:heads], refs[heads:-1]
    full, cut = refs[: 2 * whole * heads], refs[2 * whole * heads :]
    half_scale = 0.5 / math.sqrt(size)
    wide = heads * size
    seen = seen_ref[...].astype(F32)
    length = place_ref[0]
    totals = [None] * heads
    for number in range(whole + len(cut)):
        shard = place_ref[1 + number]
        if number < whole:
            parts = full[2 * number * heads : 2 * (number + 1) * heads]
            keys_of = [part[...] for part in parts[:heads]]
            values_of = [part[...] for part in parts[heads:]]
        else:
            part = cut[number - whole]
            keys_of = [part[:, h * size : (h + 1) * size] for h in range(heads)]
            values_of = [part[:, wide + h * size : wide + (h + 1) * size] for h in range(heads)]
        keys = keys_of[0].shape[0]
        row = lax.broadcasted_iota(jnp.int32, (keys, size), 0) + shard * keys
        blocks = keys // BLK
        scales = [
            jnp.where((shard * blocks + block).astype(F32) < seen, half_scale, 0.0)
            for block in range(blocks)
        ]
        for head in range(heads):
            values = jnp.where(row < length, values_of[head].astype(F32), 0.0).astype(BF16)
            scores = lax.dot_general(
                queries[head][...],
                keys_of[head],
                (((1,), (1,)), ((), ())),
                preferred_element_type=F32,
            )
            weights = []
            for block in range(blocks):
                half = scores[:, block * BLK : (block + 1) * BLK] * scales[block]
                weights.append((half * jnp.tanh(half) + half).astype(BF16))
            part = jnp.dot(
                jnp.concatenate(weights, axis=1), values, preferred_element_type=F32
            )
            totals[head] = part if totals[head] is None else totals[head] + part
    for head in range(heads):
        out_ref[:, head * size : (head + 1) * size] = totals[head].astype(BF16)


def attend(place, after, rows, full, cut, first, heads, size):
    slots, width = rows.shape[0], HEADS * size
    keys = full[0].shape[0]
    tile = min(512, slots)
    wide = heads * size
    count = len(full) + len(cut)

    def column(block, index):
        return pl.BlockSpec(block, lambda i: (0, index))

    in_specs = [
        pl.BlockSpec(memory_space=pltpu.SMEM),
        *[pl.BlockSpec(memory_space=pl.ANY) for _ in after],
        pl.BlockSpec((tile, BLK), lambda i: (i, width // BLK)),
    ]
    args = [place, *after, rows]
    for head in range(first, first + heads):
        in_specs.append(pl.BlockSpec((tile, size), lambda i, head=head: (i, head)))
        args.append(rows)
    for piece in full:
        for head in range(first, first + heads):
            in_specs.append(column((keys, size), head))
            args.append(piece)
        for head in range(first, first + heads):
            in_specs.append(column((keys, size), HEADS + head))
            args.append(piece)
    for piece in cut:
        in_specs.append(column((keys, 2 * wide), 0))
        args.append(piece)
    return pl.pallas_call(
        functools.partial(attend_kernel, heads, size, len(full), len(after)),
        grid=(slots // tile,),
        in_specs=in_specs,
        out_specs=pl.BlockSpec((tile, wide), lambda i: (i, 0)),
        out_shape=jax.ShapeDtypeStruct((slots, wide), BF16),
        compiler_params=params(60),
        cost_estimate=cost(
            4 * slots * keys * count * wide,
            2 * (2 * slots * wide + count * keys * 2 * wide),
            slots * keys * count * heads,
        ),
        name="attend",
    )(*args)


def finish_kernel(slot_ref, gain_ref, x_hbm, gate_hbm, w_hbm, *refs):
    returned = refs[:-7]
    out_hbm, x_ref, gate_ref, w_ref, out_ref, in_sems, out_sems = refs[-7:]
    loads = [
        pltpu.make_async_copy(source, target, in_sems.at[number])
        for number, (source, target) in enumerate(
            [(gate_hbm, gate_ref), (w_hbm, w_ref), (x_hbm, x_ref)]
        )
    ]
    for load in loads:
        load.start()
    rows, width = x_ref.shape
    slots = returned[0].shape[0]
    tile = rows // 2
    lane = lax.broadcasted_iota(jnp.int32, (1, BLK), 1)
    stores = []
    for half in range(2):
        span = slice(half * tile, (half + 1) * tile)
        slot = slot_ref[span, :]
        place = jnp.concatenate(
            [(lane + start == slot).astype(BF16) for start in range(0, slots, BLK)], axis=1
        )
        attn = jnp.concatenate(
            [jnp.dot(place, part[...], preferred_element_type=F32) for part in returned], axis=1
        )
        centered = attn - jnp.mean(attn, axis=1, keepdims=True)
        variance = jnp.mean(centered * centered, axis=1, keepdims=True)
        normed = (centered * lax.rsqrt(variance + norm_eps) * gain_ref[...]).astype(BF16)
        if half == 0:
            for load in loads:
                load.wait()
        mixed = (normed.astype(F32) * gate_ref[span, :].astype(F32)).astype(BF16)
        projected = jnp.dot(mixed, w_ref[...], preferred_element_type=F32)
        out_ref[span, :] = (x_ref[span, :].astype(F32) + projected).astype(BF16)
        store = pltpu.make_async_copy(out_ref.at[span, :], out_hbm.at[span, :], out_sems.at[half])
        store.start()
        stores.append(store)
    for store in stores:
        store.wait()


def finish(slot, cand_x, gate, ln_gain, w_out, returned):
    rows, width = cand_x.shape
    slots = returned[0].shape[0]
    vmem = pl.BlockSpec(memory_space=pltpu.VMEM)
    hbm = pl.BlockSpec(memory_space=pltpu.HBM)
    return pl.pallas_call(
        finish_kernel,
        in_specs=[vmem, vmem, hbm, hbm, hbm] + [vmem] * len(returned),
        out_specs=hbm,
        out_shape=jax.ShapeDtypeStruct((rows, width), BF16),
        scratch_shapes=[
            pltpu.VMEM((rows, width), BF16),
            pltpu.VMEM((rows, width), BF16),
            pltpu.VMEM((width, width), BF16),
            pltpu.VMEM((rows, width), BF16),
            pltpu.SemaphoreType.DMA((3,)),
            pltpu.SemaphoreType.DMA((2,)),
        ],
        compiler_params=params(60),
        cost_estimate=cost(
            2 * rows * width * (width + slots), 2 * (3 * rows * width + width * width + slots * width)
        ),
        name="finish",
    )(slot, ln_gain.reshape(1, width), cand_x, gate, w_out, *returned)


def swap(array, bit, count):
    return lax.ppermute(array, "user", [(i, i ^ bit) for i in range(count)])


def per_device(cand_x, cand_user, visible, hist_len, kv_cache, w_in, w_out, ln_gain):
    rows, width = cand_x.shape
    columns = lax.axis_size("cand")
    count = lax.axis_size("user")
    size = width // HEADS
    capacity = 2 * rows // columns
    slots = columns * capacity
    own = kv_cache[0]
    owner_row = cand_user.reshape(1, rows)
    visible_row = visible.reshape(1, rows)

    held = {0: own}
    bit = count // 2
    while bit > 1:
        for key in sorted(held):
            held[key | bit] = swap(held[key], bit, count)
        bit //= 2
    evens = sorted(held)
    full = [held[key] for key in evens] + [swap(own, 1, count)]
    order = evens + [1] + [key | 1 for key in evens[1:]]

    send = project_queries(owner_row, visible_row, cand_x, w_in, columns, capacity)
    got = lax.all_to_all(
        send.reshape(columns, capacity, -1), "cand", split_axis=0, concat_axis=0, tiled=True
    ).reshape(slots, -1)
    gate, slot = project_gate((full[1], full[-1]), owner_row, cand_x, w_in, columns, capacity)
    position = lax.axis_index("user").astype(jnp.int32)
    place = jnp.concatenate([hist_len, position ^ jnp.array(order, jnp.int32)])

    def forward(first, heads, behind):
        lo, hi = first * size, (first + heads) * size
        parts = [
            jnp.concatenate([held[key][:, lo:hi], held[key][:, width + lo : width + hi]], axis=1)
            for key in evens[1:]
        ]
        if behind is not None:
            parts, _ = lax.optimization_barrier((parts, behind))
        return [swap(part, 1, count) for part in parts]

    spans = [(sum(GROUPS[:number]), heads) for number, heads in enumerate(GROUPS)]
    cuts = []
    for number, (first, heads) in enumerate(spans):
        cuts.append(forward(first, heads, cuts[number - 2] if number >= 2 else None))
    returned = []
    after = [slot]
    for number, (first, heads) in enumerate(spans):
        attn = attend(place, after, got, full, cuts[number], first, heads, size)
        after = [attn] + returned[-1:]
        if number + 1 < len(spans):
            attn, _ = lax.optimization_barrier((attn, cuts[number + 1]))
        back = lax.all_to_all(
            attn.reshape(columns, capacity, heads * size),
            "cand",
            split_axis=0,
            concat_axis=0,
            tiled=True,
        )
        returned.append(back.reshape(slots, heads * size))
    return finish(slot, cand_x, gate, ln_gain, w_out, returned)


def solution(mesh):
    in_specs = (
        P(("user", "cand"), None),
        P(("user", "cand"), None),
        P(("user", "cand")),
        P("cand"),
        P("cand", "user", None),
        P(),
        P(),
        P(),
    )
    out_specs = P(("user", "cand"), None)
    return jax.shard_map(
        per_device, mesh=mesh, in_specs=in_specs, out_specs=out_specs, check_vma=False
    )
```

```python
import functools
import math

import jax
import jax.numpy as jnp
from jax import lax
from jax.experimental import pallas as pl
from jax.experimental.pallas import tpu as pltpu
from jax.sharding import PartitionSpec as P

HEADS = 8
BLK = 128
GROUPS = (3, 3, 2)
norm_eps = 1e-06
F32 = jnp.float32
BF16 = jnp.bfloat16
MIB = 1024 * 1024
BASE_COST = 4.0


def params(mib):
    return pltpu.CompilerParams(vmem_limit_bytes=mib * MIB)


def cost(flops, nbytes, transcendentals=0):
    return pl.CostEstimate(
        flops=int(flops), bytes_accessed=int(nbytes), transcendentals=int(transcendentals)
    )


def silu(v):
    half = 0.5 * v
    return half * jnp.tanh(half) + half


def earlier_mask(rows):
    first = lax.broadcasted_iota(jnp.int32, (rows, rows), 0)
    second = lax.broadcasted_iota(jnp.int32, (rows, rows), 1)
    return (first < second).astype(BF16)


def slot_row(owner_row, columns, capacity):
    rows = owner_row.shape[1]
    users = lax.broadcasted_iota(jnp.int32, (columns, rows), 0)
    mine = users == owner_row
    before = jnp.dot(mine.astype(BF16), earlier_mask(rows), preferred_element_type=F32)
    rank = jnp.sum(jnp.where(mine, before, 0.0), axis=0, keepdims=True)
    return owner_row.astype(F32) * capacity + rank


def query_kernel(columns, capacity, owner_ref, visible_ref, x_ref, w_ref, *refs):
    sends, place = refs[:-1], refs[-1]
    rows = x_ref.shape[0]
    tile = w_ref.shape[1]
    slots = columns * capacity

    @pl.when(pl.program_id(0) == 0)
    def _():
        slot = slot_row(owner_ref[...], columns, capacity).astype(jnp.int32)
        index = lax.broadcasted_iota(jnp.int32, (slots, rows), 0)
        place[...] = (index == slot).astype(BF16)

    def send(block):
        spread = jnp.dot(place[...], block, preferred_element_type=F32).astype(BF16)
        for number, ref in enumerate(sends):
            ref[...] = spread[number * capacity : (number + 1) * capacity, :]

    queries = silu(jnp.dot(x_ref[...], w_ref[...], preferred_element_type=F32)).astype(BF16)
    final = pl.program_id(0) == pl.num_programs(0) - 1

    @pl.when(jnp.logical_not(final))
    def _():
        send(queries)

    @pl.when(final)
    def _():
        seen = jnp.broadcast_to(visible_ref[...].astype(F32), (BLK, rows)).T.astype(BF16)
        send(jnp.concatenate([queries[:, : tile - BLK], seen], axis=1))


def project_queries(owner_row, visible_row, cand_x, w_in, columns, capacity):
    rows, width = cand_x.shape
    slots = columns * capacity
    steps = 3
    tile = (width + BLK) // steps
    return pl.pallas_call(
        functools.partial(query_kernel, columns, capacity),
        grid=(steps,),
        in_specs=[
            pl.BlockSpec((1, rows), lambda i: (0, 0)),
            pl.BlockSpec((1, rows), lambda i: (0, 0)),
            pl.BlockSpec((rows, width), lambda i: (0, 0)),
            pl.BlockSpec((width, tile), lambda i: (0, i)),
        ],
        out_specs=[pl.BlockSpec((capacity, tile), lambda i: (0, i))] * columns,
        out_shape=[jax.ShapeDtypeStruct((capacity, width + BLK), BF16)] * columns,
        scratch_shapes=[pltpu.VMEM((slots, rows), BF16)],
        compiler_params=params(60),
        cost_estimate=cost(
            2 * rows * width * width + 2 * slots * rows * width,
            2 * (rows * width + width * width + slots * width),
            rows * width,
        ),
        name="project_queries",
    )(owner_row, visible_row, cand_x, w_in)


def gate_kernel(columns, capacity, owner_ref, x_ref, w_ref, gate_ref, slot_ref):

    @pl.when(pl.program_id(0) == 0)
    def _():
        slot = slot_row(owner_ref[...], columns, capacity)
        slot_ref[...] = jnp.broadcast_to(slot, (BLK, slot.shape[1])).T.astype(jnp.int32)

    hidden = jnp.dot(x_ref[...], w_ref[...], preferred_element_type=F32)
    gate_ref[...] = silu(hidden).astype(BF16)


def project_gate(owner_row, cand_x, w_in, columns, capacity):
    rows, width = cand_x.shape
    tile = min(256, width)
    first = width // tile
    return pl.pallas_call(
        functools.partial(gate_kernel, columns, capacity),
        grid=(first,),
        in_specs=[
            pl.BlockSpec((1, rows), lambda i: (0, 0)),
            pl.BlockSpec((rows, width), lambda i: (0, 0)),
            pl.BlockSpec((width, tile), lambda i: (0, first + i)),
        ],
        out_specs=[
            pl.BlockSpec((rows, tile), lambda i: (0, i)),
            pl.BlockSpec((rows, BLK), lambda i: (0, 0)),
        ],
        out_shape=[
            jax.ShapeDtypeStruct((rows, width), BF16),
            jax.ShapeDtypeStruct((rows, BLK), jnp.int32),
        ],
        compiler_params=params(60),
        cost_estimate=cost(
            2 * rows * width * width, 2 * (2 * rows * width + width * width), rows * width
        ),
        name="project_gate",
    )(owner_row, cand_x, w_in)


def attend_kernel(size, behind, segments, has_base, outs, place_ref, *refs):
    refs = refs[behind:]
    seen_ref, query_ref, refs = refs[0], refs[1], refs[2:]
    parts, refs = refs[: 2 * segments], refs[2 * segments :]
    base_ref = refs[0] if has_base else None
    out_refs, scales = refs[-1 - outs : -1], refs[-1]
    slots = query_ref.shape[0]
    keys = parts[0].shape[0]
    blocks = keys // BLK

    @pl.when(pl.program_id(0) == 0)
    def _():
        seen = seen_ref[...].astype(F32)
        for number in range(segments):
            for block in range(blocks):
                first = (place_ref[1 + number] * blocks + block).astype(F32)
                scales[number * blocks + block] = jnp.where(
                    first < seen, 0.5 / math.sqrt(size), 0.0
                )

    row = lax.broadcasted_iota(jnp.int32, (keys, size), 0)
    values = []
    for number in range(segments):
        shown = row + place_ref[1 + number] * keys < place_ref[0]
        value = parts[2 * number + 1][...].astype(F32)
        values.append(jnp.where(shown, value, 0.0).astype(BF16))
    values = jnp.concatenate(values, axis=0)
    tile = min(256, slots)
    results = []
    for start in range(0, slots, tile):
        span = slice(start, start + tile)
        weights = []
        for number in range(segments):
            scores = lax.dot_general(
                query_ref[span, :],
                parts[2 * number][...],
                (((1,), (1,)), ((), ())),
                preferred_element_type=F32,
            )
            for block in range(blocks):
                half = scores[:, block * BLK : (block + 1) * BLK]
                half = half * scales[number * blocks + block, span, :]
                weights.append((half * jnp.tanh(half) + half).astype(BF16))
        total = jnp.dot(
            jnp.concatenate(weights, axis=1), values, preferred_element_type=F32
        )
        if has_base:
            total = total + base_ref[span, :]
        results.append(total)
    capacity = slots // outs
    for number, ref in enumerate(out_refs):
        start = number * capacity
        piece = results[start // tile][start % tile : start % tile + capacity, :]
        if outs == 1:
            piece = jnp.concatenate(results, axis=0)
        ref[...] = piece.astype(ref.dtype)


def attend(place, after, rows, segments, base, first, heads, size, outs, dtype, share=1.0):
    slots, width = rows.shape[0], HEADS * size
    keys = segments[0][0].shape[0]
    capacity = slots // outs
    count = len(segments)

    def column(height, index):
        return pl.BlockSpec((height, size), lambda i: (0, index + i))

    in_specs = [
        pl.BlockSpec(memory_space=pltpu.SMEM),
        *[pl.BlockSpec(memory_space=pl.ANY) for _ in after],
        pl.BlockSpec((slots, BLK), lambda i: (0, width // BLK)),
        column(slots, first),
    ]
    args = [place, *after, rows, rows]
    for piece, key, value in segments:
        in_specs += [column(keys, key), column(keys, value)]
        args += [piece, piece]
    if base is not None:
        in_specs.append(column(slots, first))
        args.append(base)
    return pl.pallas_call(
        functools.partial(attend_kernel, size, len(after), count, base is not None, outs),
        grid=(heads,),
        in_specs=in_specs,
        out_specs=[column(capacity, 0)] * outs,
        out_shape=[jax.ShapeDtypeStruct((capacity, heads * size), dtype)] * outs,
        scratch_shapes=[pltpu.VMEM((count * (keys // BLK), slots, BLK), F32)],
        compiler_params=params(60),
        cost_estimate=cost(
            share * 4 * slots * keys * count * heads * size,
            2 * (2 * slots + count * keys * 2) * heads * size,
            slots * keys * count * heads,
        ),
        name="attend",
    )(*args)


def placement(slot, slots):
    lane = lax.broadcasted_iota(jnp.int32, (1, BLK), 1)
    return jnp.concatenate(
        [(lane + start == slot).astype(BF16) for start in range(0, slots, BLK)], axis=1
    )


def collect_kernel(groups, slot_ref, *refs):
    parts, out_ref = refs[:-1], refs[-1]
    each = len(parts) // groups
    place = placement(slot_ref[...], each * parts[0].shape[0])
    first = 0
    for group in range(groups):
        rows = jnp.concatenate(
            [part[...] for part in parts[group * each : (group + 1) * each]], axis=0
        )
        last = first + rows.shape[1]
        out_ref[:, first:last] = jnp.dot(place, rows, preferred_element_type=F32).astype(BF16)
        first = last


def collect(slot, groups):
    rows = slot.shape[0]
    parts = [part for group in groups for part in group]
    width = sum(group[0].shape[1] for group in groups)
    slots = len(groups[0]) * groups[0][0].shape[0]
    vmem = pl.BlockSpec(memory_space=pltpu.VMEM)
    return pl.pallas_call(
        functools.partial(collect_kernel, len(groups)),
        in_specs=[vmem] * (1 + len(parts)),
        out_specs=vmem,
        out_shape=jax.ShapeDtypeStruct((rows, width), BF16),
        compiler_params=params(60),
        cost_estimate=cost(2 * rows * slots * width, 2 * (rows + slots) * width),
        name="collect",
    )(slot, *parts)


def finish_kernel(pieces, gain_ref, slot_hbm, early_hbm, gate_hbm, x_hbm, w_hbm, *refs):
    parts, refs = refs[:pieces], refs[pieces:]
    out_hbm, slot_ref, early_ref, gate_ref, x_ref, w_ref, rows_ref, out_ref = refs[:8]
    sems, out_sems = refs[8:]
    capacity = parts[0].shape[0]
    moves = [(slot_hbm, slot_ref)]
    for number, part in enumerate(parts):
        moves.append((part, rows_ref.at[number * capacity : (number + 1) * capacity, :]))
    needed = len(moves)
    for source, target in ((early_hbm, early_ref), (gate_hbm, gate_ref), (w_hbm, w_ref), (x_hbm, x_ref)):
        step = source.shape[0] // 4
        for quarter in range(4):
            span = slice(quarter * step, (quarter + 1) * step)
            moves.append((source.at[span, :], target.at[span, :]))
    loads = [
        pltpu.make_async_copy(source, target, sems.at[number])
        for number, (source, target) in enumerate(moves)
    ]
    for load in loads:
        load.start()
    for load in loads[:needed]:
        load.wait()
    rows = x_ref.shape[0]
    slots = rows_ref.shape[0]
    late = jnp.dot(placement(slot_ref[...], slots), rows_ref[...], preferred_element_type=F32)
    for load in loads[needed:]:
        load.wait()
    tile = rows // 2
    stores = []
    for half in range(2):
        span = slice(half * tile, (half + 1) * tile)
        attn = jnp.concatenate([early_ref[span, :].astype(F32), late[span, :]], axis=1)
        centered = attn - jnp.mean(attn, axis=1, keepdims=True)
        variance = jnp.mean(centered * centered, axis=1, keepdims=True)
        normed = (centered * lax.rsqrt(variance + norm_eps) * gain_ref[...]).astype(BF16)
        mixed = (normed.astype(F32) * gate_ref[span, :].astype(F32)).astype(BF16)
        projected = jnp.dot(mixed, w_ref[...], preferred_element_type=F32)
        out_ref[span, :] = (x_ref[span, :].astype(F32) + projected).astype(BF16)
        store = pltpu.make_async_copy(out_ref.at[span, :], out_hbm.at[span, :], out_sems.at[half])
        store.start()
        stores.append(store)
    for store in stores:
        store.wait()


def finish(slot, early, gate, cand_x, ln_gain, w_out, parts):
    rows, width = cand_x.shape
    capacity, wide = parts[0].shape
    slots = len(parts) * capacity
    vmem = pl.BlockSpec(memory_space=pltpu.VMEM)
    anywhere = pl.BlockSpec(memory_space=pl.ANY)
    return pl.pallas_call(
        functools.partial(finish_kernel, len(parts)),
        in_specs=[vmem] + [anywhere] * (5 + len(parts)),
        out_specs=anywhere,
        out_shape=jax.ShapeDtypeStruct((rows, width), BF16),
        scratch_shapes=[
            pltpu.VMEM(slot.shape, jnp.int32),
            pltpu.VMEM(early.shape, BF16),
            pltpu.VMEM((rows, width), BF16),
            pltpu.VMEM((rows, width), BF16),
            pltpu.VMEM((width, width), BF16),
            pltpu.VMEM((slots, wide), BF16),
            pltpu.VMEM((rows, width), BF16),
            pltpu.SemaphoreType.DMA((len(parts) + 17,)),
            pltpu.SemaphoreType.DMA((2,)),
        ],
        compiler_params=params(60),
        cost_estimate=cost(
            2 * rows * width * (width + slots), 2 * (3 * rows * width + width * width + slots * width)
        ),
        name="finish",
    )(ln_gain.reshape(1, width), slot, early, gate, cand_x, w_out, *parts)


def swap(array, axis, bits, count):
    return lax.ppermute(array, axis, [(i, i ^ bits) for i in range(count)])


def exchange(blocks):
    count = len(blocks)
    return [block if d == 0 else swap(block, "cand", d, count) for d, block in enumerate(blocks)]


def per_device(cand_x, cand_user, visible, hist_len, kv_cache, w_in, w_out, ln_gain):
    rows, width = cand_x.shape
    columns = lax.axis_size("cand")
    count = lax.axis_size("user")
    size = width // HEADS
    capacity = 2 * rows // columns
    own = kv_cache[0]
    owner_row = cand_user.reshape(1, rows) ^ lax.axis_index("cand").astype(jnp.int32)
    visible_row = visible.reshape(1, rows)

    held = {0: own}
    bit = count // 2
    while bit > 1:
        for key in sorted(held):
            held[key | bit] = swap(held[key], "user", bit, count)
        bit //= 2
    evens = sorted(held)
    near = swap(own, "user", 1, count)

    send = project_queries(owner_row, visible_row, cand_x, w_in, columns, capacity)
    got = jnp.concatenate(exchange(send), axis=0)
    gate, slot = project_gate(owner_row, cand_x, w_in, columns, capacity)
    position = lax.axis_index("user").astype(jnp.int32)
    order = evens[1:] + [key | 1 for key in evens[1:]]
    place_first = jnp.concatenate([hist_len, position ^ jnp.array([0, 1], jnp.int32)])
    place = jnp.concatenate([hist_len, position ^ jnp.array(order, jnp.int32)])
    base = attend(
        place_first,
        [slot, held[evens[-1]]],
        got,
        [(own, 0, HEADS), (near, 0, HEADS)],
        None,
        0,
        HEADS,
        size,
        1,
        F32,
        BASE_COST,
    )[0]

    def forward(first, heads, behind):
        lo, hi = first * size, (first + heads) * size
        parts = [
            jnp.concatenate([held[key][:, lo:hi], held[key][:, width + lo : width + hi]], axis=1)
            for key in evens[1:]
        ]
        if behind is not None:
            parts, _ = lax.optimization_barrier((parts, behind))
        return [swap(part, "user", 1, count) for part in parts]

    spans = [(sum(GROUPS[:number]), heads) for number, heads in enumerate(GROUPS)]
    cuts = [forward(*spans[0], None)]
    returned = []
    after = []
    done = base
    for number, (first, heads) in enumerate(spans):
        if number + 1 < len(spans):
            cuts.append(forward(*spans[number + 1], (cuts[number], done)))
        segments = [(held[key], first, HEADS + first) for key in evens[1:]]
        segments += [(cut, 0, heads) for cut in cuts[number]]
        attn = attend(place, after, got, segments, base, first, heads, size, columns, BF16)
        done = attn[0]
        after = [attn[0]] + [group[-1] for group in returned[-1:]]
        returned.append(exchange(attn))
    early = collect(slot, returned[:-1])
    return finish(slot, early, gate, cand_x, ln_gain, w_out, returned[-1])


def solution(mesh):
    in_specs = (
        P(("user", "cand"), None),
        P(("user", "cand"), None),
        P(("user", "cand")),
        P("cand"),
        P("cand", "user", None),
        P(),
        P(),
        P(),
    )
    out_specs = P(("user", "cand"), None)
    return jax.shard_map(
        per_device, mesh=mesh, in_specs=in_specs, out_specs=out_specs, check_vma=False
    )
```

```python
import functools
import math

import jax
import jax.numpy as jnp
from jax import lax
from jax.experimental import pallas as pl
from jax.experimental.pallas import tpu as pltpu
from jax.sharding import PartitionSpec as P

HEADS = 8
BLK = 128
GROUPS = (3, 3, 2)
norm_eps = 1e-06
F32 = jnp.float32
BF16 = jnp.bfloat16
MIB = 1024 * 1024
WAIT_COST = 20.0


def params(mib):
    return pltpu.CompilerParams(vmem_limit_bytes=mib * MIB)


def cost(flops, nbytes, transcendentals=0):
    return pl.CostEstimate(
        flops=int(flops), bytes_accessed=int(nbytes), transcendentals=int(transcendentals)
    )


def silu(v):
    half = 0.5 * v
    return half * jnp.tanh(half) + half


def earlier_mask(rows):
    first = lax.broadcasted_iota(jnp.int32, (rows, rows), 0)
    second = lax.broadcasted_iota(jnp.int32, (rows, rows), 1)
    return (first < second).astype(BF16)


def slot_row(owner_row, columns, capacity):
    rows = owner_row.shape[1]
    users = lax.broadcasted_iota(jnp.int32, (columns, rows), 0)
    mine = users == owner_row
    before = jnp.dot(mine.astype(BF16), earlier_mask(rows), preferred_element_type=F32)
    rank = jnp.sum(jnp.where(mine, before, 0.0), axis=0, keepdims=True)
    return owner_row.astype(F32) * capacity + rank


def query_kernel(columns, capacity, owner_ref, visible_ref, x_ref, w_ref, send_ref, place):
    rows = x_ref.shape[0]
    tile = w_ref.shape[1]
    slots = columns * capacity

    @pl.when(pl.program_id(0) == 0)
    def _():
        slot = slot_row(owner_ref[...], columns, capacity).astype(jnp.int32)
        index = lax.broadcasted_iota(jnp.int32, (slots, rows), 0)
        place[...] = (index == slot).astype(BF16)

    def send(block):
        send_ref[...] = jnp.dot(place[...], block, preferred_element_type=F32).astype(BF16)

    queries = silu(jnp.dot(x_ref[...], w_ref[...], preferred_element_type=F32)).astype(BF16)
    final = pl.program_id(0) == pl.num_programs(0) - 1

    @pl.when(jnp.logical_not(final))
    def _():
        send(queries)

    @pl.when(final)
    def _():
        seen = jnp.broadcast_to(visible_ref[...].astype(F32), (BLK, rows)).T.astype(BF16)
        send(jnp.concatenate([queries[:, : tile - BLK], seen], axis=1))


def project_queries(owner_row, visible_row, cand_x, w_in, columns, capacity):
    rows, width = cand_x.shape
    slots = columns * capacity
    steps = 3
    tile = (width + BLK) // steps
    return pl.pallas_call(
        functools.partial(query_kernel, columns, capacity),
        grid=(steps,),
        in_specs=[
            pl.BlockSpec((1, rows), lambda i: (0, 0)),
            pl.BlockSpec((1, rows), lambda i: (0, 0)),
            pl.BlockSpec((rows, width), lambda i: (0, 0)),
            pl.BlockSpec((width, tile), lambda i: (0, i)),
        ],
        out_specs=pl.BlockSpec((slots, tile), lambda i: (0, i)),
        out_shape=jax.ShapeDtypeStruct((slots, width + BLK), BF16),
        scratch_shapes=[pltpu.VMEM((slots, rows), BF16)],
        compiler_params=params(60),
        cost_estimate=cost(
            2 * rows * width * width + 2 * slots * rows * width,
            2 * (rows * width + width * width + slots * width),
            rows * width,
        ),
        name="project_queries",
    )(owner_row, visible_row, cand_x, w_in)


def gate_kernel(x_ref, w_ref, gate_ref):
    hidden = jnp.dot(x_ref[...], w_ref[...], preferred_element_type=F32)
    gate_ref[...] = silu(hidden).astype(BF16)


def project_gate(cand_x, w_in):
    rows, width = cand_x.shape
    tile = min(256, width)
    first = width // tile
    return pl.pallas_call(
        gate_kernel,
        grid=(first,),
        in_specs=[
            pl.BlockSpec((rows, width), lambda i: (0, 0)),
            pl.BlockSpec((width, tile), lambda i: (0, first + i)),
        ],
        out_specs=pl.BlockSpec((rows, tile), lambda i: (0, i)),
        out_shape=jax.ShapeDtypeStruct((rows, width), BF16),
        compiler_params=params(60),
        cost_estimate=cost(
            2 * rows * width * width, 2 * (2 * rows * width + width * width), rows * width
        ),
        name="project_gate",
    )(cand_x, w_in)


def slots_kernel(columns, capacity, owner_ref, *refs):
    slot = slot_row(owner_ref[...], columns, capacity)
    refs[-1][...] = jnp.broadcast_to(slot, (BLK, slot.shape[1])).T.astype(jnp.int32)


def slot_column(owner_row, columns, capacity, after):
    rows = owner_row.shape[1]
    vmem = pl.BlockSpec(memory_space=pltpu.VMEM)
    return pl.pallas_call(
        functools.partial(slots_kernel, columns, capacity),
        in_specs=[vmem] + [pl.BlockSpec(memory_space=pl.ANY)] * len(after),
        out_specs=vmem,
        out_shape=jax.ShapeDtypeStruct((rows, BLK), jnp.int32),
        compiler_params=params(60),
        cost_estimate=cost(WAIT_COST * 1e9, 4 * rows * BLK),
        name="slot_column",
    )(owner_row, *after)


def attend_kernel(size, behind, segments, has_base, outs, place_ref, *refs):
    refs = refs[behind:]
    seen_ref, query_ref, refs = refs[0], refs[1], refs[2:]
    parts, refs = refs[: 2 * segments], refs[2 * segments :]
    base_ref = refs[0] if has_base else None
    out_refs, shown = refs[-2 - outs : -2], refs[-2]
    result = out_refs[0] if outs == 1 else refs[-1]
    slots = query_ref.shape[0]
    keys = parts[0].shape[0]
    blocks = keys // BLK

    @pl.when(pl.program_id(0) == 0)
    def _():
        seen = seen_ref[...].astype(F32)
        for number in range(segments):
            for block in range(blocks):
                first = (place_ref[2 + number] * blocks + block).astype(F32)
                shown[number * blocks + block] = (first < seen).astype(F32).astype(BF16)

    row = lax.broadcasted_iota(jnp.int32, (keys, size), 0)
    values = []
    for number in range(segments):
        inside = row + place_ref[2 + number] * keys < place_ref[0]
        value = parts[2 * number + 1][...].astype(F32)
        values.append(jnp.where(inside, value, 0.0).astype(BF16))
    values = jnp.concatenate(values, axis=0)
    tile = min(512, slots)
    for start in range(0, slots, tile):
        span = slice(start, start + tile)
        weights = []
        for number in range(segments):
            scores = lax.dot_general(
                query_ref[span, :],
                parts[2 * number][...],
                (((1,), (1,)), ((), ())),
                preferred_element_type=F32,
            )
            for block in range(blocks):
                half = scores[:, block * BLK : (block + 1) * BLK] * (0.5 / math.sqrt(size))
                half = half.astype(BF16) * shown[number * blocks + block, span, :]
                weights.append(half * jnp.tanh(half) + half)
        total = jnp.dot(
            jnp.concatenate(weights, axis=1), values, preferred_element_type=F32
        )
        if has_base:
            total = total + base_ref[span, :]
        result[span, :] = total.astype(result.dtype)
    if outs > 1:
        capacity = slots // outs
        for number, ref in enumerate(out_refs):
            start = pl.multiple_of((place_ref[1] ^ number) * capacity, capacity)
            ref[...] = result[pl.ds(start, capacity), :]


def attend(place, after, rows, segments, base, first, heads, size, outs, dtype):
    slots, width = rows.shape[0], HEADS * size
    keys = segments[0][0].shape[0]
    capacity = slots // outs
    count = len(segments)

    def column(height, index):
        return pl.BlockSpec((height, size), lambda i: (0, index + i))

    in_specs = [
        pl.BlockSpec(memory_space=pltpu.SMEM),
        *[pl.BlockSpec(memory_space=pl.ANY) for _ in after],
        pl.BlockSpec((slots, BLK), lambda i: (0, width // BLK)),
        column(slots, first),
    ]
    args = [place, *after, rows, rows]
    for piece, key, value in segments:
        in_specs += [column(keys, key), column(keys, value)]
        args += [piece, piece]
    if base is not None:
        in_specs.append(column(slots, first))
        args.append(base)
    return pl.pallas_call(
        functools.partial(attend_kernel, size, len(after), count, base is not None, outs),
        grid=(heads,),
        in_specs=in_specs,
        out_specs=[column(capacity, 0)] * outs,
        out_shape=[jax.ShapeDtypeStruct((capacity, heads * size), dtype)] * outs,
        scratch_shapes=[
            pltpu.VMEM((count * (keys // BLK), slots, BLK), BF16),
            pltpu.VMEM((slots, size), BF16),
        ],
        compiler_params=params(60),
        cost_estimate=cost(
            4 * slots * keys * count * heads * size,
            2 * (2 * slots + count * keys * 2) * heads * size,
            slots * keys * count * heads,
        ),
        name="attend",
    )(*args)


def placement(slot, slots):
    lane = lax.broadcasted_iota(jnp.int32, (1, BLK), 1)
    return jnp.concatenate(
        [(lane + start == slot).astype(BF16) for start in range(0, slots, BLK)], axis=1
    )


def collect_kernel(groups, slot_ref, *refs):
    parts, out_ref = refs[:-1], refs[-1]
    each = len(parts) // groups
    place = placement(slot_ref[...], each * parts[0].shape[0])
    first = 0
    for group in range(groups):
        rows = jnp.concatenate(
            [part[...] for part in parts[group * each : (group + 1) * each]], axis=0
        )
        last = first + rows.shape[1]
        out_ref[:, first:last] = jnp.dot(place, rows, preferred_element_type=F32).astype(BF16)
        first = last


def collect(slot, groups):
    rows = slot.shape[0]
    parts = [part for group in groups for part in group]
    width = sum(group[0].shape[1] for group in groups)
    slots = len(groups[0]) * groups[0][0].shape[0]
    vmem = pl.BlockSpec(memory_space=pltpu.VMEM)
    return pl.pallas_call(
        functools.partial(collect_kernel, len(groups)),
        in_specs=[vmem] * (1 + len(parts)),
        out_specs=vmem,
        out_shape=jax.ShapeDtypeStruct((rows, width), BF16),
        compiler_params=params(60),
        cost_estimate=cost(2 * rows * slots * width, 2 * (rows + slots) * width),
        name="collect",
    )(slot, *parts)


def finish_kernel(pieces, gain_ref, slot_hbm, early_hbm, gate_hbm, x_hbm, w_hbm, *refs):
    parts, refs = refs[:pieces], refs[pieces:]
    out_hbm, slot_ref, early_ref, gate_ref, x_ref, w_ref, rows_ref, out_ref = refs[:8]
    sems, out_sems = refs[8:]
    capacity = parts[0].shape[0]
    moves = [(slot_hbm, slot_ref)]
    for number, part in enumerate(parts):
        moves.append((part, rows_ref.at[number * capacity : (number + 1) * capacity, :]))
    needed = len(moves)
    for source, target in ((early_hbm, early_ref), (gate_hbm, gate_ref), (w_hbm, w_ref), (x_hbm, x_ref)):
        step = source.shape[0] // 4
        for quarter in range(4):
            span = slice(quarter * step, (quarter + 1) * step)
            moves.append((source.at[span, :], target.at[span, :]))
    loads = [
        pltpu.make_async_copy(source, target, sems.at[number])
        for number, (source, target) in enumerate(moves)
    ]
    for load in loads:
        load.start()
    for load in loads[:needed]:
        load.wait()
    rows = x_ref.shape[0]
    slots = rows_ref.shape[0]
    late = jnp.dot(placement(slot_ref[...], slots), rows_ref[...], preferred_element_type=F32)
    for load in loads[needed:]:
        load.wait()
    tile = rows // 2
    stores = []
    for half in range(2):
        span = slice(half * tile, (half + 1) * tile)
        attn = jnp.concatenate([early_ref[span, :].astype(F32), late[span, :]], axis=1)
        centered = attn - jnp.mean(attn, axis=1, keepdims=True)
        variance = jnp.mean(centered * centered, axis=1, keepdims=True)
        normed = (centered * lax.rsqrt(variance + norm_eps) * gain_ref[...]).astype(BF16)
        mixed = (normed.astype(F32) * gate_ref[span, :].astype(F32)).astype(BF16)
        projected = jnp.dot(mixed, w_ref[...], preferred_element_type=F32)
        out_ref[span, :] = (x_ref[span, :].astype(F32) + projected).astype(BF16)
        store = pltpu.make_async_copy(out_ref.at[span, :], out_hbm.at[span, :], out_sems.at[half])
        store.start()
        stores.append(store)
    for store in stores:
        store.wait()


def finish(slot, early, gate, cand_x, ln_gain, w_out, parts):
    rows, width = cand_x.shape
    capacity, wide = parts[0].shape
    slots = len(parts) * capacity
    vmem = pl.BlockSpec(memory_space=pltpu.VMEM)
    anywhere = pl.BlockSpec(memory_space=pl.ANY)
    return pl.pallas_call(
        functools.partial(finish_kernel, len(parts)),
        in_specs=[vmem] + [anywhere] * (5 + len(parts)),
        out_specs=anywhere,
        out_shape=jax.ShapeDtypeStruct((rows, width), BF16),
        scratch_shapes=[
            pltpu.VMEM(slot.shape, jnp.int32),
            pltpu.VMEM(early.shape, BF16),
            pltpu.VMEM((rows, width), BF16),
            pltpu.VMEM((rows, width), BF16),
            pltpu.VMEM((width, width), BF16),
            pltpu.VMEM((slots, wide), BF16),
            pltpu.VMEM((rows, width), BF16),
            pltpu.SemaphoreType.DMA((len(parts) + 17,)),
            pltpu.SemaphoreType.DMA((2,)),
        ],
        compiler_params=params(60),
        cost_estimate=cost(
            2 * rows * width * (width + slots), 2 * (3 * rows * width + width * width + slots * width)
        ),
        name="finish",
    )(ln_gain.reshape(1, width), slot, early, gate, cand_x, w_out, *parts)


def swap(array, axis, bits, count):
    return lax.ppermute(array, axis, [(i, i ^ bits) for i in range(count)])


def exchange(blocks):
    count = len(blocks)
    return [block if d == 0 else swap(block, "cand", d, count) for d, block in enumerate(blocks)]


def per_device(cand_x, cand_user, visible, hist_len, kv_cache, w_in, w_out, ln_gain):
    rows, width = cand_x.shape
    columns = lax.axis_size("cand")
    count = lax.axis_size("user")
    size = width // HEADS
    capacity = 2 * rows // columns
    own = kv_cache[0]
    me = lax.axis_index("cand").astype(jnp.int32)
    owner_row = cand_user.reshape(1, rows)
    visible_row = visible.reshape(1, rows)

    spans = [(sum(GROUPS[:number]), heads) for number, heads in enumerate(GROUPS)]
    far = []
    for first, heads in spans:
        lo, hi = first * size, (first + heads) * size
        held = {0: jnp.concatenate([own[:, lo:hi], own[:, width + lo : width + hi]], axis=1)}
        bit = count // 2
        while bit > 1:
            for key in sorted(held):
                held[key | bit] = swap(held[key], "user", bit, count)
            bit //= 2
        far.append(held)
    evens = sorted(far[0])
    near = swap(own, "user", 1, count)

    send = project_queries(owner_row, visible_row, cand_x, w_in, columns, capacity)
    got = lax.all_to_all(
        send.reshape(columns, capacity, -1), "cand", split_axis=0, concat_axis=0, tiled=True
    ).reshape(columns * capacity, -1)
    gate = project_gate(cand_x, w_in)
    arrived = [near] + [held[evens[-1]] for held in far]
    slot = slot_column(owner_row ^ me, columns, capacity, [gate] + arrived)
    position = lax.axis_index("user").astype(jnp.int32)
    order = [0, 1] + evens[1:] + [key | 1 for key in evens[1:]]
    shards = position ^ jnp.array(order, jnp.int32)
    head = jnp.concatenate([hist_len, me[None]])
    place_first = jnp.concatenate([head, shards[:2]])
    place = jnp.concatenate([head, shards[2:]])
    base = attend(
        place_first,
        [slot],
        got,
        [(own, 0, HEADS), (near, 0, HEADS)],
        None,
        0,
        HEADS,
        size,
        1,
        F32,
    )[0]

    def forward(number, behind):
        parts = [far[number][key] for key in evens[1:]]
        if behind is not None:
            parts, _ = lax.optimization_barrier((parts, behind))
        return [swap(part, "user", 1, count) for part in parts]

    cuts = [forward(0, None)]
    returned = []
    after = []
    done = base
    for number, (first, heads) in enumerate(spans):
        if number + 1 < len(spans):
            cuts.append(forward(number + 1, (cuts[number], done)))
        segments = [(far[number][key], 0, heads) for key in evens[1:]]
        segments += [(cut, 0, heads) for cut in cuts[number]]
        attn = attend(place, after, got, segments, base, first, heads, size, columns, BF16)
        done = attn[0]
        after = [attn[0]] + [group[-1] for group in returned[-1:]]
        returned.append(exchange(attn))
    early = collect(slot, returned[:-1])
    return finish(slot, early, gate, cand_x, ln_gain, w_out, returned[-1])


def solution(mesh):
    in_specs = (
        P(("user", "cand"), None),
        P(("user", "cand"), None),
        P(("user", "cand")),
        P("cand"),
        P("cand", "user", None),
        P(),
        P(),
        P(),
    )
    out_specs = P(("user", "cand"), None)
    return jax.shard_map(
        per_device, mesh=mesh, in_specs=in_specs, out_specs=out_specs, check_vma=False
    )
```

```python
import functools
import math

import jax
import jax.numpy as jnp
from jax import lax
from jax.experimental import pallas as pl
from jax.experimental.pallas import tpu as pltpu
from jax.sharding import PartitionSpec as P

HEADS = 8
BLK = 128
GROUPS = (4, 4)
norm_eps = 1e-06
F32 = jnp.float32
BF16 = jnp.bfloat16
MIB = 1024 * 1024
WAIT_COST = 20.0
KERNEL_MIB = 24


def params(mib):
    return pltpu.CompilerParams(vmem_limit_bytes=mib * MIB)


def cost(flops, nbytes, transcendentals=0):
    return pl.CostEstimate(
        flops=int(flops), bytes_accessed=int(nbytes), transcendentals=int(transcendentals)
    )


def silu(v):
    half = 0.5 * v
    return half * jnp.tanh(half) + half


def earlier_mask(rows):
    first = lax.broadcasted_iota(jnp.int32, (rows, rows), 0)
    second = lax.broadcasted_iota(jnp.int32, (rows, rows), 1)
    return (first < second).astype(BF16)


def slot_row(owner_row, columns, capacity):
    rows = owner_row.shape[1]
    users = lax.broadcasted_iota(jnp.int32, (columns, rows), 0)
    mine = users == owner_row
    before = jnp.dot(mine.astype(BF16), earlier_mask(rows), preferred_element_type=F32)
    rank = jnp.sum(jnp.where(mine, before, 0.0), axis=0, keepdims=True)
    return owner_row.astype(F32) * capacity + rank


def whole(count=1):
    return [pl.BlockSpec(memory_space=pltpu.VMEM)] * count


def unread(arrays):
    return [pl.BlockSpec(memory_space=pl.ANY)] * len(arrays)


def query_kernel(columns, capacity, owner_ref, visible_ref, x_ref, w_ref, send_ref):
    rows, width = x_ref.shape
    slots = columns * capacity
    slot = slot_row(owner_ref[...], columns, capacity).astype(jnp.int32)
    index = lax.broadcasted_iota(jnp.int32, (slots, rows), 0)
    place = (index == slot).astype(BF16)
    tile = min(256, width)
    for start in range(0, width, tile):
        span = slice(start, start + tile)
        hidden = jnp.dot(x_ref[...], w_ref[:, span], preferred_element_type=F32)
        moved = jnp.dot(place, silu(hidden).astype(BF16), preferred_element_type=F32)
        send_ref[:, span] = moved.astype(BF16)
    seen = jnp.broadcast_to(visible_ref[...].astype(F32), (BLK, rows)).T.astype(BF16)
    send_ref[:, width:] = jnp.dot(place, seen, preferred_element_type=F32).astype(BF16)


def project_queries(owner_row, visible_row, cand_x, w_in, columns, capacity):
    rows, width = cand_x.shape
    slots = columns * capacity
    return pl.pallas_call(
        functools.partial(query_kernel, columns, capacity),
        in_specs=whole(4),
        out_specs=whole()[0],
        out_shape=jax.ShapeDtypeStruct((slots, width + BLK), BF16),
        compiler_params=params(KERNEL_MIB),
        cost_estimate=cost(
            2 * rows * width * width + 2 * slots * rows * width,
            2 * (rows * width + width * width + slots * width),
            rows * width,
        ),
        name="project_queries",
    )(owner_row, visible_row, cand_x, w_in)


def gate_kernel(x_ref, w_ref, gate_ref):
    width = x_ref.shape[1]
    tile = min(256, width)
    for start in range(0, width, tile):
        columns = w_ref[:, width + start : width + start + tile]
        hidden = jnp.dot(x_ref[...], columns, preferred_element_type=F32)
        gate_ref[:, start : start + tile] = silu(hidden).astype(BF16)


def project_gate(cand_x, w_in):
    rows, width = cand_x.shape
    return pl.pallas_call(
        gate_kernel,
        in_specs=whole(2),
        out_specs=whole()[0],
        out_shape=jax.ShapeDtypeStruct((rows, width), BF16),
        compiler_params=params(KERNEL_MIB),
        cost_estimate=cost(
            2 * rows * width * width, 2 * (2 * rows * width + width * width), rows * width
        ),
        name="project_gate",
    )(cand_x, w_in)


def slots_kernel(columns, capacity, owner_ref, *refs):
    slot = slot_row(owner_ref[...], columns, capacity)
    refs[-1][...] = jnp.broadcast_to(slot, (BLK, slot.shape[1])).T.astype(jnp.int32)


def slot_column(owner_row, columns, capacity, after):
    rows = owner_row.shape[1]
    return pl.pallas_call(
        functools.partial(slots_kernel, columns, capacity),
        in_specs=whole() + unread(after),
        out_specs=whole()[0],
        out_shape=jax.ShapeDtypeStruct((rows, BLK), jnp.int32),
        compiler_params=params(KERNEL_MIB),
        cost_estimate=cost(WAIT_COST * 1e9, 4 * rows * BLK),
        name="slot_column",
    )(owner_row, *after)


def attend_kernel(size, heads, first, starts, behind, has_base, outs, place_ref, *refs):
    refs = refs[behind:]
    rows_ref, refs = refs[0], refs[1:]
    parts, refs = refs[: len(starts)], refs[len(starts) :]
    base_ref = refs[0] if has_base else None
    out_refs, shown = refs[int(has_base) : int(has_base) + outs], refs[int(has_base) + outs]
    result = out_refs[0] if outs == 1 else refs[-1]
    slots = rows_ref.shape[0]
    keys = parts[0].shape[0]
    blocks = keys // BLK
    seen = rows_ref[:, HEADS * size :].astype(F32)
    for number in range(len(parts)):
        for block in range(blocks):
            start = (place_ref[2 + number] * blocks + block).astype(F32)
            shown[number * blocks + block] = jnp.where(start < seen, 0.5 / math.sqrt(size), 0.0)
    row = lax.broadcasted_iota(jnp.int32, (keys, size), 0)
    tile = min(512, slots)

    def columns(head):
        return pl.ds(pl.multiple_of(head * size, size), size)

    def one_head(head, carry):
        values = []
        for number, part in enumerate(parts):
            inside = row + place_ref[2 + number] * keys < place_ref[0]
            value = part[:, columns(starts[number][1] + head)].astype(F32)
            values.append(jnp.where(inside, value, 0.0).astype(BF16))
        values = jnp.concatenate(values, axis=0)
        for start in range(0, slots, tile):
            span = slice(start, start + tile)
            queries = rows_ref[span, columns(first + head)]
            weights = []
            for number, part in enumerate(parts):
                scores = lax.dot_general(
                    queries,
                    part[:, columns(starts[number][0] + head)],
                    (((1,), (1,)), ((), ())),
                    preferred_element_type=F32,
                )
                for block in range(blocks):
                    half = scores[:, block * BLK : (block + 1) * BLK]
                    half = half * shown[number * blocks + block, span, :]
                    weights.append((half * jnp.tanh(half) + half).astype(BF16))
            total = jnp.dot(
                jnp.concatenate(weights, axis=1), values, preferred_element_type=F32
            )
            if has_base:
                total = total + base_ref[span, columns(first + head)]
            result[span, columns(head)] = total.astype(result.dtype)
        return carry

    lax.fori_loop(0, heads, one_head, 0)
    if outs > 1:
        capacity = slots // outs
        for number, ref in enumerate(out_refs):
            start = pl.multiple_of((place_ref[1] ^ number) * capacity, capacity)
            ref[...] = result[pl.ds(start, capacity), :]


def attend(place, after, rows, segments, base, first, heads, size, outs, dtype):
    slots = rows.shape[0]
    keys = segments[0][0].shape[0]
    count = len(segments)
    starts = [(key, value) for _, key, value in segments]
    extra = [] if base is None else [base]
    scratch = [pltpu.VMEM((count * (keys // BLK), slots, BLK), F32)]
    if outs > 1:
        scratch.append(pltpu.VMEM((slots, heads * size), BF16))
    return pl.pallas_call(
        functools.partial(
            attend_kernel, size, heads, first, starts, len(after), base is not None, outs
        ),
        in_specs=[pl.BlockSpec(memory_space=pltpu.SMEM)]
        + unread(after)
        + whole(1 + count + len(extra)),
        out_specs=whole(outs),
        out_shape=[jax.ShapeDtypeStruct((slots // outs, heads * size), dtype)] * outs,
        scratch_shapes=scratch,
        compiler_params=params(KERNEL_MIB),
        cost_estimate=cost(
            4 * slots * keys * count * heads * size,
            2 * (2 * slots + count * keys * 2) * heads * size,
            slots * keys * count * heads,
        ),
        name="attend",
    )(place, *after, rows, *[piece for piece, _, _ in segments], *extra)


def placement(slot, slots):
    lane = lax.broadcasted_iota(jnp.int32, (1, BLK), 1)
    return jnp.concatenate(
        [(lane + start == slot).astype(BF16) for start in range(0, slots, BLK)], axis=1
    )


def collect_kernel(groups, slot_ref, *refs):
    parts, out_ref = refs[:-1], refs[-1]
    each = len(parts) // groups
    place = placement(slot_ref[...], each * parts[0].shape[0])
    first = 0
    for group in range(groups):
        rows = jnp.concatenate(
            [part[...] for part in parts[group * each : (group + 1) * each]], axis=0
        )
        last = first + rows.shape[1]
        out_ref[:, first:last] = jnp.dot(place, rows, preferred_element_type=F32).astype(BF16)
        first = last


def collect(slot, groups):
    rows = slot.shape[0]
    parts = [part for group in groups for part in group]
    width = sum(group[0].shape[1] for group in groups)
    slots = len(groups[0]) * groups[0][0].shape[0]
    vmem = pl.BlockSpec(memory_space=pltpu.VMEM)
    return pl.pallas_call(
        functools.partial(collect_kernel, len(groups)),
        in_specs=[vmem] * (1 + len(parts)),
        out_specs=vmem,
        out_shape=jax.ShapeDtypeStruct((rows, width), BF16),
        compiler_params=params(KERNEL_MIB),
        cost_estimate=cost(2 * rows * slots * width, 2 * (rows + slots) * width),
        name="collect",
    )(slot, *parts)


def finish_kernel(slot_ref, gain_ref, early_ref, gate_ref, x_ref, w_ref, *refs):
    parts, (out_hbm, out_ref, sems) = refs[:-3], refs[-3:]
    rows = x_ref.shape[0]
    returned = jnp.concatenate([part[...] for part in parts], axis=0)
    place = placement(slot_ref[...], returned.shape[0])
    late = jnp.dot(place, returned, preferred_element_type=F32)
    tile = rows // 2
    stores = []
    for half in range(2):
        span = slice(half * tile, (half + 1) * tile)
        attn = jnp.concatenate([early_ref[span, :].astype(F32), late[span, :]], axis=1)
        centered = attn - jnp.mean(attn, axis=1, keepdims=True)
        variance = jnp.mean(centered * centered, axis=1, keepdims=True)
        normed = (centered * lax.rsqrt(variance + norm_eps) * gain_ref[...]).astype(BF16)
        mixed = (normed.astype(F32) * gate_ref[span, :].astype(F32)).astype(BF16)
        projected = jnp.dot(mixed, w_ref[...], preferred_element_type=F32)
        out_ref[span, :] = (x_ref[span, :].astype(F32) + projected).astype(BF16)
        store = pltpu.make_async_copy(out_ref.at[span, :], out_hbm.at[span, :], sems.at[half])
        store.start()
        stores.append(store)
    for store in stores:
        store.wait()


def finish(slot, early, gate, cand_x, ln_gain, w_out, parts):
    rows, width = cand_x.shape
    slots = len(parts) * parts[0].shape[0]
    return pl.pallas_call(
        finish_kernel,
        in_specs=whole(6 + len(parts)),
        out_specs=pl.BlockSpec(memory_space=pl.ANY),
        out_shape=jax.ShapeDtypeStruct((rows, width), BF16),
        scratch_shapes=[pltpu.VMEM((rows, width), BF16), pltpu.SemaphoreType.DMA((2,))],
        compiler_params=params(KERNEL_MIB),
        cost_estimate=cost(
            2 * rows * width * (width + slots), 2 * (3 * rows * width + width * width + slots * width)
        ),
        name="finish",
    )(slot, ln_gain.reshape(1, width), early, gate, cand_x, w_out, *parts)


def swap(array, axis, bits, count):
    return lax.ppermute(array, axis, [(i, i ^ bits) for i in range(count)])


def exchange(blocks):
    count = len(blocks)
    return [block if d == 0 else swap(block, "cand", d, count) for d, block in enumerate(blocks)]


def per_device(cand_x, cand_user, visible, hist_len, kv_cache, w_in, w_out, ln_gain):
    rows, width = cand_x.shape
    columns = lax.axis_size("cand")
    count = lax.axis_size("user")
    size = width // HEADS
    capacity = 2 * rows // columns
    own = kv_cache[0]
    me = lax.axis_index("cand").astype(jnp.int32)
    owner_row = cand_user.reshape(1, rows)
    visible_row = visible.reshape(1, rows)

    spans = [(sum(GROUPS[:number]), heads) for number, heads in enumerate(GROUPS)]
    far = []
    for first, heads in spans:
        lo, hi = first * size, (first + heads) * size
        held = {0: jnp.concatenate([own[:, lo:hi], own[:, width + lo : width + hi]], axis=1)}
        bit = count // 2
        while bit > 1:
            for key in sorted(held):
                held[key | bit] = swap(held[key], "user", bit, count)
            bit //= 2
        far.append(held)
    evens = sorted(far[0])
    near = swap(own, "user", 1, count)

    send = project_queries(owner_row, visible_row, cand_x, w_in, columns, capacity)
    got = lax.all_to_all(
        send.reshape(columns, capacity, -1), "cand", split_axis=0, concat_axis=0, tiled=True
    ).reshape(columns * capacity, -1)
    gate = project_gate(cand_x, w_in)
    arrived = [near] + [held[evens[-1]] for held in far]
    slot = slot_column(owner_row ^ me, columns, capacity, [gate] + arrived)
    position = lax.axis_index("user").astype(jnp.int32)
    order = [0, 1] + evens[1:] + [key | 1 for key in evens[1:]]
    shards = position ^ jnp.array(order, jnp.int32)
    head = jnp.concatenate([hist_len, me[None]])
    place_first = jnp.concatenate([head, shards[:2]])
    place = jnp.concatenate([head, shards[2:]])
    base = attend(
        place_first,
        [slot],
        got,
        [(own, 0, HEADS), (near, 0, HEADS)],
        None,
        0,
        HEADS,
        size,
        1,
        F32,
    )[0]

    def forward(number, behind):
        parts = [far[number][key] for key in evens[1:]]
        if behind is not None:
            parts, _ = lax.optimization_barrier((parts, behind))
        return [swap(part, "user", 1, count) for part in parts]

    cuts = [forward(0, None)]
    returned = []
    after = []
    done = base
    for number, (first, heads) in enumerate(spans):
        if number + 1 < len(spans):
            cuts.append(forward(number + 1, (cuts[number], done)))
        segments = [(far[number][key], 0, heads) for key in evens[1:]]
        segments += [(cut, 0, heads) for cut in cuts[number]]
        attn = attend(place, after, got, segments, base, first, heads, size, columns, BF16)
        done = attn[0]
        after = [done] + [group[-1] for group in returned[-1:]]
        returned.append(exchange(attn))
    early = collect(slot, returned[:-1])
    return finish(slot, early, gate, cand_x, ln_gain, w_out, returned[-1])


def solution(mesh):
    in_specs = (
        P(("user", "cand"), None),
        P(("user", "cand"), None),
        P(("user", "cand")),
        P("cand"),
        P("cand", "user", None),
        P(),
        P(),
        P(),
    )
    out_specs = P(("user", "cand"), None)
    return jax.shard_map(
        per_device, mesh=mesh, in_specs=in_specs, out_specs=out_specs, check_vma=False
    )
```

```python
import functools
import math

import jax
import jax.numpy as jnp
from jax import lax
from jax.experimental import pallas as pl
from jax.experimental.pallas import tpu as pltpu
from jax.sharding import PartitionSpec as P

HEADS = 8
BLK = 128
GROUPS = (4, 4)
norm_eps = 1e-06
F32 = jnp.float32
BF16 = jnp.bfloat16
MIB = 1024 * 1024
WAIT_COST = 20.0
KERNEL_MIB = 24
QUERY_MIB = 60


def params(mib):
    return pltpu.CompilerParams(vmem_limit_bytes=mib * MIB)


def cost(flops, nbytes, transcendentals=0):
    return pl.CostEstimate(
        flops=int(flops), bytes_accessed=int(nbytes), transcendentals=int(transcendentals)
    )


def silu(v):
    half = 0.5 * v
    return half * jnp.tanh(half) + half


def earlier_mask(rows):
    first = lax.broadcasted_iota(jnp.int32, (rows, rows), 0)
    second = lax.broadcasted_iota(jnp.int32, (rows, rows), 1)
    return (first < second).astype(BF16)


def slot_row(owner_row, columns, capacity):
    rows = owner_row.shape[1]
    users = lax.broadcasted_iota(jnp.int32, (columns, rows), 0)
    mine = users == owner_row
    before = jnp.dot(mine.astype(BF16), earlier_mask(rows), preferred_element_type=F32)
    rank = jnp.sum(jnp.where(mine, before, 0.0), axis=0, keepdims=True)
    return owner_row.astype(F32) * capacity + rank


def whole(count=1):
    return [pl.BlockSpec(memory_space=pltpu.VMEM)] * count


def unread(arrays):
    return [pl.BlockSpec(memory_space=pl.ANY)] * len(arrays)


def split_kernel(spans, size, kv_ref, *out_refs):
    width = kv_ref.shape[1] // 2
    for (first, heads), ref in zip(spans, out_refs):
        lo, hi = first * size, (first + heads) * size
        ref[:, : hi - lo] = kv_ref[:, lo:hi]
        ref[:, hi - lo :] = kv_ref[:, width + lo : width + hi]


def split(kv, spans, size):
    rows = kv.shape[0]
    return pl.pallas_call(
        functools.partial(split_kernel, spans, size),
        in_specs=whole(),
        out_specs=whole(len(spans)),
        out_shape=[jax.ShapeDtypeStruct((rows, 2 * heads * size), BF16) for _, heads in spans],
        compiler_params=params(KERNEL_MIB),
        cost_estimate=cost(0, 4 * kv.size),
        name="split",
    )(kv)


def query_kernel(columns, capacity, owner_ref, visible_ref, x_hbm, w_hbm, send_hbm, *scratch):
    x_ref, w_ref, send_ref, x_sem, w_sems, out_sems = scratch
    rows, width = x_ref.shape
    slots = columns * capacity
    tile = min(256, width)
    spans = [slice(start, start + tile) for start in range(0, width, tile)]
    x_load = pltpu.make_async_copy(x_hbm, x_ref, x_sem)
    x_load.start()
    w_loads = []
    for number, span in enumerate(spans):
        load = pltpu.make_async_copy(w_hbm.at[:, span], w_ref.at[:, span], w_sems.at[number])
        load.start()
        w_loads.append(load)
    slot = slot_row(owner_ref[...], columns, capacity).astype(jnp.int32)
    index = lax.broadcasted_iota(jnp.int32, (slots, rows), 0)
    place = (index == slot).astype(BF16)
    seen = jnp.broadcast_to(visible_ref[...].astype(F32), (BLK, rows)).T.astype(BF16)
    send_ref[:, width:] = jnp.dot(place, seen, preferred_element_type=F32).astype(BF16)
    stores = []

    def store(span):
        copy = pltpu.make_async_copy(
            send_ref.at[:, span], send_hbm.at[:, span], out_sems.at[len(stores)]
        )
        copy.start()
        stores.append(copy)

    store(slice(width, width + BLK))
    x_load.wait()
    for number, span in enumerate(spans):
        w_loads[number].wait()
        hidden = jnp.dot(x_ref[...], w_ref[:, span], preferred_element_type=F32)
        moved = jnp.dot(place, silu(hidden).astype(BF16), preferred_element_type=F32)
        send_ref[:, span] = moved.astype(BF16)
        store(span)
    for copy in stores:
        copy.wait()


def project_queries(owner_row, visible_row, cand_x, w_in, columns, capacity):
    rows, width = cand_x.shape
    slots = columns * capacity
    count = width // min(256, width)
    anywhere = pl.BlockSpec(memory_space=pl.ANY)
    return pl.pallas_call(
        functools.partial(query_kernel, columns, capacity),
        in_specs=whole(2) + [anywhere, anywhere],
        out_specs=anywhere,
        out_shape=jax.ShapeDtypeStruct((slots, width + BLK), BF16),
        scratch_shapes=[
            pltpu.VMEM((rows, width), BF16),
            pltpu.VMEM((width, width), BF16),
            pltpu.VMEM((slots, width + BLK), BF16),
            pltpu.SemaphoreType.DMA,
            pltpu.SemaphoreType.DMA((count,)),
            pltpu.SemaphoreType.DMA((count + 1,)),
        ],
        compiler_params=params(QUERY_MIB),
        cost_estimate=cost(
            2 * rows * width * width + 2 * slots * rows * width,
            2 * (rows * width + width * width + slots * width),
            rows * width,
        ),
        name="project_queries",
    )(owner_row, visible_row, cand_x, w_in)


def gate_kernel(x_ref, w_ref, gate_ref):
    width = x_ref.shape[1]
    tile = min(256, width)
    for start in range(0, width, tile):
        columns = w_ref[:, width + start : width + start + tile]
        hidden = jnp.dot(x_ref[...], columns, preferred_element_type=F32)
        gate_ref[:, start : start + tile] = silu(hidden).astype(BF16)


def project_gate(cand_x, w_in):
    rows, width = cand_x.shape
    return pl.pallas_call(
        gate_kernel,
        in_specs=whole(2),
        out_specs=whole()[0],
        out_shape=jax.ShapeDtypeStruct((rows, width), BF16),
        compiler_params=params(KERNEL_MIB),
        cost_estimate=cost(
            2 * rows * width * width, 2 * (2 * rows * width + width * width), rows * width
        ),
        name="project_gate",
    )(cand_x, w_in)


def slots_kernel(columns, capacity, owner_ref, *refs):
    slot = slot_row(owner_ref[...], columns, capacity)
    refs[-1][...] = jnp.broadcast_to(slot, (BLK, slot.shape[1])).T.astype(jnp.int32)


def slot_column(owner_row, columns, capacity, after):
    rows = owner_row.shape[1]
    return pl.pallas_call(
        functools.partial(slots_kernel, columns, capacity),
        in_specs=whole() + unread(after),
        out_specs=whole()[0],
        out_shape=jax.ShapeDtypeStruct((rows, BLK), jnp.int32),
        compiler_params=params(KERNEL_MIB),
        cost_estimate=cost(WAIT_COST * 1e9, 4 * rows * BLK),
        name="slot_column",
    )(owner_row, *after)


def attend_kernel(size, heads, first, starts, behind, has_base, outs, place_ref, *refs):
    refs = refs[behind:]
    rows_ref, refs = refs[0], refs[1:]
    count = len(starts)
    parts, refs = refs[:count], refs[count:]
    base_ref = refs[0] if has_base else None
    out_refs, shown = refs[int(has_base) : int(has_base) + outs], refs[int(has_base) + outs]
    result = out_refs[0] if outs == 1 else refs[-1]
    slots = rows_ref.shape[0]
    keys = parts[0].shape[0]
    blocks = keys // BLK
    seen = rows_ref[:, HEADS * size :].astype(F32)
    for number in range(count):
        for block in range(blocks):
            start = (place_ref[2 + number] * blocks + block).astype(F32)
            shown[number * blocks + block] = (start < seen).astype(F32).astype(BF16)
    row = lax.broadcasted_iota(jnp.int32, (keys, size), 0)
    tile = min(512, slots)

    def columns(start):
        return pl.ds(pl.multiple_of(start, size), size)

    def one_head(head, carry):
        values = []
        for number, part in enumerate(parts):
            inside = row + place_ref[2 + number] * keys < place_ref[0]
            value = part[:, columns((starts[number][1] + head) * size)].astype(F32)
            values.append(jnp.where(inside, value, 0.0).astype(BF16))
        values = jnp.concatenate(values, axis=0)
        for start in range(0, slots, tile):
            span = slice(start, start + tile)
            queries = rows_ref[span, columns((first + head) * size)]
            weights = []
            for number, part in enumerate(parts):
                scores = lax.dot_general(
                    queries,
                    part[:, columns((starts[number][0] + head) * size)],
                    (((1,), (1,)), ((), ())),
                    preferred_element_type=F32,
                )
                for block in range(blocks):
                    half = scores[:, block * BLK : (block + 1) * BLK] * (0.5 / math.sqrt(size))
                    half = half.astype(BF16) * shown[number * blocks + block, span, :]
                    weights.append(half * jnp.tanh(half) + half)
            total = jnp.dot(
                jnp.concatenate(weights, axis=1), values, preferred_element_type=F32
            )
            if has_base:
                total = total + base_ref[span, columns((first + head) * size)]
            result[span, columns(head * size)] = total.astype(result.dtype)
        return carry

    lax.fori_loop(0, heads, one_head, 0)
    if outs > 1:
        capacity = slots // outs
        for number, ref in enumerate(out_refs):
            start = pl.multiple_of((place_ref[1] ^ number) * capacity, capacity)
            ref[...] = result[pl.ds(start, capacity), :]


def attend(place, after, rows, segments, base, first, heads, size, outs, dtype):
    slots = rows.shape[0]
    keys = segments[0][0].shape[0]
    count = len(segments)
    starts = [(key, value) for _, key, value in segments]
    extra = [] if base is None else [base]
    scratch = [pltpu.VMEM((count * (keys // BLK), slots, BLK), BF16)]
    if outs > 1:
        scratch.append(pltpu.VMEM((slots, heads * size), BF16))
    return pl.pallas_call(
        functools.partial(
            attend_kernel, size, heads, first, starts, len(after), base is not None, outs
        ),
        in_specs=[pl.BlockSpec(memory_space=pltpu.SMEM)]
        + unread(after)
        + whole(1 + count + len(extra)),
        out_specs=whole(outs),
        out_shape=[jax.ShapeDtypeStruct((slots // outs, heads * size), dtype)] * outs,
        scratch_shapes=scratch,
        compiler_params=params(KERNEL_MIB),
        cost_estimate=cost(
            4 * slots * keys * count * heads * size,
            2 * (2 * slots + count * keys * 2) * heads * size,
            slots * keys * count * heads,
        ),
        name="attend",
    )(place, *after, rows, *[piece for piece, _, _ in segments], *extra)


def placement(slot, slots):
    lane = lax.broadcasted_iota(jnp.int32, (1, BLK), 1)
    return jnp.concatenate(
        [(lane + start == slot).astype(BF16) for start in range(0, slots, BLK)], axis=1
    )


def collect_kernel(groups, slot_ref, *refs):
    parts, out_ref = refs[:-1], refs[-1]
    each = len(parts) // groups
    place = placement(slot_ref[...], each * parts[0].shape[0])
    first = 0
    for group in range(groups):
        rows = jnp.concatenate(
            [part[...] for part in parts[group * each : (group + 1) * each]], axis=0
        )
        last = first + rows.shape[1]
        out_ref[:, first:last] = jnp.dot(place, rows, preferred_element_type=F32).astype(BF16)
        first = last


def collect(slot, groups):
    rows = slot.shape[0]
    parts = [part for group in groups for part in group]
    width = sum(group[0].shape[1] for group in groups)
    slots = len(groups[0]) * groups[0][0].shape[0]
    vmem = pl.BlockSpec(memory_space=pltpu.VMEM)
    return pl.pallas_call(
        functools.partial(collect_kernel, len(groups)),
        in_specs=[vmem] * (1 + len(parts)),
        out_specs=vmem,
        out_shape=jax.ShapeDtypeStruct((rows, width), BF16),
        compiler_params=params(KERNEL_MIB),
        cost_estimate=cost(2 * rows * slots * width, 2 * (rows + slots) * width),
        name="collect",
    )(slot, *parts)


def finish_kernel(slot_ref, gain_ref, early_ref, gate_ref, x_ref, w_ref, *refs):
    parts, (out_hbm, out_ref, sems) = refs[:-3], refs[-3:]
    rows = x_ref.shape[0]
    returned = jnp.concatenate([part[...] for part in parts], axis=0)
    place = placement(slot_ref[...], returned.shape[0])
    late = jnp.dot(place, returned, preferred_element_type=F32)
    tile = rows // 2
    stores = []
    for half in range(2):
        span = slice(half * tile, (half + 1) * tile)
        attn = jnp.concatenate([early_ref[span, :].astype(F32), late[span, :]], axis=1)
        centered = attn - jnp.mean(attn, axis=1, keepdims=True)
        variance = jnp.mean(centered * centered, axis=1, keepdims=True)
        normed = (centered * lax.rsqrt(variance + norm_eps) * gain_ref[...]).astype(BF16)
        mixed = (normed.astype(F32) * gate_ref[span, :].astype(F32)).astype(BF16)
        projected = jnp.dot(mixed, w_ref[...], preferred_element_type=F32)
        out_ref[span, :] = (x_ref[span, :].astype(F32) + projected).astype(BF16)
        store = pltpu.make_async_copy(out_ref.at[span, :], out_hbm.at[span, :], sems.at[half])
        store.start()
        stores.append(store)
    for store in stores:
        store.wait()


def finish(slot, early, gate, cand_x, ln_gain, w_out, parts):
    rows, width = cand_x.shape
    slots = len(parts) * parts[0].shape[0]
    return pl.pallas_call(
        finish_kernel,
        in_specs=whole(6 + len(parts)),
        out_specs=pl.BlockSpec(memory_space=pl.ANY),
        out_shape=jax.ShapeDtypeStruct((rows, width), BF16),
        scratch_shapes=[pltpu.VMEM((rows, width), BF16), pltpu.SemaphoreType.DMA((2,))],
        compiler_params=params(KERNEL_MIB),
        cost_estimate=cost(
            2 * rows * width * (width + slots), 2 * (3 * rows * width + width * width + slots * width)
        ),
        name="finish",
    )(slot, ln_gain.reshape(1, width), early, gate, cand_x, w_out, *parts)


def swap(array, axis, bits, count):
    return lax.ppermute(array, axis, [(i, i ^ bits) for i in range(count)])


def exchange(blocks):
    count = len(blocks)
    order = sorted(range(1, count), key=lambda d: (d & 1, d >> 1 == (count >> 1) - 1, d))
    back = {0: blocks[0]}
    for d in order:
        back[d] = swap(blocks[d], "cand", d, count)
    return [back[d] for d in range(count)]


def per_device(cand_x, cand_user, visible, hist_len, kv_cache, w_in, w_out, ln_gain):
    rows, width = cand_x.shape
    columns = lax.axis_size("cand")
    count = lax.axis_size("user")
    size = width // HEADS
    capacity = 2 * rows // columns
    slots = columns * capacity
    me = lax.axis_index("cand").astype(jnp.int32)
    owner_row = cand_user.reshape(1, rows)
    visible_row = visible.reshape(1, rows)
    spans = [(sum(GROUPS[:number]), heads) for number, heads in enumerate(GROUPS)]

    held = {0: kv_cache[0], 1: swap(kv_cache[0], "user", 1, count)}
    bit = count // 2
    while bit > 1:
        for key in sorted(key for key in held if key != 1):
            held[key | bit] = swap(held[key], "user", bit, count)
        bit //= 2
    ready = sorted(held)
    late = [key | 1 for key in ready if key > 1]

    send = project_queries(owner_row, visible_row, cand_x, w_in, columns, capacity)
    got = lax.all_to_all(
        send.reshape(columns, capacity, -1), "cand", split_axis=0, concat_axis=0, tiled=True
    ).reshape(slots, -1)
    gate = project_gate(cand_x, w_in)
    arrived = [held[key] for key in ready if key]
    slot = slot_column(owner_row ^ me, columns, capacity, [gate] + arrived)
    position = lax.axis_index("user").astype(jnp.int32)
    shards = position ^ jnp.array(ready + late, jnp.int32)
    head = jnp.concatenate([hist_len, me[None]])
    place_ready = jnp.concatenate([head, shards[: len(ready)]])
    place_late = jnp.concatenate([head, shards[len(ready) :]])

    segments = [(held[key], 0, HEADS) for key in ready]
    base = attend(place_ready, [slot], got, segments, None, 0, HEADS, size, 1, F32)[0]
    passed = [split(held[key ^ 1], spans, size) for key in late]
    cuts = []
    for number in range(len(spans)):
        parts = [pieces[number] for pieces in passed]
        if number:
            parts, _ = lax.optimization_barrier((parts, (cuts[-1], base)))
        cuts.append([swap(part, "user", 1, count) for part in parts])
    returned = []
    after = []
    for number, (first, heads) in enumerate(spans):
        segments = [(cut, 0, heads) for cut in cuts[number]]
        attn = attend(
            place_late, after, got, segments, base, first, heads, size, columns, BF16
        )
        after = [attn[0]]
        returned.append(exchange(attn))
    early = collect(slot, returned[:-1])
    return finish(slot, early, gate, cand_x, ln_gain, w_out, returned[-1])


def solution(mesh):
    in_specs = (
        P(("user", "cand"), None),
        P(("user", "cand"), None),
        P(("user", "cand")),
        P("cand"),
        P("cand", "user", None),
        P(),
        P(),
        P(),
    )
    out_specs = P(("user", "cand"), None)
    return jax.shard_map(
        per_device, mesh=mesh, in_specs=in_specs, out_specs=out_specs, check_vma=False
    )
```

```python
import functools
import math

import jax
import jax.numpy as jnp
from jax import lax
from jax.experimental import pallas as pl
from jax.experimental.pallas import tpu as pltpu
from jax.sharding import PartitionSpec as P

HEADS = 8
BLK = 128
GROUPS = (4, 4)
norm_eps = 1e-06
F32 = jnp.float32
BF16 = jnp.bfloat16
MIB = 1024 * 1024
WAIT_COST = 30.0
LATE_SHARE = 20.0
COLLECT_COST = 20.0
KERNEL_MIB = 24
QUERY_MIB = 60


def params(mib):
    return pltpu.CompilerParams(vmem_limit_bytes=mib * MIB)


def cost(flops, nbytes, transcendentals=0):
    return pl.CostEstimate(
        flops=int(flops), bytes_accessed=int(nbytes), transcendentals=int(transcendentals)
    )


def silu(v):
    half = 0.5 * v
    return half * jnp.tanh(half) + half


def earlier_mask(rows):
    first = lax.broadcasted_iota(jnp.int32, (rows, rows), 0)
    second = lax.broadcasted_iota(jnp.int32, (rows, rows), 1)
    return (first < second).astype(BF16)


def slot_row(owner_row, columns, capacity):
    rows = owner_row.shape[1]
    users = lax.broadcasted_iota(jnp.int32, (columns, rows), 0)
    mine = users == owner_row
    before = jnp.dot(mine.astype(BF16), earlier_mask(rows), preferred_element_type=F32)
    rank = jnp.sum(jnp.where(mine, before, 0.0), axis=0, keepdims=True)
    return owner_row.astype(F32) * capacity + rank


def whole(count=1):
    return [pl.BlockSpec(memory_space=pltpu.VMEM)] * count


def unread(arrays):
    return [pl.BlockSpec(memory_space=pl.ANY)] * len(arrays)


def split_kernel(spans, size, kv_ref, *out_refs):
    width = kv_ref.shape[1] // 2
    for (first, heads), ref in zip(spans, out_refs):
        lo, hi = first * size, (first + heads) * size
        ref[:, : hi - lo] = kv_ref[:, lo:hi]
        ref[:, hi - lo :] = kv_ref[:, width + lo : width + hi]


def split(kv, spans, size):
    rows = kv.shape[0]
    return pl.pallas_call(
        functools.partial(split_kernel, spans, size),
        in_specs=whole(),
        out_specs=whole(len(spans)),
        out_shape=[jax.ShapeDtypeStruct((rows, 2 * heads * size), BF16) for _, heads in spans],
        compiler_params=params(KERNEL_MIB),
        cost_estimate=cost(0, 4 * kv.size),
        name="split",
    )(kv)


def query_kernel(columns, capacity, owner_ref, visible_ref, x_hbm, w_hbm, send_hbm, *scratch):
    x_ref, w_ref, send_ref, x_sem, w_sems, out_sems = scratch
    rows, width = x_ref.shape
    slots = columns * capacity
    tile = min(256, width)
    spans = [slice(start, start + tile) for start in range(0, width, tile)]
    x_load = pltpu.make_async_copy(x_hbm, x_ref, x_sem)
    x_load.start()
    w_loads = []
    for number, span in enumerate(spans):
        load = pltpu.make_async_copy(w_hbm.at[:, span], w_ref.at[:, span], w_sems.at[number])
        load.start()
        w_loads.append(load)
    slot = slot_row(owner_ref[...], columns, capacity).astype(jnp.int32)
    index = lax.broadcasted_iota(jnp.int32, (slots, rows), 0)
    place = (index == slot).astype(BF16)
    seen = jnp.broadcast_to(visible_ref[...].astype(F32), (BLK, rows)).T.astype(BF16)
    send_ref[:, width:] = jnp.dot(place, seen, preferred_element_type=F32).astype(BF16)
    stores = []

    def store(span):
        copy = pltpu.make_async_copy(
            send_ref.at[:, span], send_hbm.at[:, span], out_sems.at[len(stores)]
        )
        copy.start()
        stores.append(copy)

    store(slice(width, width + BLK))
    x_load.wait()
    for number, span in enumerate(spans):
        w_loads[number].wait()
        hidden = jnp.dot(x_ref[...], w_ref[:, span], preferred_element_type=F32)
        moved = jnp.dot(place, silu(hidden).astype(BF16), preferred_element_type=F32)
        send_ref[:, span] = moved.astype(BF16)
        store(span)
    for copy in stores:
        copy.wait()


def project_queries(owner_row, visible_row, cand_x, w_in, columns, capacity):
    rows, width = cand_x.shape
    slots = columns * capacity
    count = width // min(256, width)
    anywhere = pl.BlockSpec(memory_space=pl.ANY)
    return pl.pallas_call(
        functools.partial(query_kernel, columns, capacity),
        in_specs=whole(2) + [anywhere, anywhere],
        out_specs=anywhere,
        out_shape=jax.ShapeDtypeStruct((slots, width + BLK), BF16),
        scratch_shapes=[
            pltpu.VMEM((rows, width), BF16),
            pltpu.VMEM((width, width), BF16),
            pltpu.VMEM((slots, width + BLK), BF16),
            pltpu.SemaphoreType.DMA,
            pltpu.SemaphoreType.DMA((count,)),
            pltpu.SemaphoreType.DMA((count + 1,)),
        ],
        compiler_params=params(QUERY_MIB),
        cost_estimate=cost(
            2 * rows * width * width + 2 * slots * rows * width,
            2 * (rows * width + width * width + slots * width),
            rows * width,
        ),
        name="project_queries",
    )(owner_row, visible_row, cand_x, w_in)


def gate_kernel(x_ref, w_ref, gate_ref):
    width = x_ref.shape[1]
    tile = min(256, width)
    for start in range(0, width, tile):
        columns = w_ref[:, width + start : width + start + tile]
        hidden = jnp.dot(x_ref[...], columns, preferred_element_type=F32)
        gate_ref[:, start : start + tile] = silu(hidden).astype(BF16)


def project_gate(cand_x, w_in):
    rows, width = cand_x.shape
    return pl.pallas_call(
        gate_kernel,
        in_specs=whole(2),
        out_specs=whole()[0],
        out_shape=jax.ShapeDtypeStruct((rows, width), BF16),
        compiler_params=params(KERNEL_MIB),
        cost_estimate=cost(
            2 * rows * width * width, 2 * (2 * rows * width + width * width), rows * width
        ),
        name="project_gate",
    )(cand_x, w_in)


def slots_kernel(columns, capacity, owner_ref, *refs):
    slot = slot_row(owner_ref[...], columns, capacity)
    refs[-1][...] = jnp.broadcast_to(slot, (BLK, slot.shape[1])).T.astype(jnp.int32)


def slot_column(owner_row, columns, capacity, after):
    rows = owner_row.shape[1]
    return pl.pallas_call(
        functools.partial(slots_kernel, columns, capacity),
        in_specs=whole() + unread(after),
        out_specs=whole()[0],
        out_shape=jax.ShapeDtypeStruct((rows, BLK), jnp.int32),
        compiler_params=params(KERNEL_MIB),
        cost_estimate=cost(WAIT_COST * 1e9, 4 * rows * BLK),
        name="slot_column",
    )(owner_row, *after)


def attend_kernel(size, heads, first, starts, behind, has_base, capacity, place_ref, *refs):
    refs = refs[behind:]
    rows_ref, refs = refs[0], refs[1:]
    count = len(starts)
    parts = []
    for _, _, pieces in starts:
        parts.append(refs[:pieces])
        refs = refs[pieces:]
    base_ref = refs[0] if has_base else None
    outs = 3 if capacity else 1
    out_refs, shown = refs[int(has_base) : int(has_base) + outs], refs[int(has_base) + outs]
    result = out_refs[0] if outs == 1 else refs[-1]
    slots = rows_ref.shape[0]
    columns_of = slots // capacity if capacity else 1
    keys = sum(piece.shape[0] for piece in parts[0])
    blocks = keys // BLK
    seen = rows_ref[:, HEADS * size :].astype(F32)
    for number in range(count):
        for block in range(blocks):
            start = (place_ref[2 + number] * blocks + block).astype(F32)
            shown[number * blocks + block] = (start < seen).astype(F32).astype(BF16)
    row = lax.broadcasted_iota(jnp.int32, (keys, size), 0)
    tile = min(512, slots)

    def columns(start):
        return pl.ds(pl.multiple_of(start, size), size)

    def read(part, start):
        return jnp.concatenate([piece[:, columns(start)] for piece in part], axis=0)

    def one_head(head, carry):
        values = []
        for number, part in enumerate(parts):
            inside = row + place_ref[2 + number] * keys < place_ref[0]
            value = read(part, (starts[number][1] + head) * size).astype(F32)
            values.append(jnp.where(inside, value, 0.0).astype(BF16))
        values = jnp.concatenate(values, axis=0)
        for start in range(0, slots, tile):
            span = slice(start, start + tile)
            queries = rows_ref[span, columns((first + head) * size)]
            weights = []
            for number, part in enumerate(parts):
                scores = lax.dot_general(
                    queries,
                    read(part, (starts[number][0] + head) * size),
                    (((1,), (1,)), ((), ())),
                    preferred_element_type=F32,
                )
                for block in range(blocks):
                    half = scores[:, block * BLK : (block + 1) * BLK] * (0.5 / math.sqrt(size))
                    half = half.astype(BF16) * shown[number * blocks + block, span, :]
                    weights.append(half * jnp.tanh(half) + half)
            total = jnp.dot(
                jnp.concatenate(weights, axis=1), values, preferred_element_type=F32
            )
            if has_base:
                total = total + base_ref[span, columns(head * size)]
            result[span, columns(head * size)] = total.astype(result.dtype)
        return carry

    lax.fori_loop(0, heads, one_head, 0)
    if outs > 1:
        numbers = list(range(0, columns_of, 2)) + list(range(1, columns_of, 2))
        for ref in out_refs:
            for start in range(0, ref.shape[0], capacity):
                block = place_ref[1] ^ numbers.pop(0)
                source = pl.ds(pl.multiple_of(block * capacity, capacity), capacity)
                ref[start : start + capacity, :] = result[source, :]


def attend(place, after, rows, segments, base, first, heads, size, capacity, dtype, share):
    slots = rows.shape[0]
    keys = sum(piece.shape[0] for piece in segments[0][0])
    count = len(segments)
    starts = [(key, value, len(pieces)) for pieces, key, value in segments]
    pieces = [piece for pieces, _, _ in segments for piece in pieces]
    heights = [slots // 2, slots // 4, slots // 4] if capacity else [slots]
    outs = len(heights)
    extra = [] if base is None else [base]
    scratch = [pltpu.VMEM((count * (keys // BLK), slots, BLK), BF16)]
    if outs > 1:
        scratch.append(pltpu.VMEM((slots, heads * size), BF16))
    return pl.pallas_call(
        functools.partial(
            attend_kernel, size, heads, first, starts, len(after), base is not None, capacity
        ),
        in_specs=[pl.BlockSpec(memory_space=pltpu.SMEM)]
        + unread(after)
        + whole(1 + len(pieces) + len(extra)),
        out_specs=whole(outs),
        out_shape=[jax.ShapeDtypeStruct((height, heads * size), dtype) for height in heights],
        scratch_shapes=scratch,
        compiler_params=params(KERNEL_MIB),
        cost_estimate=cost(
            share * 4 * slots * keys * count * heads * size,
            2 * (2 * slots + count * keys * 2) * heads * size,
            slots * keys * count * heads,
        ),
        name="attend",
    )(place, *after, rows, *pieces, *extra)


def placement(slot, slots):
    lane = lax.broadcasted_iota(jnp.int32, (1, BLK), 1)
    return jnp.concatenate(
        [(lane + start == slot).astype(BF16) for start in range(0, slots, BLK)], axis=1
    )


def in_slots(parts, capacity):
    return jnp.concatenate(
        [part[:capacity, :] for part in parts[:2]] + [part[...] for part in parts[2:]], axis=0
    )


def collect_kernel(capacity, slots, slot_ref, *refs):
    rows = in_slots(refs[:-1], capacity)
    place = placement(slot_ref[...], slots)
    refs[-1][...] = jnp.dot(place, rows, preferred_element_type=F32).astype(BF16)


def collect(slot, parts, capacity, slots):
    rows, width = slot.shape[0], parts[0].shape[1]
    return pl.pallas_call(
        functools.partial(collect_kernel, capacity, slots),
        in_specs=whole(1 + len(parts)),
        out_specs=whole()[0],
        out_shape=jax.ShapeDtypeStruct((rows, width), BF16),
        compiler_params=params(KERNEL_MIB),
        cost_estimate=cost(COLLECT_COST * 1e9, 2 * (rows + slots) * width),
        name="collect",
    )(slot, *parts)


def finish_kernel(groups, capacity, slots, slot_ref, gain_ref, gate_ref, x_ref, w_ref, *refs):
    early, parts, (out_hbm, out_ref, sems) = refs[:groups], refs[groups:-3], refs[-3:]
    rows = x_ref.shape[0]
    place = placement(slot_ref[...], slots)
    late = jnp.dot(place, in_slots(parts, capacity), preferred_element_type=F32)
    tile = rows // 2
    stores = []
    for half in range(2):
        span = slice(half * tile, (half + 1) * tile)
        attn = jnp.concatenate([part[span, :].astype(F32) for part in early] + [late[span, :]], axis=1)
        centered = attn - jnp.mean(attn, axis=1, keepdims=True)
        variance = jnp.mean(centered * centered, axis=1, keepdims=True)
        normed = (centered * lax.rsqrt(variance + norm_eps) * gain_ref[...]).astype(BF16)
        mixed = (normed.astype(F32) * gate_ref[span, :].astype(F32)).astype(BF16)
        projected = jnp.dot(mixed, w_ref[...], preferred_element_type=F32)
        out_ref[span, :] = (x_ref[span, :].astype(F32) + projected).astype(BF16)
        store = pltpu.make_async_copy(out_ref.at[span, :], out_hbm.at[span, :], sems.at[half])
        store.start()
        stores.append(store)
    for store in stores:
        store.wait()


def finish(slot, early, gate, cand_x, ln_gain, w_out, parts, capacity, slots):
    rows, width = cand_x.shape
    return pl.pallas_call(
        functools.partial(finish_kernel, len(early), capacity, slots),
        in_specs=whole(5 + len(early) + len(parts)),
        out_specs=pl.BlockSpec(memory_space=pl.ANY),
        out_shape=jax.ShapeDtypeStruct((rows, width), BF16),
        scratch_shapes=[pltpu.VMEM((rows, width), BF16), pltpu.SemaphoreType.DMA((2,))],
        compiler_params=params(KERNEL_MIB),
        cost_estimate=cost(
            2 * rows * width * (width + slots), 2 * (3 * rows * width + width * width + slots * width)
        ),
        name="finish",
    )(slot, ln_gain.reshape(1, width), gate, cand_x, w_out, *early, *parts)


def swap(array, axis, bits, count):
    return lax.ppermute(array, axis, [(i, i ^ bits) for i in range(count)])


def forward(piece, number, count):
    if number == 0:
        return [swap(piece, "user", 1, count)]
    half = piece.shape[0] // 2
    upper = swap(piece[:half], "user", 1, count)
    lower, _ = lax.optimization_barrier((piece[half:], upper))
    return [upper, swap(lower, "user", 1, count)]


def exchange_cores(even, odds, capacity, count, behind):
    others = [swap(odd, "cand", 1, count) for odd in odds]
    if behind is not None:
        (even, others), _ = lax.optimization_barrier(((even, others), behind))
    pairs = []
    for d in range(1, count // 2):
        first, second = d * capacity, (d * capacity) % odds[0].shape[0]
        other = others[first // odds[0].shape[0]]
        pairs.append(
            jnp.concatenate(
                [even[first : first + capacity], other[second : second + capacity]], axis=0
            )
        )
    return [even, others[0]], pairs


def exchange_chips(pairs, count):
    return [swap(pair, "cand", 2 * d, count) for d, pair in enumerate(pairs, 1)]


def per_device(cand_x, cand_user, visible, hist_len, kv_cache, w_in, w_out, ln_gain):
    rows, width = cand_x.shape
    columns = lax.axis_size("cand")
    count = lax.axis_size("user")
    size = width // HEADS
    capacity = 2 * rows // columns
    slots = columns * capacity
    me = lax.axis_index("cand").astype(jnp.int32)
    owner_row = cand_user.reshape(1, rows)
    visible_row = visible.reshape(1, rows)
    spans = [(sum(GROUPS[:number]), heads) for number, heads in enumerate(GROUPS)]

    near = swap(kv_cache[0], "user", 1, count)
    far = []
    for own in split(kv_cache[0], spans, size):
        held = {0: own}
        bit = count // 2
        while bit > 1:
            for key in sorted(held):
                held[key | bit] = swap(held[key], "user", bit, count)
            bit //= 2
        far.append(held)
    evens = sorted(far[0])
    late = [key | 1 for key in evens[1:]]

    send = project_queries(owner_row, visible_row, cand_x, w_in, columns, capacity)
    got = lax.all_to_all(
        send.reshape(columns, capacity, -1), "cand", split_axis=0, concat_axis=0, tiled=True
    ).reshape(slots, -1)
    gate = project_gate(cand_x, w_in)
    arrived = [near] + [far[0][key] for key in evens[1:]]
    slot = slot_column(owner_row ^ me, columns, capacity, [gate] + arrived)
    position = lax.axis_index("user").astype(jnp.int32)
    shards = position ^ jnp.array(evens + [1] + late, jnp.int32)
    head = jnp.concatenate([hist_len, me[None]])
    place_ready = jnp.concatenate([head, shards[: len(evens) + 1]])
    place_late = jnp.concatenate([head, shards[len(evens) + 1 :]])

    early = []
    after = [slot]
    for number, (first, heads) in enumerate(spans):
        held = far[number]
        cuts = [(forward(held[key], number, count), 0, heads) for key in evens[1:]]
        segments = [([held[key]], 0, heads) for key in evens]
        segments.append(([near], first, HEADS + first))
        base = attend(
            place_ready, after, got, segments, None, first, heads, size, None, F32, 0.0
        )[0]
        attn = attend(
            place_late, [], got, cuts, base, first, heads, size, capacity, BF16, LATE_SHARE * (number > 0)
        )
        here, pairs = exchange_cores(attn[0], attn[1:], capacity, columns, early[-1] if early else None)
        after = [slot, attn[0]] + pairs
        returned = here + exchange_chips(pairs, columns)
        if number + 1 < len(spans):
            early.append(collect(slot, returned, capacity, slots))
    return finish(slot, early, gate, cand_x, ln_gain, w_out, returned, capacity, slots)


def solution(mesh):
    in_specs = (
        P(("user", "cand"), None),
        P(("user", "cand"), None),
        P(("user", "cand")),
        P("cand"),
        P("cand", "user", None),
        P(),
        P(),
        P(),
    )
    out_specs = P(("user", "cand"), None)
    return jax.shard_map(
        per_device, mesh=mesh, in_specs=in_specs, out_specs=out_specs, check_vma=False
    )
```

```python
import functools
import math

import jax
import jax.numpy as jnp
from jax import lax
from jax.experimental import pallas as pl
from jax.experimental.pallas import tpu as pltpu
from jax.sharding import PartitionSpec as P

HEADS = 8
BLK = 128
GROUPS = (4, 4)
norm_eps = 1e-06
F32 = jnp.float32
BF16 = jnp.bfloat16
MIB = 1024 * 1024
TOKEN = jax.ShapeDtypeStruct((8, BLK), jnp.int32)
WAIT_COST = 20.0
LATE_SHARE = 20.0
COLLECT_COST = 20.0
SPLIT_COST = 6.0
KERNEL_MIB = 24


def params(mib):
    return pltpu.CompilerParams(vmem_limit_bytes=mib * MIB)


def cost(flops, nbytes, transcendentals=0):
    return pl.CostEstimate(
        flops=int(flops), bytes_accessed=int(nbytes), transcendentals=int(transcendentals)
    )


def silu(v):
    half = 0.5 * v
    return half * jnp.tanh(half) + half


def earlier_mask(rows):
    first = lax.broadcasted_iota(jnp.int32, (rows, rows), 0)
    second = lax.broadcasted_iota(jnp.int32, (rows, rows), 1)
    return (first < second).astype(BF16)


def slot_row(owner_row, columns, capacity):
    rows = owner_row.shape[1]
    users = lax.broadcasted_iota(jnp.int32, (columns, rows), 0)
    mine = users == owner_row
    before = jnp.dot(mine.astype(BF16), earlier_mask(rows), preferred_element_type=F32)
    rank = jnp.sum(jnp.where(mine, before, 0.0), axis=0, keepdims=True)
    return owner_row.astype(F32) * capacity + rank


def whole(count=1):
    return [pl.BlockSpec(memory_space=pltpu.VMEM)] * count


def unread(arrays):
    return [pl.BlockSpec(memory_space=pl.ANY)] * len(arrays)


def split_kernel(spans, size, kv_hbm, *refs):
    out_refs, sems = refs[:-1], refs[-1]
    width = kv_hbm.shape[1] // 2
    copies = []
    for (first, heads), ref in zip(spans, out_refs):
        wide = heads * size
        for half in range(2):
            source = kv_hbm.at[:, half * width + first * size : half * width + first * size + wide]
            target = ref.at[:, half * wide : (half + 1) * wide]
            copies.append(pltpu.make_async_copy(source, target, sems.at[len(copies)]))
    for copy in copies:
        copy.start()
    for copy in copies:
        copy.wait()


def split(kv, spans, size):
    rows = kv.shape[0]
    return pl.pallas_call(
        functools.partial(split_kernel, spans, size),
        in_specs=[pl.BlockSpec(memory_space=pl.ANY)],
        out_specs=whole(len(spans)),
        out_shape=[jax.ShapeDtypeStruct((rows, 2 * heads * size), BF16) for _, heads in spans],
        scratch_shapes=[pltpu.SemaphoreType.DMA((2 * len(spans),))],
        compiler_params=params(KERNEL_MIB),
        cost_estimate=cost(SPLIT_COST * 1e9, 4 * kv.size),
        name="split",
    )(kv)


def query_kernel(columns, capacity, owner_ref, visible_ref, x_ref, w_ref, send_hbm, send_ref, sems):
    rows, width = x_ref.shape
    slots = columns * capacity
    slot = slot_row(owner_ref[...], columns, capacity).astype(jnp.int32)
    index = lax.broadcasted_iota(jnp.int32, (slots, rows), 0)
    place = (index == slot).astype(BF16)
    stores = []

    def store(span):
        copy = pltpu.make_async_copy(
            send_ref.at[:, span], send_hbm.at[:, span], sems.at[len(stores)]
        )
        copy.start()
        stores.append(copy)

    seen = jnp.broadcast_to(visible_ref[...].astype(F32), (BLK, rows)).T.astype(BF16)
    send_ref[:, width:] = jnp.dot(place, seen, preferred_element_type=F32).astype(BF16)
    store(slice(width, width + BLK))
    tile = min(256, width)
    for start in range(0, width, tile):
        span = slice(start, start + tile)
        hidden = jnp.dot(x_ref[...], w_ref[:, span], preferred_element_type=F32)
        moved = jnp.dot(place, silu(hidden).astype(BF16), preferred_element_type=F32)
        send_ref[:, span] = moved.astype(BF16)
        store(span)
    for copy in stores:
        copy.wait()


def project_queries(owner_row, visible_row, cand_x, w_in, columns, capacity):
    rows, width = cand_x.shape
    slots = columns * capacity
    return pl.pallas_call(
        functools.partial(query_kernel, columns, capacity),
        in_specs=whole(4),
        out_specs=pl.BlockSpec(memory_space=pltpu.HBM),
        out_shape=jax.ShapeDtypeStruct((slots, width + BLK), BF16),
        scratch_shapes=[
            pltpu.VMEM((slots, width + BLK), BF16),
            pltpu.SemaphoreType.DMA((width // min(256, width) + 1,)),
        ],
        compiler_params=params(KERNEL_MIB),
        cost_estimate=cost(
            2 * rows * width * width + 2 * slots * rows * width,
            2 * (rows * width + width * width + slots * width),
            rows * width,
        ),
        name="project_queries",
    )(owner_row, visible_row, cand_x, w_in)


def gate_kernel(x_ref, w_ref, gate_ref, token_ref):
    token_ref[...] = jnp.zeros_like(token_ref)
    width = x_ref.shape[1]
    tile = min(256, width)
    for start in range(0, width, tile):
        columns = w_ref[:, width + start : width + start + tile]
        hidden = jnp.dot(x_ref[...], columns, preferred_element_type=F32)
        gate_ref[:, start : start + tile] = silu(hidden).astype(BF16)


def project_gate(cand_x, w_in):
    rows, width = cand_x.shape
    return pl.pallas_call(
        gate_kernel,
        in_specs=whole(2),
        out_specs=whole(2),
        out_shape=[jax.ShapeDtypeStruct((rows, width), BF16), TOKEN],
        compiler_params=params(KERNEL_MIB),
        cost_estimate=cost(
            2 * rows * width * width, 2 * (2 * rows * width + width * width), rows * width
        ),
        name="project_gate",
    )(cand_x, w_in)


def slots_kernel(columns, capacity, owner_ref, *refs):
    refs[-1][...] = jnp.zeros_like(refs[-1])
    slot = slot_row(owner_ref[...], columns, capacity)
    refs[-2][...] = jnp.broadcast_to(slot, (BLK, slot.shape[1])).T.astype(jnp.int32)


def slot_column(owner_row, columns, capacity, after):
    rows = owner_row.shape[1]
    return pl.pallas_call(
        functools.partial(slots_kernel, columns, capacity),
        in_specs=whole() + unread(after),
        out_specs=whole(2),
        out_shape=[jax.ShapeDtypeStruct((rows, BLK), jnp.int32), TOKEN],
        compiler_params=params(KERNEL_MIB),
        cost_estimate=cost(WAIT_COST * 1e9, 4 * rows * BLK),
        name="slot_column",
    )(owner_row, *after)


def attend_kernel(size, heads, first, starts, behind, has_base, capacity, place_ref, *refs):
    refs = refs[behind:]
    rows_ref, refs = refs[0], refs[1:]
    count = len(starts)
    parts = []
    for _, _, pieces in starts:
        parts.append(refs[:pieces])
        refs = refs[pieces:]
    base_ref = refs[0] if has_base else None
    outs = 3 if capacity else 1
    out_refs, shown = refs[int(has_base) : int(has_base) + outs], refs[int(has_base) + outs]
    result = out_refs[0] if outs == 1 else refs[-1]
    slots = rows_ref.shape[0]
    columns_of = slots // capacity if capacity else 1
    keys = sum(piece.shape[0] for piece in parts[0])
    blocks = keys // BLK
    seen = rows_ref[:, HEADS * size :].astype(F32)
    for number in range(count):
        for block in range(blocks):
            start = (place_ref[2 + number] * blocks + block).astype(F32)
            shown[number * blocks + block] = (start < seen).astype(F32).astype(BF16)
    row = lax.broadcasted_iota(jnp.int32, (keys, size), 0)
    tile = min(512, slots)

    def columns(start):
        return slice(start, start + size)

    def read(part, start):
        return jnp.concatenate([piece[:, columns(start)] for piece in part], axis=0)

    def one_head(head):
        values = []
        for number, part in enumerate(parts):
            inside = row + place_ref[2 + number] * keys < place_ref[0]
            value = read(part, (starts[number][1] + head) * size).astype(F32)
            values.append(jnp.where(inside, value, 0.0).astype(BF16))
        values = jnp.concatenate(values, axis=0)
        for start in range(0, slots, tile):
            span = slice(start, start + tile)
            queries = rows_ref[span, columns((first + head) * size)]
            weights = []
            for number, part in enumerate(parts):
                scores = lax.dot_general(
                    queries,
                    read(part, (starts[number][0] + head) * size),
                    (((1,), (1,)), ((), ())),
                    preferred_element_type=F32,
                )
                for block in range(blocks):
                    half = scores[:, block * BLK : (block + 1) * BLK] * (0.5 / math.sqrt(size))
                    half = half.astype(BF16) * shown[number * blocks + block, span, :]
                    weights.append(half * jnp.tanh(half) + half)
            total = jnp.dot(
                jnp.concatenate(weights, axis=1), values, preferred_element_type=F32
            )
            if has_base:
                total = total + base_ref[span, columns(head * size)]
            result[span, columns(head * size)] = total.astype(result.dtype)

    for head in range(heads):
        one_head(head)
    if outs > 1:
        numbers = list(range(0, columns_of, 2)) + list(range(1, columns_of, 2))
        for ref in out_refs:
            for start in range(0, ref.shape[0], capacity):
                block = place_ref[1] ^ numbers.pop(0)
                source = pl.ds(pl.multiple_of(block * capacity, capacity), capacity)
                ref[start : start + capacity, :] = result[source, :]


def attend(place, after, rows, segments, base, first, heads, size, capacity, dtype, share):
    slots = rows.shape[0]
    keys = sum(piece.shape[0] for piece in segments[0][0])
    count = len(segments)
    starts = [(key, value, len(pieces)) for pieces, key, value in segments]
    pieces = [piece for pieces, _, _ in segments for piece in pieces]
    heights = [slots // 2, slots // 4, slots // 4] if capacity else [slots]
    outs = len(heights)
    extra = [] if base is None else [base]
    scratch = [pltpu.VMEM((count * (keys // BLK), slots, BLK), BF16)]
    if outs > 1:
        scratch.append(pltpu.VMEM((slots, heads * size), BF16))
    return pl.pallas_call(
        functools.partial(
            attend_kernel, size, heads, first, starts, len(after), base is not None, capacity
        ),
        in_specs=[pl.BlockSpec(memory_space=pltpu.SMEM)]
        + unread(after)
        + whole(1 + len(pieces) + len(extra)),
        out_specs=whole(outs),
        out_shape=[jax.ShapeDtypeStruct((height, heads * size), dtype) for height in heights],
        scratch_shapes=scratch,
        compiler_params=params(KERNEL_MIB),
        cost_estimate=cost(
            share * 4 * slots * keys * count * heads * size,
            2 * (2 * slots + count * keys * 2) * heads * size,
            slots * keys * count * heads,
        ),
        name="attend",
    )(place, *after, rows, *pieces, *extra)


def placement(slot, slots):
    lane = lax.broadcasted_iota(jnp.int32, (1, BLK), 1)
    return jnp.concatenate(
        [(lane + start == slot).astype(BF16) for start in range(0, slots, BLK)], axis=1
    )


def in_slots(parts, capacity):
    return jnp.concatenate(
        [part[:capacity, :] for part in parts[:2]] + [part[...] for part in parts[2:]], axis=0
    )


def collect_kernel(capacity, slots, slot_ref, *refs):
    rows = in_slots(refs[:-1], capacity)
    place = placement(slot_ref[...], slots)
    refs[-1][...] = jnp.dot(place, rows, preferred_element_type=F32).astype(BF16)


def collect(slot, parts, capacity, slots):
    rows, width = slot.shape[0], parts[0].shape[1]
    return pl.pallas_call(
        functools.partial(collect_kernel, capacity, slots),
        in_specs=whole(1 + len(parts)),
        out_specs=whole()[0],
        out_shape=jax.ShapeDtypeStruct((rows, width), BF16),
        compiler_params=params(KERNEL_MIB),
        cost_estimate=cost(COLLECT_COST * 1e9, 2 * (rows + slots) * width),
        name="collect",
    )(slot, *parts)


def finish_kernel(groups, capacity, slots, slot_ref, gain_ref, gate_ref, x_ref, w_ref, *refs):
    early, parts, (out_hbm, out_ref, sems) = refs[:groups], refs[groups:-3], refs[-3:]
    rows = x_ref.shape[0]
    place = placement(slot_ref[...], slots)
    late = jnp.dot(place, in_slots(parts, capacity), preferred_element_type=F32)
    tile = rows // 2
    stores = []
    for half in range(2):
        span = slice(half * tile, (half + 1) * tile)
        attn = jnp.concatenate([part[span, :].astype(F32) for part in early] + [late[span, :]], axis=1)
        centered = attn - jnp.mean(attn, axis=1, keepdims=True)
        variance = jnp.mean(centered * centered, axis=1, keepdims=True)
        normed = (centered * lax.rsqrt(variance + norm_eps) * gain_ref[...]).astype(BF16)
        mixed = (normed.astype(F32) * gate_ref[span, :].astype(F32)).astype(BF16)
        projected = jnp.dot(mixed, w_ref[...], preferred_element_type=F32)
        out_ref[span, :] = (x_ref[span, :].astype(F32) + projected).astype(BF16)
        store = pltpu.make_async_copy(out_ref.at[span, :], out_hbm.at[span, :], sems.at[half])
        store.start()
        stores.append(store)
    for store in stores:
        store.wait()


def finish(slot, early, gate, cand_x, ln_gain, w_out, parts, capacity, slots):
    rows, width = cand_x.shape
    return pl.pallas_call(
        functools.partial(finish_kernel, len(early), capacity, slots),
        in_specs=whole(5 + len(early) + len(parts)),
        out_specs=pl.BlockSpec(memory_space=pl.ANY),
        out_shape=jax.ShapeDtypeStruct((rows, width), BF16),
        scratch_shapes=[pltpu.VMEM((rows, width), BF16), pltpu.SemaphoreType.DMA((2,))],
        compiler_params=params(KERNEL_MIB),
        cost_estimate=cost(
            2 * rows * width * (width + slots), 2 * (3 * rows * width + width * width + slots * width)
        ),
        name="finish",
    )(slot, ln_gain.reshape(1, width), gate, cand_x, w_out, *early, *parts)


def swap(array, axis, bits, count):
    return lax.ppermute(array, axis, [(i, i ^ bits) for i in range(count)])


def exchange_cores(even, odds, capacity, count, behind):
    others = [swap(odd, "cand", 1, count) for odd in odds]
    if behind is not None:
        (even, others), _ = lax.optimization_barrier(((even, others), behind))
    pairs = []
    for d in range(1, count // 2):
        first, second = d * capacity, (d * capacity) % odds[0].shape[0]
        other = others[first // odds[0].shape[0]]
        pairs.append(
            jnp.concatenate(
                [even[first : first + capacity], other[second : second + capacity]], axis=0
            )
        )
    return [even, others[0]], pairs


def exchange_chips(pairs, count):
    return [swap(pair, "cand", 2 * d, count) for d, pair in enumerate(pairs, 1)]


def per_device(cand_x, cand_user, visible, hist_len, kv_cache, w_in, w_out, ln_gain):
    rows, width = cand_x.shape
    columns = lax.axis_size("cand")
    count = lax.axis_size("user")
    size = width // HEADS
    capacity = 2 * rows // columns
    slots = columns * capacity
    me = lax.axis_index("cand").astype(jnp.int32)
    owner_row = cand_user.reshape(1, rows)
    visible_row = visible.reshape(1, rows)
    spans = [(sum(GROUPS[:number]), heads) for number, heads in enumerate(GROUPS)]

    near = swap(kv_cache[0], "user", 1, count)
    far = []
    for own in split(kv_cache[0], spans, size):
        held = {0: own}
        bit = count // 2
        while bit > 1:
            for key in sorted(held):
                held[key | bit] = swap(held[key], "user", bit, count)
            bit //= 2
        far.append(held)
    evens = sorted(far[0])
    late = [key | 1 for key in evens[1:]]

    send = project_queries(owner_row, visible_row, cand_x, w_in, columns, capacity)
    got = lax.all_to_all(
        send.reshape(columns, capacity, -1), "cand", split_axis=0, concat_axis=0, tiled=True
    ).reshape(slots, -1)
    gate, gated = project_gate(cand_x, w_in)
    arrived = [near] + [held[key] for held in far for key in evens[1:]]
    slot, started = slot_column(owner_row ^ me, columns, capacity, [gated] + arrived)
    position = lax.axis_index("user").astype(jnp.int32)
    shards = position ^ jnp.array(evens + [1] + late, jnp.int32)
    head = jnp.concatenate([hist_len, me[None]])
    place_ready = jnp.concatenate([head, shards[: len(evens) + 1]])
    place_late = jnp.concatenate([head, shards[len(evens) + 1 :]])

    bases = []
    cuts = []
    for number, (first, heads) in enumerate(spans):
        held = far[number]
        segments = [([held[key]], 0, heads) for key in evens]
        segments.append(([near], first, HEADS + first))
        base = attend(
            place_ready, [started] + bases, got, segments, None, first, heads, size, None, F32, 0.0
        )[0]
        passed = [held[key] for key in evens[1:]]
        if number:
            passed, _ = lax.optimization_barrier((passed, bases[-1]))
        cuts.append([([swap(part, "user", 1, count)], 0, heads) for part in passed])
        bases.append(base)
    early = []
    after = []
    for number, (first, heads) in enumerate(spans):
        attn = attend(
            place_late,
            after,
            got,
            cuts[number],
            bases[number],
            first,
            heads,
            size,
            capacity,
            BF16,
            LATE_SHARE * (number > 0),
        )
        here, pairs = exchange_cores(
            attn[0], attn[1:], capacity, columns, early[-1] if early else None
        )
        after = [attn[0]] + pairs
        returned = here + exchange_chips(pairs, columns)
        if number + 1 < len(spans):
            early.append(collect(slot, returned, capacity, slots))
    return finish(slot, early, gate, cand_x, ln_gain, w_out, returned, capacity, slots)


def solution(mesh):
    in_specs = (
        P(("user", "cand"), None),
        P(("user", "cand"), None),
        P(("user", "cand")),
        P("cand"),
        P("cand", "user", None),
        P(),
        P(),
        P(),
    )
    out_specs = P(("user", "cand"), None)
    return jax.shard_map(
        per_device, mesh=mesh, in_specs=in_specs, out_specs=out_specs, check_vma=False
    )
```

```python
import functools
import math

import jax
import jax.numpy as jnp
from jax import lax
from jax.experimental import pallas as pl
from jax.experimental.pallas import tpu as pltpu
from jax.sharding import PartitionSpec as P

HEADS = 8
BLK = 128
GROUPS = (4, 4)
norm_eps = 1e-06
F32 = jnp.float32
BF16 = jnp.bfloat16
MIB = 1024 * 1024
TOKEN = jax.ShapeDtypeStruct((8, BLK), jnp.int32)
WAIT_COST = 20.0
LATE_SHARE = 20.0
COLLECT_COST = 20.0
SLOTS_COST = 6.0
KERNEL_MIB = 24


def params(mib):
    return pltpu.CompilerParams(vmem_limit_bytes=mib * MIB)


def cost(flops, nbytes, transcendentals=0):
    return pl.CostEstimate(
        flops=int(flops), bytes_accessed=int(nbytes), transcendentals=int(transcendentals)
    )


def silu(v):
    half = 0.5 * v
    return half * jnp.tanh(half) + half


def earlier_mask(rows):
    first = lax.broadcasted_iota(jnp.int32, (rows, rows), 0)
    second = lax.broadcasted_iota(jnp.int32, (rows, rows), 1)
    return (first < second).astype(BF16)


def slot_row(owner_row, columns, capacity):
    rows = owner_row.shape[1]
    users = lax.broadcasted_iota(jnp.int32, (columns, rows), 0)
    mine = users == owner_row
    before = jnp.dot(mine.astype(BF16), earlier_mask(rows), preferred_element_type=F32)
    rank = jnp.sum(jnp.where(mine, before, 0.0), axis=0, keepdims=True)
    return owner_row.astype(F32) * capacity + rank


def whole(count=1):
    return [pl.BlockSpec(memory_space=pltpu.VMEM)] * count


def unread(arrays):
    return [pl.BlockSpec(memory_space=pl.ANY)] * len(arrays)


def split_kernel(spans, size, kv_ref, *out_refs):
    width = kv_ref.shape[1] // 2
    for (first, heads), ref in zip(spans, out_refs):
        lo, hi = first * size, (first + heads) * size
        ref[:, : hi - lo] = kv_ref[:, lo:hi]
        ref[:, hi - lo :] = kv_ref[:, width + lo : width + hi]


def split(kv, spans, size):
    rows = kv.shape[0]
    return pl.pallas_call(
        functools.partial(split_kernel, spans, size),
        in_specs=whole(),
        out_specs=whole(len(spans)),
        out_shape=[jax.ShapeDtypeStruct((rows, 2 * heads * size), BF16) for _, heads in spans],
        compiler_params=params(KERNEL_MIB),
        cost_estimate=cost(0, 4 * kv.size),
        name="split",
    )(kv)


def query_kernel(slot_ref, visible_ref, x_ref, w_ref, send_ref):
    rows, width = x_ref.shape
    slots = send_ref.shape[0]
    index = lax.broadcasted_iota(jnp.int32, (slots, rows), 0)
    place = (index == slot_ref[:1, :]).astype(BF16)
    seen = jnp.broadcast_to(visible_ref[...].astype(F32), (BLK, rows)).T.astype(BF16)
    send_ref[:, width:] = jnp.dot(place, seen, preferred_element_type=F32).astype(BF16)
    tile = min(256, width)
    for start in range(0, width, tile):
        span = slice(start, start + tile)
        hidden = jnp.dot(x_ref[...], w_ref[:, span], preferred_element_type=F32)
        moved = jnp.dot(place, silu(hidden).astype(BF16), preferred_element_type=F32)
        send_ref[:, span] = moved.astype(BF16)


def project_queries(slot, visible_row, cand_x, w_in, slots):
    rows, width = cand_x.shape
    return pl.pallas_call(
        query_kernel,
        in_specs=whole(4),
        out_specs=whole()[0],
        out_shape=jax.ShapeDtypeStruct((slots, width + BLK), BF16),
        compiler_params=params(KERNEL_MIB),
        cost_estimate=cost(
            2 * rows * width * width + 2 * slots * rows * width,
            2 * (rows * width + width * width + slots * width),
            rows * width,
        ),
        name="project_queries",
    )(slot, visible_row, cand_x, w_in)


def gate_kernel(x_ref, w_ref, gate_ref, token_ref):
    token_ref[...] = jnp.zeros_like(token_ref)
    width = x_ref.shape[1]
    tile = min(256, width)
    for start in range(0, width, tile):
        columns = w_ref[:, width + start : width + start + tile]
        hidden = jnp.dot(x_ref[...], columns, preferred_element_type=F32)
        gate_ref[:, start : start + tile] = silu(hidden).astype(BF16)


def project_gate(cand_x, w_in):
    rows, width = cand_x.shape
    return pl.pallas_call(
        gate_kernel,
        in_specs=whole(2),
        out_specs=whole(2),
        out_shape=[jax.ShapeDtypeStruct((rows, width), BF16), TOKEN],
        compiler_params=params(KERNEL_MIB),
        cost_estimate=cost(
            2 * rows * width * width, 2 * (2 * rows * width + width * width), rows * width
        ),
        name="project_gate",
    )(cand_x, w_in)


def slots_kernel(columns, capacity, owner_ref, row_ref):
    row = slot_row(owner_ref[...], columns, capacity)
    row_ref[...] = jnp.broadcast_to(row, row_ref.shape).astype(jnp.int32)


def find_slots(owner_row, columns, capacity):
    return pl.pallas_call(
        functools.partial(slots_kernel, columns, capacity),
        in_specs=whole(),
        out_specs=whole()[0],
        out_shape=jax.ShapeDtypeStruct((8, owner_row.shape[1]), jnp.int32),
        compiler_params=params(KERNEL_MIB),
        cost_estimate=cost(SLOTS_COST * 1e9, 0),
        name="find_slots",
    )(owner_row)


def column_kernel(columns, capacity, owner_ref, *refs):
    column_ref, token_ref = refs[-2:]
    token_ref[...] = jnp.zeros_like(token_ref)
    row = slot_row(owner_ref[...], columns, capacity)
    column_ref[...] = jnp.broadcast_to(row, (BLK, row.shape[1])).T.astype(jnp.int32)


def slot_column(owner_row, columns, capacity, after):
    rows = owner_row.shape[1]
    return pl.pallas_call(
        functools.partial(column_kernel, columns, capacity),
        in_specs=whole() + unread(after),
        out_specs=whole(2),
        out_shape=[jax.ShapeDtypeStruct((rows, BLK), jnp.int32), TOKEN],
        compiler_params=params(KERNEL_MIB),
        cost_estimate=cost(WAIT_COST * 1e9, 4 * rows * BLK),
        name="slot_column",
    )(owner_row, *after)


def attend_kernel(size, heads, first, starts, behind, has_base, capacity, place_ref, *refs):
    refs = refs[behind:]
    rows_ref, refs = refs[0], refs[1:]
    count = len(starts)
    parts = []
    for _, _, pieces in starts:
        parts.append(refs[:pieces])
        refs = refs[pieces:]
    base_ref = refs[0] if has_base else None
    outs = 3 if capacity else 1
    out_refs, shown = refs[int(has_base) : int(has_base) + outs], refs[int(has_base) + outs]
    result = out_refs[0] if outs == 1 else refs[-1]
    slots = rows_ref.shape[0]
    columns_of = slots // capacity if capacity else 1
    keys = sum(piece.shape[0] for piece in parts[0])
    blocks = keys // BLK
    seen = rows_ref[:, HEADS * size :].astype(F32)
    for number in range(count):
        for block in range(blocks):
            start = (place_ref[2 + number] * blocks + block).astype(F32)
            shown[number * blocks + block] = (start < seen).astype(F32).astype(BF16)
    row = lax.broadcasted_iota(jnp.int32, (keys, size), 0)
    tile = min(512, slots)

    def columns(start):
        return slice(start, start + size)

    def read(part, start):
        return jnp.concatenate([piece[:, columns(start)] for piece in part], axis=0)

    def one_head(head):
        values = []
        for number, part in enumerate(parts):
            inside = row + place_ref[2 + number] * keys < place_ref[0]
            value = read(part, (starts[number][1] + head) * size).astype(F32)
            values.append(jnp.where(inside, value, 0.0).astype(BF16))
        values = jnp.concatenate(values, axis=0)
        for start in range(0, slots, tile):
            span = slice(start, start + tile)
            queries = rows_ref[span, columns((first + head) * size)]
            weights = []
            for number, part in enumerate(parts):
                scores = lax.dot_general(
                    queries,
                    read(part, (starts[number][0] + head) * size),
                    (((1,), (1,)), ((), ())),
                    preferred_element_type=F32,
                )
                for block in range(blocks):
                    half = scores[:, block * BLK : (block + 1) * BLK] * (0.5 / math.sqrt(size))
                    half = half.astype(BF16) * shown[number * blocks + block, span, :]
                    weights.append(half * jnp.tanh(half) + half)
            total = jnp.dot(
                jnp.concatenate(weights, axis=1), values, preferred_element_type=F32
            )
            if has_base:
                total = total + base_ref[span, columns(head * size)]
            result[span, columns(head * size)] = total.astype(result.dtype)

    for head in range(heads):
        one_head(head)
    if outs > 1:
        numbers = list(range(0, columns_of, 2)) + list(range(1, columns_of, 2))
        for ref in out_refs:
            for start in range(0, ref.shape[0], capacity):
                block = place_ref[1] ^ numbers.pop(0)
                source = pl.ds(pl.multiple_of(block * capacity, capacity), capacity)
                ref[start : start + capacity, :] = result[source, :]


def attend(place, after, rows, segments, base, first, heads, size, capacity, dtype, share):
    slots = rows.shape[0]
    keys = sum(piece.shape[0] for piece in segments[0][0])
    count = len(segments)
    starts = [(key, value, len(pieces)) for pieces, key, value in segments]
    pieces = [piece for pieces, _, _ in segments for piece in pieces]
    heights = [slots // 2, slots // 4, slots // 4] if capacity else [slots]
    outs = len(heights)
    extra = [] if base is None else [base]
    scratch = [pltpu.VMEM((count * (keys // BLK), slots, BLK), BF16)]
    if outs > 1:
        scratch.append(pltpu.VMEM((slots, heads * size), BF16))
    return pl.pallas_call(
        functools.partial(
            attend_kernel, size, heads, first, starts, len(after), base is not None, capacity
        ),
        in_specs=[pl.BlockSpec(memory_space=pltpu.SMEM)]
        + unread(after)
        + whole(1 + len(pieces) + len(extra)),
        out_specs=whole(outs),
        out_shape=[jax.ShapeDtypeStruct((height, heads * size), dtype) for height in heights],
        scratch_shapes=scratch,
        compiler_params=params(KERNEL_MIB),
        cost_estimate=cost(
            share * 4 * slots * keys * count * heads * size,
            2 * (2 * slots + count * keys * 2) * heads * size,
            slots * keys * count * heads,
        ),
        name="attend",
    )(place, *after, rows, *pieces, *extra)


def placement(slot, slots):
    lane = lax.broadcasted_iota(jnp.int32, (1, BLK), 1)
    return jnp.concatenate(
        [(lane + start == slot).astype(BF16) for start in range(0, slots, BLK)], axis=1
    )


def in_slots(parts, capacity):
    return jnp.concatenate(
        [part[:capacity, :] for part in parts[:2]] + [part[...] for part in parts[2:]], axis=0
    )


def collect_kernel(capacity, slots, slot_ref, *refs):
    rows = in_slots(refs[:-1], capacity)
    place = placement(slot_ref[...], slots)
    refs[-1][...] = jnp.dot(place, rows, preferred_element_type=F32).astype(BF16)


def collect(slot, parts, capacity, slots):
    rows, width = slot.shape[0], parts[0].shape[1]
    return pl.pallas_call(
        functools.partial(collect_kernel, capacity, slots),
        in_specs=whole(1 + len(parts)),
        out_specs=whole()[0],
        out_shape=jax.ShapeDtypeStruct((rows, width), BF16),
        compiler_params=params(KERNEL_MIB),
        cost_estimate=cost(COLLECT_COST * 1e9, 2 * (rows + slots) * width),
        name="collect",
    )(slot, *parts)


def finish_kernel(groups, capacity, slots, slot_ref, gain_ref, gate_ref, x_ref, w_ref, *refs):
    early, parts, (out_hbm, out_ref, sems) = refs[:groups], refs[groups:-3], refs[-3:]
    rows = x_ref.shape[0]
    place = placement(slot_ref[...], slots)
    late = jnp.dot(place, in_slots(parts, capacity), preferred_element_type=F32)
    tile = rows // 2
    stores = []
    for half in range(2):
        span = slice(half * tile, (half + 1) * tile)
        attn = jnp.concatenate([part[span, :].astype(F32) for part in early] + [late[span, :]], axis=1)
        centered = attn - jnp.mean(attn, axis=1, keepdims=True)
        variance = jnp.mean(centered * centered, axis=1, keepdims=True)
        normed = (centered * lax.rsqrt(variance + norm_eps) * gain_ref[...]).astype(BF16)
        mixed = (normed.astype(F32) * gate_ref[span, :].astype(F32)).astype(BF16)
        projected = jnp.dot(mixed, w_ref[...], preferred_element_type=F32)
        out_ref[span, :] = (x_ref[span, :].astype(F32) + projected).astype(BF16)
        store = pltpu.make_async_copy(out_ref.at[span, :], out_hbm.at[span, :], sems.at[half])
        store.start()
        stores.append(store)
    for store in stores:
        store.wait()


def finish(slot, early, gate, cand_x, ln_gain, w_out, parts, capacity, slots):
    rows, width = cand_x.shape
    return pl.pallas_call(
        functools.partial(finish_kernel, len(early), capacity, slots),
        in_specs=whole(5 + len(early) + len(parts)),
        out_specs=pl.BlockSpec(memory_space=pl.ANY),
        out_shape=jax.ShapeDtypeStruct((rows, width), BF16),
        scratch_shapes=[pltpu.VMEM((rows, width), BF16), pltpu.SemaphoreType.DMA((2,))],
        compiler_params=params(KERNEL_MIB),
        cost_estimate=cost(
            2 * rows * width * (width + slots), 2 * (3 * rows * width + width * width + slots * width)
        ),
        name="finish",
    )(slot, ln_gain.reshape(1, width), gate, cand_x, w_out, *early, *parts)


def swap(array, axis, bits, count):
    return lax.ppermute(array, axis, [(i, i ^ bits) for i in range(count)])


def exchange_cores(even, odds, capacity, count, behind):
    others = [swap(odd, "cand", 1, count) for odd in odds]
    if behind is not None:
        (even, others), _ = lax.optimization_barrier(((even, others), behind))
    pairs = []
    for d in range(1, count // 2):
        first, second = d * capacity, (d * capacity) % odds[0].shape[0]
        other = others[first // odds[0].shape[0]]
        pairs.append(
            jnp.concatenate(
                [even[first : first + capacity], other[second : second + capacity]], axis=0
            )
        )
    return [even, others[0]], pairs


def exchange_chips(pairs, count):
    return [swap(pair, "cand", 2 * d, count) for d, pair in enumerate(pairs, 1)]


def per_device(cand_x, cand_user, visible, hist_len, kv_cache, w_in, w_out, ln_gain):
    rows, width = cand_x.shape
    columns = lax.axis_size("cand")
    count = lax.axis_size("user")
    size = width // HEADS
    capacity = 2 * rows // columns
    slots = columns * capacity
    me = lax.axis_index("cand").astype(jnp.int32)
    owner_row = cand_user.reshape(1, rows)
    visible_row = visible.reshape(1, rows)
    spans = [(sum(GROUPS[:number]), heads) for number, heads in enumerate(GROUPS)]

    row = find_slots(owner_row, columns, capacity)
    own, _ = lax.optimization_barrier((kv_cache[0], row))
    held = {0: own}
    bit = count // 2
    while bit > 1:
        for key in sorted(held):
            held[key | bit] = swap(held[key], "user", bit, count)
        bit //= 2
    held[1] = swap(own, "user", 1, count)
    ready = sorted(held)
    late = [key | 1 for key in ready if key > 1]

    send = project_queries(row, visible_row, cand_x, w_in, slots)
    got = lax.all_to_all(
        send.reshape(columns, capacity, -1), "cand", split_axis=0, concat_axis=0, tiled=True
    ).reshape(slots, -1)
    gate, gated = project_gate(cand_x, w_in)
    arrived = [gated] + [held[key] for key in ready if key]
    slot, started = slot_column(owner_row ^ me, columns, capacity, arrived)
    position = lax.axis_index("user").astype(jnp.int32)
    shards = position ^ jnp.array(ready + late, jnp.int32)
    head = jnp.concatenate([hist_len, me[None]])
    place_ready = jnp.concatenate([head, shards[: len(ready)]])
    place_late = jnp.concatenate([head, shards[len(ready) :]])

    passed = [split(held[key ^ 1], spans, size) for key in late]
    bases = []
    for number, (first, heads) in enumerate(spans):
        segments = [([held[key]], first, HEADS + first) for key in ready]
        bases += attend(
            place_ready, [started] + bases, got, segments, None, first, heads, size, None, F32, 0.0
        )
    cuts = []
    for number, (first, heads) in enumerate(spans):
        parts = [pieces[number] for pieces in passed]
        if number:
            parts, _ = lax.optimization_barrier((parts, bases))
        cuts.append([([swap(part, "user", 1, count)], 0, heads) for part in parts])
    early = []
    after = bases
    behind = None
    for number, (first, heads) in enumerate(spans):
        attn = attend(
            place_late,
            after,
            got,
            cuts[number],
            bases[number],
            first,
            heads,
            size,
            capacity,
            BF16,
            LATE_SHARE * (number > 0),
        )
        here, pairs = exchange_cores(attn[0], attn[1:], capacity, columns, behind)
        after = [attn[0]] + pairs
        away = exchange_chips(pairs, columns)
        behind = away
        if number + 1 < len(spans):
            early.append(collect(slot, here + away, capacity, slots))
            behind = early[-1]
    return finish(slot, early, gate, cand_x, ln_gain, w_out, here + away, capacity, slots)


def solution(mesh):
    in_specs = (
        P(("user", "cand"), None),
        P(("user", "cand"), None),
        P(("user", "cand")),
        P("cand"),
        P("cand", "user", None),
        P(),
        P(),
        P(),
    )
    out_specs = P(("user", "cand"), None)
    return jax.shard_map(
        per_device, mesh=mesh, in_specs=in_specs, out_specs=out_specs, check_vma=False
    )
```

```python
import functools
import math

import jax
import jax.numpy as jnp
from jax import lax
from jax.experimental import pallas as pl
from jax.experimental.pallas import tpu as pltpu
from jax.sharding import PartitionSpec as P

HEADS = 8
BLK = 128
GROUPS = (4, 4)
norm_eps = 1e-06
F32 = jnp.float32
BF16 = jnp.bfloat16
MIB = 1024 * 1024
TOKEN = jax.ShapeDtypeStruct((8, BLK), jnp.int32)
WAIT_COST = 20.0
LATE_SHARE = 20.0
COLLECT_COST = 20.0
SLOTS_COST = 6.0
KERNEL_MIB = 24


def params(mib):
    return pltpu.CompilerParams(vmem_limit_bytes=mib * MIB)


def cost(flops, nbytes, transcendentals=0):
    return pl.CostEstimate(
        flops=int(flops), bytes_accessed=int(nbytes), transcendentals=int(transcendentals)
    )


def silu(v):
    half = 0.5 * v
    return half * jnp.tanh(half) + half


def earlier_mask(rows):
    first = lax.broadcasted_iota(jnp.int32, (rows, rows), 0)
    second = lax.broadcasted_iota(jnp.int32, (rows, rows), 1)
    return (first < second).astype(BF16)


def slot_row(owner_row, columns, capacity):
    rows = owner_row.shape[1]
    users = lax.broadcasted_iota(jnp.int32, (columns, rows), 0)
    mine = users == owner_row
    before = jnp.dot(mine.astype(BF16), earlier_mask(rows), preferred_element_type=F32)
    rank = jnp.sum(jnp.where(mine, before, 0.0), axis=0, keepdims=True)
    return owner_row.astype(F32) * capacity + rank


def whole(count=1):
    return [pl.BlockSpec(memory_space=pltpu.VMEM)] * count


def unread(arrays):
    return [pl.BlockSpec(memory_space=pl.ANY)] * len(arrays)


def query_kernel(slot_ref, visible_ref, x_ref, w_ref, send_ref):
    rows, width = x_ref.shape
    slots = send_ref.shape[0]
    index = lax.broadcasted_iota(jnp.int32, (slots, rows), 0)
    place = (index == slot_ref[:1, :]).astype(BF16)
    seen = jnp.broadcast_to(visible_ref[...].astype(F32), (BLK, rows)).T.astype(BF16)
    send_ref[:, width:] = jnp.dot(place, seen, preferred_element_type=F32).astype(BF16)
    tile = min(256, width)
    for start in range(0, width, tile):
        span = slice(start, start + tile)
        hidden = jnp.dot(x_ref[...], w_ref[:, span], preferred_element_type=F32)
        moved = jnp.dot(place, silu(hidden).astype(BF16), preferred_element_type=F32)
        send_ref[:, span] = moved.astype(BF16)


def project_queries(slot, visible_row, cand_x, w_in, slots):
    rows, width = cand_x.shape
    return pl.pallas_call(
        query_kernel,
        in_specs=whole(4),
        out_specs=whole()[0],
        out_shape=jax.ShapeDtypeStruct((slots, width + BLK), BF16),
        compiler_params=params(KERNEL_MIB),
        cost_estimate=cost(
            2 * rows * width * width + 2 * slots * rows * width,
            2 * (rows * width + width * width + slots * width),
            rows * width,
        ),
        name="project_queries",
    )(slot, visible_row, cand_x, w_in)


def gate_kernel(x_ref, w_ref, gate_ref, token_ref):
    token_ref[...] = jnp.zeros_like(token_ref)
    width = x_ref.shape[1]
    tile = min(256, width)
    for start in range(0, width, tile):
        columns = w_ref[:, width + start : width + start + tile]
        hidden = jnp.dot(x_ref[...], columns, preferred_element_type=F32)
        gate_ref[:, start : start + tile] = silu(hidden).astype(BF16)


def project_gate(cand_x, w_in):
    rows, width = cand_x.shape
    return pl.pallas_call(
        gate_kernel,
        in_specs=whole(2),
        out_specs=whole(2),
        out_shape=[jax.ShapeDtypeStruct((rows, width), BF16), TOKEN],
        compiler_params=params(KERNEL_MIB),
        cost_estimate=cost(
            2 * rows * width * width, 2 * (2 * rows * width + width * width), rows * width
        ),
        name="project_gate",
    )(cand_x, w_in)


def prepare_kernel(columns, capacity, spans, size, owner_ref, kv_hbm, row_ref, *refs):
    part_refs, sems = refs[:-1], refs[-1]
    width = kv_hbm.shape[1] // 2
    copies = []
    for (first, heads), ref in zip(spans, part_refs):
        wide = heads * size
        for start in (0, width):
            source = kv_hbm.at[:, start + first * size : start + first * size + wide]
            target = ref.at[:, wide * (start > 0) : wide * (start > 0) + wide]
            copies.append(pltpu.make_async_copy(source, target, sems.at[len(copies)]))
    for copy in copies:
        copy.start()
    row = slot_row(owner_ref[...], columns, capacity)
    row_ref[...] = jnp.broadcast_to(row, row_ref.shape).astype(jnp.int32)
    for copy in copies:
        copy.wait()


def prepare(owner_row, kv, spans, size, columns, capacity):
    rows = kv.shape[0]
    return pl.pallas_call(
        functools.partial(prepare_kernel, columns, capacity, spans, size),
        in_specs=whole() + [pl.BlockSpec(memory_space=pl.ANY)],
        out_specs=whole(1 + len(spans)),
        out_shape=[jax.ShapeDtypeStruct((8, owner_row.shape[1]), jnp.int32)]
        + [jax.ShapeDtypeStruct((rows, 2 * heads * size), BF16) for _, heads in spans],
        scratch_shapes=[pltpu.SemaphoreType.DMA((2 * len(spans),))],
        compiler_params=params(KERNEL_MIB),
        cost_estimate=cost(SLOTS_COST * 1e9, 0),
        name="prepare",
    )(owner_row, kv)


def wait_kernel(*refs):
    refs[-1][...] = jnp.zeros_like(refs[-1])


def wait_for(arrays):
    return pl.pallas_call(
        wait_kernel,
        in_specs=unread(arrays),
        out_specs=whole()[0],
        out_shape=TOKEN,
        compiler_params=params(KERNEL_MIB),
        cost_estimate=cost(WAIT_COST * 1e9, 0),
        name="wait_for",
    )(*arrays)


def column_kernel(columns, capacity, owner_ref, *refs):
    column_ref, token_ref = refs[-2:]
    token_ref[...] = jnp.zeros_like(token_ref)
    row = slot_row(owner_ref[...], columns, capacity)
    column_ref[...] = jnp.broadcast_to(row, (BLK, row.shape[1])).T.astype(jnp.int32)


def slot_column(owner_row, columns, capacity, after):
    rows = owner_row.shape[1]
    return pl.pallas_call(
        functools.partial(column_kernel, columns, capacity),
        in_specs=whole() + unread(after),
        out_specs=whole(2),
        out_shape=[jax.ShapeDtypeStruct((rows, BLK), jnp.int32), TOKEN],
        compiler_params=params(KERNEL_MIB),
        cost_estimate=cost(WAIT_COST * 1e9, 4 * rows * BLK),
        name="slot_column",
    )(owner_row, *after)


def attend_kernel(size, heads, first, starts, behind, has_base, capacity, place_ref, *refs):
    refs = refs[behind:]
    rows_ref, refs = refs[0], refs[1:]
    count = len(starts)
    parts = []
    for _, _, pieces in starts:
        parts.append(refs[:pieces])
        refs = refs[pieces:]
    base_ref = refs[0] if has_base else None
    outs = 3 if capacity else 1
    out_refs, shown = refs[int(has_base) : int(has_base) + outs], refs[int(has_base) + outs]
    result = out_refs[0] if outs == 1 else refs[-1]
    slots = rows_ref.shape[0]
    columns_of = slots // capacity if capacity else 1
    keys = sum(piece.shape[0] for piece in parts[0])
    blocks = keys // BLK
    seen = rows_ref[:, HEADS * size :].astype(F32)
    for number in range(count):
        for block in range(blocks):
            start = (place_ref[2 + number] * blocks + block).astype(F32)
            shown[number * blocks + block] = (start < seen).astype(F32).astype(BF16)
    row = lax.broadcasted_iota(jnp.int32, (keys, size), 0)
    tile = min(512, slots)

    def columns(start):
        return slice(start, start + size)

    def read(part, start):
        return jnp.concatenate([piece[:, columns(start)] for piece in part], axis=0)

    def one_head(head):
        values = []
        for number, part in enumerate(parts):
            inside = row + place_ref[2 + number] * keys < place_ref[0]
            value = read(part, (starts[number][1] + head) * size).astype(F32)
            values.append(jnp.where(inside, value, 0.0).astype(BF16))
        values = jnp.concatenate(values, axis=0)
        for start in range(0, slots, tile):
            span = slice(start, start + tile)
            queries = rows_ref[span, columns((first + head) * size)]
            weights = []
            for number, part in enumerate(parts):
                scores = lax.dot_general(
                    queries,
                    read(part, (starts[number][0] + head) * size),
                    (((1,), (1,)), ((), ())),
                    preferred_element_type=F32,
                )
                for block in range(blocks):
                    half = scores[:, block * BLK : (block + 1) * BLK] * (0.5 / math.sqrt(size))
                    half = half.astype(BF16) * shown[number * blocks + block, span, :]
                    weights.append(half * jnp.tanh(half) + half)
            total = jnp.dot(
                jnp.concatenate(weights, axis=1), values, preferred_element_type=F32
            )
            if has_base:
                total = total + base_ref[span, columns(head * size)]
            result[span, columns(head * size)] = total.astype(result.dtype)

    for head in range(heads):
        one_head(head)
    if outs > 1:
        numbers = list(range(0, columns_of, 2)) + list(range(1, columns_of, 2))
        for ref in out_refs:
            for start in range(0, ref.shape[0], capacity):
                block = place_ref[1] ^ numbers.pop(0)
                source = pl.ds(pl.multiple_of(block * capacity, capacity), capacity)
                ref[start : start + capacity, :] = result[source, :]


def attend(place, after, rows, segments, base, first, heads, size, capacity, dtype, share):
    slots = rows.shape[0]
    keys = sum(piece.shape[0] for piece in segments[0][0])
    count = len(segments)
    starts = [(key, value, len(pieces)) for pieces, key, value in segments]
    pieces = [piece for pieces, _, _ in segments for piece in pieces]
    heights = [slots // 2, slots // 4, slots // 4] if capacity else [slots]
    outs = len(heights)
    extra = [] if base is None else [base]
    scratch = [pltpu.VMEM((count * (keys // BLK), slots, BLK), BF16)]
    if outs > 1:
        scratch.append(pltpu.VMEM((slots, heads * size), BF16))
    return pl.pallas_call(
        functools.partial(
            attend_kernel, size, heads, first, starts, len(after), base is not None, capacity
        ),
        in_specs=[pl.BlockSpec(memory_space=pltpu.SMEM)]
        + unread(after)
        + whole(1 + len(pieces) + len(extra)),
        out_specs=whole(outs),
        out_shape=[jax.ShapeDtypeStruct((height, heads * size), dtype) for height in heights],
        scratch_shapes=scratch,
        compiler_params=params(KERNEL_MIB),
        cost_estimate=cost(
            share * 4 * slots * keys * count * heads * size,
            2 * (2 * slots + count * keys * 2) * heads * size,
            slots * keys * count * heads,
        ),
        name="attend",
    )(place, *after, rows, *pieces, *extra)


def placement(slot, slots):
    lane = lax.broadcasted_iota(jnp.int32, (1, BLK), 1)
    return jnp.concatenate(
        [(lane + start == slot).astype(BF16) for start in range(0, slots, BLK)], axis=1
    )


def in_slots(parts, capacity):
    return jnp.concatenate(
        [part[:capacity, :] for part in parts[:2]] + [part[...] for part in parts[2:]], axis=0
    )


def collect_kernel(capacity, slots, slot_ref, *refs):
    rows = in_slots(refs[:-1], capacity)
    place = placement(slot_ref[...], slots)
    refs[-1][...] = jnp.dot(place, rows, preferred_element_type=F32).astype(BF16)


def collect(slot, parts, capacity, slots):
    rows, width = slot.shape[0], parts[0].shape[1]
    return pl.pallas_call(
        functools.partial(collect_kernel, capacity, slots),
        in_specs=whole(1 + len(parts)),
        out_specs=whole()[0],
        out_shape=jax.ShapeDtypeStruct((rows, width), BF16),
        compiler_params=params(KERNEL_MIB),
        cost_estimate=cost(COLLECT_COST * 1e9, 2 * (rows + slots) * width),
        name="collect",
    )(slot, *parts)


def finish_kernel(groups, capacity, slots, slot_ref, gain_ref, gate_ref, x_ref, w_ref, *refs):
    early, parts, (out_hbm, out_ref, sems) = refs[:groups], refs[groups:-3], refs[-3:]
    rows = x_ref.shape[0]
    place = placement(slot_ref[...], slots)
    late = jnp.dot(place, in_slots(parts, capacity), preferred_element_type=F32)
    tile = rows // 2
    stores = []
    for half in range(2):
        span = slice(half * tile, (half + 1) * tile)
        attn = jnp.concatenate([part[span, :].astype(F32) for part in early] + [late[span, :]], axis=1)
        centered = attn - jnp.mean(attn, axis=1, keepdims=True)
        variance = jnp.mean(centered * centered, axis=1, keepdims=True)
        normed = (centered * lax.rsqrt(variance + norm_eps) * gain_ref[...]).astype(BF16)
        mixed = (normed.astype(F32) * gate_ref[span, :].astype(F32)).astype(BF16)
        projected = jnp.dot(mixed, w_ref[...], preferred_element_type=F32)
        out_ref[span, :] = (x_ref[span, :].astype(F32) + projected).astype(BF16)
        store = pltpu.make_async_copy(out_ref.at[span, :], out_hbm.at[span, :], sems.at[half])
        store.start()
        stores.append(store)
    for store in stores:
        store.wait()


def finish(slot, early, gate, cand_x, ln_gain, w_out, parts, capacity, slots):
    rows, width = cand_x.shape
    return pl.pallas_call(
        functools.partial(finish_kernel, len(early), capacity, slots),
        in_specs=whole(5 + len(early) + len(parts)),
        out_specs=pl.BlockSpec(memory_space=pl.ANY),
        out_shape=jax.ShapeDtypeStruct((rows, width), BF16),
        scratch_shapes=[pltpu.VMEM((rows, width), BF16), pltpu.SemaphoreType.DMA((2,))],
        compiler_params=params(KERNEL_MIB),
        cost_estimate=cost(
            2 * rows * width * (width + slots), 2 * (3 * rows * width + width * width + slots * width)
        ),
        name="finish",
    )(slot, ln_gain.reshape(1, width), gate, cand_x, w_out, *early, *parts)


def swap(array, axis, bits, count):
    return lax.ppermute(array, axis, [(i, i ^ bits) for i in range(count)])


def exchange_cores(even, odds, capacity, count, behind):
    others = [swap(odd, "cand", 1, count) for odd in odds]
    if behind is not None:
        (even, others), _ = lax.optimization_barrier(((even, others), behind))
    pairs = []
    for d in range(1, count // 2):
        first, second = d * capacity, (d * capacity) % odds[0].shape[0]
        other = others[first // odds[0].shape[0]]
        pairs.append(
            jnp.concatenate(
                [even[first : first + capacity], other[second : second + capacity]], axis=0
            )
        )
    return [even, others[0]], pairs


def exchange_chips(pairs, count):
    return [swap(pair, "cand", 2 * d, count) for d, pair in enumerate(pairs, 1)]


def per_device(cand_x, cand_user, visible, hist_len, kv_cache, w_in, w_out, ln_gain):
    rows, width = cand_x.shape
    columns = lax.axis_size("cand")
    count = lax.axis_size("user")
    size = width // HEADS
    capacity = 2 * rows // columns
    slots = columns * capacity
    me = lax.axis_index("cand").astype(jnp.int32)
    owner_row = cand_user.reshape(1, rows)
    visible_row = visible.reshape(1, rows)
    spans = [(sum(GROUPS[:number]), heads) for number, heads in enumerate(GROUPS)]

    row, *parts = prepare(owner_row, kv_cache[0], spans, size, columns, capacity)
    near = None
    far = []
    for part in parts:
        if far:
            part, _ = lax.optimization_barrier((part, far[-1]))
        held = {0: part}
        bit = count // 2
        while bit > 1:
            for key in sorted(held):
                held[key | bit] = swap(held[key], "user", bit, count)
            bit //= 2
        if near is None:
            own, _ = lax.optimization_barrier((kv_cache[0], row))
            near = swap(own, "user", 1, count)
        far.append(held)
    evens = sorted(far[0])
    late = [key | 1 for key in evens[1:]]

    send = project_queries(row, visible_row, cand_x, w_in, slots)
    got = lax.all_to_all(
        send.reshape(columns, capacity, -1), "cand", split_axis=0, concat_axis=0, tiled=True
    ).reshape(slots, -1)
    gate, gated = project_gate(cand_x, w_in)
    arrived = [gated, near] + [far[0][key] for key in evens[1:]]
    slot, started = slot_column(owner_row ^ me, columns, capacity, arrived)
    position = lax.axis_index("user").astype(jnp.int32)
    shards = position ^ jnp.array(evens + [1] + late, jnp.int32)
    head = jnp.concatenate([hist_len, me[None]])
    place_ready = jnp.concatenate([head, shards[: len(evens) + 1]])
    place_late = jnp.concatenate([head, shards[len(evens) + 1 :]])

    early = []
    after = [started]
    behind = None
    for number, (first, heads) in enumerate(spans):
        held = far[number]
        cuts = [([swap(held[key], "user", 1, count)], 0, heads) for key in evens[1:]]
        segments = [([held[key]], 0, heads) for key in evens]
        segments.append(([near], first, HEADS + first))
        base = attend(
            place_ready, after, got, segments, None, first, heads, size, None, F32, 0.0
        )[0]
        attn = attend(
            place_late,
            [],
            got,
            cuts,
            base,
            first,
            heads,
            size,
            capacity,
            BF16,
            LATE_SHARE * (number > 0),
        )
        here, pairs = exchange_cores(attn[0], attn[1:], capacity, columns, behind)
        away = exchange_chips(pairs, columns)
        if number + 1 < len(spans):
            token = wait_for([attn[0]] + [far[number + 1][key] for key in evens[1:]])
            after = [token] + pairs
            early.append(collect(slot, here + away, capacity, slots))
            behind = early[-1]
    return finish(slot, early, gate, cand_x, ln_gain, w_out, here + away, capacity, slots)


def solution(mesh):
    in_specs = (
        P(("user", "cand"), None),
        P(("user", "cand"), None),
        P(("user", "cand")),
        P("cand"),
        P("cand", "user", None),
        P(),
        P(),
        P(),
    )
    out_specs = P(("user", "cand"), None)
    return jax.shard_map(
        per_device, mesh=mesh, in_specs=in_specs, out_specs=out_specs, check_vma=False
    )
```

```python
import functools
import math

import jax
import jax.numpy as jnp
from jax import lax
from jax.experimental import pallas as pl
from jax.experimental.pallas import tpu as pltpu
from jax.sharding import PartitionSpec as P

HEADS = 8
BLK = 128
GROUPS = (4, 4)
norm_eps = 1e-06
F32 = jnp.float32
BF16 = jnp.bfloat16
MIB = 1024 * 1024
TOKEN = jax.ShapeDtypeStruct((8, BLK), jnp.int32)
WAIT_COST = 12.0
LATE_SHARE = 20.0
COLLECT_COST = 20.0
SLOTS_COST = 6.0
KERNEL_MIB = 24


def params(mib):
    return pltpu.CompilerParams(vmem_limit_bytes=mib * MIB)


def cost(flops, nbytes, transcendentals=0):
    return pl.CostEstimate(
        flops=int(flops), bytes_accessed=int(nbytes), transcendentals=int(transcendentals)
    )


def silu(v):
    half = 0.5 * v
    return half * jnp.tanh(half) + half


def earlier_mask(rows):
    first = lax.broadcasted_iota(jnp.int32, (rows, rows), 0)
    second = lax.broadcasted_iota(jnp.int32, (rows, rows), 1)
    return (first < second).astype(BF16)


def slot_row(owner_row, columns, capacity):
    rows = owner_row.shape[1]
    users = lax.broadcasted_iota(jnp.int32, (columns, rows), 0)
    mine = users == owner_row
    before = jnp.dot(mine.astype(BF16), earlier_mask(rows), preferred_element_type=F32)
    rank = jnp.sum(jnp.where(mine, before, 0.0), axis=0, keepdims=True)
    return owner_row.astype(F32) * capacity + rank


def whole(count=1):
    return [pl.BlockSpec(memory_space=pltpu.VMEM)] * count


def unread(arrays):
    return [pl.BlockSpec(memory_space=pl.ANY)] * len(arrays)


def query_kernel(slot_ref, visible_ref, x_ref, w_ref, send_ref):
    rows, width = x_ref.shape
    slots = send_ref.shape[0]
    index = lax.broadcasted_iota(jnp.int32, (slots, rows), 0)
    place = (index == slot_ref[:1, :]).astype(BF16)
    seen = jnp.broadcast_to(visible_ref[...].astype(F32), (BLK, rows)).T.astype(BF16)
    send_ref[:, width:] = jnp.dot(place, seen, preferred_element_type=F32).astype(BF16)
    tile = min(256, width)
    for start in range(0, width, tile):
        span = slice(start, start + tile)
        hidden = jnp.dot(x_ref[...], w_ref[:, span], preferred_element_type=F32)
        moved = jnp.dot(place, silu(hidden).astype(BF16), preferred_element_type=F32)
        send_ref[:, span] = moved.astype(BF16)


def project_queries(slot, visible_row, cand_x, w_in, slots):
    rows, width = cand_x.shape
    return pl.pallas_call(
        query_kernel,
        in_specs=whole(4),
        out_specs=whole()[0],
        out_shape=jax.ShapeDtypeStruct((slots, width + BLK), BF16),
        compiler_params=params(KERNEL_MIB),
        cost_estimate=cost(
            2 * rows * width * width + 2 * slots * rows * width,
            2 * (rows * width + width * width + slots * width),
            rows * width,
        ),
        name="project_queries",
    )(slot, visible_row, cand_x, w_in)


def gate_kernel(x_ref, w_ref, gate_ref, token_ref):
    token_ref[...] = jnp.zeros_like(token_ref)
    width = x_ref.shape[1]
    tile = min(256, width)
    for start in range(0, width, tile):
        columns = w_ref[:, width + start : width + start + tile]
        hidden = jnp.dot(x_ref[...], columns, preferred_element_type=F32)
        gate_ref[:, start : start + tile] = silu(hidden).astype(BF16)


def project_gate(cand_x, w_in):
    rows, width = cand_x.shape
    return pl.pallas_call(
        gate_kernel,
        in_specs=whole(2),
        out_specs=whole(2),
        out_shape=[jax.ShapeDtypeStruct((rows, width), BF16), TOKEN],
        compiler_params=params(KERNEL_MIB),
        cost_estimate=cost(
            2 * rows * width * width, 2 * (2 * rows * width + width * width), rows * width
        ),
        name="project_gate",
    )(cand_x, w_in)


def prepare_kernel(columns, capacity, spans, size, owner_ref, kv_hbm, row_ref, *refs):
    part_refs, sems = refs[:-1], refs[-1]
    width = kv_hbm.shape[1] // 2
    copies = []
    for (first, heads), ref in zip(spans, part_refs):
        wide = heads * size
        for start in (0, width):
            source = kv_hbm.at[:, start + first * size : start + first * size + wide]
            target = ref.at[:, wide * (start > 0) : wide * (start > 0) + wide]
            copies.append(pltpu.make_async_copy(source, target, sems.at[len(copies)]))
    for copy in copies:
        copy.start()
    row = slot_row(owner_ref[...], columns, capacity)
    row_ref[...] = jnp.broadcast_to(row, row_ref.shape).astype(jnp.int32)
    for copy in copies:
        copy.wait()


def prepare(owner_row, kv, spans, size, columns, capacity):
    rows = kv.shape[0]
    return pl.pallas_call(
        functools.partial(prepare_kernel, columns, capacity, spans, size),
        in_specs=whole() + [pl.BlockSpec(memory_space=pl.ANY)],
        out_specs=whole(1 + len(spans)),
        out_shape=[jax.ShapeDtypeStruct((8, owner_row.shape[1]), jnp.int32)]
        + [jax.ShapeDtypeStruct((rows, 2 * heads * size), BF16) for _, heads in spans],
        scratch_shapes=[pltpu.SemaphoreType.DMA((2 * len(spans),))],
        compiler_params=params(KERNEL_MIB),
        cost_estimate=cost(SLOTS_COST * 1e9, 0),
        name="prepare",
    )(owner_row, kv)


def wait_kernel(*refs):
    refs[-1][...] = jnp.zeros_like(refs[-1])


def wait_for(arrays):
    return pl.pallas_call(
        wait_kernel,
        in_specs=unread(arrays),
        out_specs=whole()[0],
        out_shape=TOKEN,
        compiler_params=params(KERNEL_MIB),
        cost_estimate=cost(WAIT_COST * 1e9, 0),
        name="wait_for",
    )(*arrays)


def column_kernel(columns, capacity, owner_ref, *refs):
    column_ref, token_ref = refs[-2:]
    token_ref[...] = jnp.zeros_like(token_ref)
    row = slot_row(owner_ref[...], columns, capacity)
    column_ref[...] = jnp.broadcast_to(row, (BLK, row.shape[1])).T.astype(jnp.int32)


def slot_column(owner_row, columns, capacity, after):
    rows = owner_row.shape[1]
    return pl.pallas_call(
        functools.partial(column_kernel, columns, capacity),
        in_specs=whole() + unread(after),
        out_specs=whole(2),
        out_shape=[jax.ShapeDtypeStruct((rows, BLK), jnp.int32), TOKEN],
        compiler_params=params(KERNEL_MIB),
        cost_estimate=cost(WAIT_COST * 1e9, 4 * rows * BLK),
        name="slot_column",
    )(owner_row, *after)


def attend_kernel(size, heads, first, starts, behind, has_base, capacity, length_ref, *refs):
    refs = refs[behind:]
    rows_ref, refs = refs[0], refs[1:]
    count = len(starts)
    parts = []
    for _, _, _, pieces in starts:
        parts.append(refs[:pieces])
        refs = refs[pieces:]
    base_ref = refs[0] if has_base else None
    outs = 3 if capacity else 1
    out_refs, shown = refs[int(has_base) : int(has_base) + outs], refs[int(has_base) + outs]
    result = out_refs[0] if outs == 1 else refs[-1]
    me = lax.axis_index("cand")
    places = [lax.axis_index("user") ^ start[0] for start in starts]
    slots = rows_ref.shape[0]
    columns_of = slots // capacity if capacity else 1
    keys = sum(piece.shape[0] for piece in parts[0])
    blocks = keys // BLK
    seen = rows_ref[:, HEADS * size :].astype(F32)
    for number in range(count):
        for block in range(blocks):
            start = (places[number] * blocks + block).astype(F32)
            shown[number * blocks + block] = (start < seen).astype(F32).astype(BF16)
    row = lax.broadcasted_iota(jnp.int32, (keys, size), 0)
    tile = min(512, slots)

    def columns(start):
        return slice(start, start + size)

    def read(part, start):
        return jnp.concatenate([piece[:, columns(start)] for piece in part], axis=0)

    def one_head(head):
        values = []
        for number, part in enumerate(parts):
            inside = row + places[number] * keys < length_ref[0]
            value = read(part, (starts[number][2] + head) * size).astype(F32)
            values.append(jnp.where(inside, value, 0.0).astype(BF16))
        values = jnp.concatenate(values, axis=0)
        for start in range(0, slots, tile):
            span = slice(start, start + tile)
            queries = rows_ref[span, columns((first + head) * size)]
            weights = []
            for number, part in enumerate(parts):
                scores = lax.dot_general(
                    queries,
                    read(part, (starts[number][1] + head) * size),
                    (((1,), (1,)), ((), ())),
                    preferred_element_type=F32,
                )
                for block in range(blocks):
                    half = scores[:, block * BLK : (block + 1) * BLK] * (0.5 / math.sqrt(size))
                    half = half.astype(BF16) * shown[number * blocks + block, span, :]
                    weights.append(half * jnp.tanh(half) + half)
            total = jnp.dot(
                jnp.concatenate(weights, axis=1), values, preferred_element_type=F32
            )
            if has_base:
                total = total + base_ref[span, columns(head * size)]
            result[span, columns(head * size)] = total.astype(result.dtype)

    for head in range(heads):
        one_head(head)
    if outs > 1:
        numbers = list(range(0, columns_of, 2)) + list(range(1, columns_of, 2))
        for ref in out_refs:
            for start in range(0, ref.shape[0], capacity):
                block = me ^ numbers.pop(0)
                source = pl.ds(pl.multiple_of(block * capacity, capacity), capacity)
                ref[start : start + capacity, :] = result[source, :]


def attend(length, after, rows, segments, base, first, heads, size, capacity, dtype, share):
    slots = rows.shape[0]
    keys = sum(piece.shape[0] for piece in segments[0][1])
    count = len(segments)
    starts = [(place, key, value, len(pieces)) for place, pieces, key, value in segments]
    pieces = [piece for _, pieces, _, _ in segments for piece in pieces]
    heights = [slots // 2, slots // 4, slots // 4] if capacity else [slots]
    outs = len(heights)
    extra = [] if base is None else [base]
    scratch = [pltpu.VMEM((count * (keys // BLK), slots, BLK), BF16)]
    if outs > 1:
        scratch.append(pltpu.VMEM((slots, heads * size), BF16))
    return pl.pallas_call(
        functools.partial(
            attend_kernel, size, heads, first, starts, len(after), base is not None, capacity
        ),
        in_specs=[pl.BlockSpec(memory_space=pltpu.SMEM)]
        + unread(after)
        + whole(1 + len(pieces) + len(extra)),
        out_specs=whole(outs),
        out_shape=[jax.ShapeDtypeStruct((height, heads * size), dtype) for height in heights],
        scratch_shapes=scratch,
        compiler_params=params(KERNEL_MIB),
        cost_estimate=cost(
            share * 4 * slots * keys * count * heads * size,
            2 * (2 * slots + count * keys * 2) * heads * size,
            slots * keys * count * heads,
        ),
        name="attend",
    )(length, *after, rows, *pieces, *extra)


def placement(slot, slots):
    lane = lax.broadcasted_iota(jnp.int32, (1, BLK), 1)
    return jnp.concatenate(
        [(lane + start == slot).astype(BF16) for start in range(0, slots, BLK)], axis=1
    )


def in_slots(parts, capacity):
    return jnp.concatenate(
        [part[:capacity, :] for part in parts[:2]] + [part[...] for part in parts[2:]], axis=0
    )


def collect_kernel(capacity, slots, slot_ref, *refs):
    rows = in_slots(refs[:-1], capacity)
    place = placement(slot_ref[...], slots)
    refs[-1][...] = jnp.dot(place, rows, preferred_element_type=F32).astype(BF16)


def collect(slot, parts, capacity, slots):
    rows, width = slot.shape[0], parts[0].shape[1]
    return pl.pallas_call(
        functools.partial(collect_kernel, capacity, slots),
        in_specs=whole(1 + len(parts)),
        out_specs=whole()[0],
        out_shape=jax.ShapeDtypeStruct((rows, width), BF16),
        compiler_params=params(KERNEL_MIB),
        cost_estimate=cost(COLLECT_COST * 1e9, 2 * (rows + slots) * width),
        name="collect",
    )(slot, *parts)


def finish_kernel(groups, capacity, slots, slot_ref, gain_ref, gate_ref, x_ref, w_ref, *refs):
    early, parts, (out_hbm, out_ref, sems) = refs[:groups], refs[groups:-3], refs[-3:]
    rows = x_ref.shape[0]
    place = placement(slot_ref[...], slots)
    late = jnp.dot(place, in_slots(parts, capacity), preferred_element_type=F32)
    tile = rows // 2
    stores = []
    for half in range(2):
        span = slice(half * tile, (half + 1) * tile)
        attn = jnp.concatenate([part[span, :].astype(F32) for part in early] + [late[span, :]], axis=1)
        centered = attn - jnp.mean(attn, axis=1, keepdims=True)
        variance = jnp.mean(centered * centered, axis=1, keepdims=True)
        normed = (centered * lax.rsqrt(variance + norm_eps) * gain_ref[...]).astype(BF16)
        mixed = (normed.astype(F32) * gate_ref[span, :].astype(F32)).astype(BF16)
        projected = jnp.dot(mixed, w_ref[...], preferred_element_type=F32)
        out_ref[span, :] = (x_ref[span, :].astype(F32) + projected).astype(BF16)
        store = pltpu.make_async_copy(out_ref.at[span, :], out_hbm.at[span, :], sems.at[half])
        store.start()
        stores.append(store)
    for store in stores:
        store.wait()


def finish(slot, early, gate, cand_x, ln_gain, w_out, parts, capacity, slots):
    rows, width = cand_x.shape
    return pl.pallas_call(
        functools.partial(finish_kernel, len(early), capacity, slots),
        in_specs=whole(5 + len(early) + len(parts)),
        out_specs=pl.BlockSpec(memory_space=pl.ANY),
        out_shape=jax.ShapeDtypeStruct((rows, width), BF16),
        scratch_shapes=[pltpu.VMEM((rows, width), BF16), pltpu.SemaphoreType.DMA((2,))],
        compiler_params=params(KERNEL_MIB),
        cost_estimate=cost(
            2 * rows * width * (width + slots), 2 * (3 * rows * width + width * width + slots * width)
        ),
        name="finish",
    )(slot, ln_gain.reshape(1, width), gate, cand_x, w_out, *early, *parts)


def swap(array, axis, bits, count):
    return lax.ppermute(array, axis, [(i, i ^ bits) for i in range(count)])


def exchange_cores(even, odds, capacity, count, behind):
    others = [swap(odd, "cand", 1, count) for odd in odds]
    if behind is not None:
        (even, others), _ = lax.optimization_barrier(((even, others), behind))
    pairs = []
    for d in range(1, count // 2):
        first, second = d * capacity, (d * capacity) % odds[0].shape[0]
        other = others[first // odds[0].shape[0]]
        pairs.append(
            jnp.concatenate(
                [even[first : first + capacity], other[second : second + capacity]], axis=0
            )
        )
    return [even, others[0]], pairs


def exchange_chips(pairs, count):
    return [swap(pair, "cand", 2 * d, count) for d, pair in enumerate(pairs, 1)]


def per_device(cand_x, cand_user, visible, hist_len, kv_cache, w_in, w_out, ln_gain):
    rows, width = cand_x.shape
    columns = lax.axis_size("cand")
    count = lax.axis_size("user")
    size = width // HEADS
    capacity = 2 * rows // columns
    slots = columns * capacity
    me = lax.axis_index("cand").astype(jnp.int32)
    owner_row = cand_user.reshape(1, rows)
    visible_row = visible.reshape(1, rows)
    spans = [(sum(GROUPS[:number]), heads) for number, heads in enumerate(GROUPS)]

    gate, gated = project_gate(cand_x, w_in)
    row, *parts = prepare(owner_row, kv_cache[0], spans, size, columns, capacity)
    send = project_queries(row, visible_row, cand_x, w_in, slots)
    near = None
    far = []
    for part in parts:
        if far:
            part, _ = lax.optimization_barrier((part, (far[-1], gated, send)))
        held = {0: part}
        bit = count // 2
        while bit > 1:
            for key in sorted(held):
                held[key | bit] = swap(held[key], "user", bit, count)
            bit //= 2
        if near is None:
            own, _ = lax.optimization_barrier((kv_cache[0], row))
            near = swap(own, "user", 1, count)
        far.append(held)
    evens = sorted(far[0])

    got = lax.all_to_all(
        send.reshape(columns, capacity, -1), "cand", split_axis=0, concat_axis=0, tiled=True
    ).reshape(slots, -1)
    arrived = [gated, near] + [far[0][key] for key in evens[1:]]
    slot, started = slot_column(owner_row ^ me, columns, capacity, arrived)
    early = []
    after = [started]
    behind = None
    for number, (first, heads) in enumerate(spans):
        held = far[number]
        cuts = [(key | 1, [swap(held[key], "user", 1, count)], 0, heads) for key in evens[1:]]
        segments = [(key, [held[key]], 0, heads) for key in evens]
        segments.append((1, [near], first, HEADS + first))
        base = attend(
            hist_len, after, got, segments, None, first, heads, size, None, F32, 0.0
        )[0]
        attn = attend(
            hist_len,
            [],
            got,
            cuts,
            base,
            first,
            heads,
            size,
            capacity,
            BF16,
            LATE_SHARE * (number > 0),
        )
        here, pairs = exchange_cores(attn[0], attn[1:], capacity, columns, behind)
        away = exchange_chips(pairs, columns)
        if number + 1 < len(spans):
            token = wait_for([attn[0]] + [far[number + 1][key] for key in evens[1:]])
            after = [token] + pairs
            early.append(collect(slot, here + away, capacity, slots))
            behind = early[-1]
    return finish(slot, early, gate, cand_x, ln_gain, w_out, here + away, capacity, slots)


def solution(mesh):
    in_specs = (
        P(("user", "cand"), None),
        P(("user", "cand"), None),
        P(("user", "cand")),
        P("cand"),
        P("cand", "user", None),
        P(),
        P(),
        P(),
    )
    out_specs = P(("user", "cand"), None)
    return jax.shard_map(
        per_device, mesh=mesh, in_specs=in_specs, out_specs=out_specs, check_vma=False
    )
```

```python
import functools
import math

import jax
import jax.numpy as jnp
from jax import lax
from jax.experimental import pallas as pl
from jax.experimental.pallas import tpu as pltpu
from jax.sharding import PartitionSpec as P

HEADS = 8
BLK = 128
GROUPS = (4, 4)
PIECES = (1, 1)
norm_eps = 1e-06
F32 = jnp.float32
BF16 = jnp.bfloat16
MIB = 1024 * 1024
TOKEN = jax.ShapeDtypeStruct((8, BLK), jnp.int32)
WAIT_COST = 20.0
LATE_SHARE = 20.0
COLLECT_COST = 20.0
SLOTS_COST = 6.0
KERNEL_MIB = 24


def params(mib):
    return pltpu.CompilerParams(vmem_limit_bytes=mib * MIB)


def cost(flops, nbytes, transcendentals=0):
    return pl.CostEstimate(
        flops=int(flops), bytes_accessed=int(nbytes), transcendentals=int(transcendentals)
    )


def silu(v):
    half = 0.5 * v
    return half * jnp.tanh(half) + half


def earlier_mask(rows):
    first = lax.broadcasted_iota(jnp.int32, (rows, rows), 0)
    second = lax.broadcasted_iota(jnp.int32, (rows, rows), 1)
    return (first < second).astype(BF16)


def slot_row(owner_row, columns, capacity):
    rows = owner_row.shape[1]
    users = lax.broadcasted_iota(jnp.int32, (columns, rows), 0)
    mine = users == owner_row
    before = jnp.dot(mine.astype(BF16), earlier_mask(rows), preferred_element_type=F32)
    rank = jnp.sum(jnp.where(mine, before, 0.0), axis=0, keepdims=True)
    return owner_row.astype(F32) * capacity + rank


def whole(count=1):
    return [pl.BlockSpec(memory_space=pltpu.VMEM)] * count


def unread(arrays):
    return [pl.BlockSpec(memory_space=pl.ANY)] * len(arrays)


def query_kernel(slot_ref, visible_ref, x_ref, w_ref, send_ref):
    rows, width = x_ref.shape
    slots = send_ref.shape[0]
    index = lax.broadcasted_iota(jnp.int32, (slots, rows), 0)
    place = (index == slot_ref[:1, :]).astype(BF16)
    seen = jnp.broadcast_to(visible_ref[...].astype(F32), (BLK, rows)).T.astype(BF16)
    send_ref[:, width:] = jnp.dot(place, seen, preferred_element_type=F32).astype(BF16)
    tile = min(256, width)
    for start in range(0, width, tile):
        span = slice(start, start + tile)
        hidden = jnp.dot(x_ref[...], w_ref[:, span], preferred_element_type=F32)
        moved = jnp.dot(place, silu(hidden).astype(BF16), preferred_element_type=F32)
        send_ref[:, span] = moved.astype(BF16)


def project_queries(slot, visible_row, cand_x, w_in, slots):
    rows, width = cand_x.shape
    return pl.pallas_call(
        query_kernel,
        in_specs=whole(4),
        out_specs=whole()[0],
        out_shape=jax.ShapeDtypeStruct((slots, width + BLK), BF16),
        compiler_params=params(KERNEL_MIB),
        cost_estimate=cost(
            2 * rows * width * width + 2 * slots * rows * width,
            2 * (rows * width + width * width + slots * width),
            rows * width,
        ),
        name="project_queries",
    )(slot, visible_row, cand_x, w_in)


def gate_kernel(x_ref, w_ref, gate_ref, token_ref):
    token_ref[...] = jnp.zeros_like(token_ref)
    width = x_ref.shape[1]
    tile = min(256, width)
    for start in range(0, width, tile):
        columns = w_ref[:, width + start : width + start + tile]
        hidden = jnp.dot(x_ref[...], columns, preferred_element_type=F32)
        gate_ref[:, start : start + tile] = silu(hidden).astype(BF16)


def project_gate(cand_x, w_in):
    rows, width = cand_x.shape
    return pl.pallas_call(
        gate_kernel,
        in_specs=whole(2),
        out_specs=whole(2),
        out_shape=[jax.ShapeDtypeStruct((rows, width), BF16), TOKEN],
        compiler_params=params(KERNEL_MIB),
        cost_estimate=cost(
            2 * rows * width * width, 2 * (2 * rows * width + width * width), rows * width
        ),
        name="project_gate",
    )(cand_x, w_in)


def prepare_kernel(columns, capacity, spans, size, owner_ref, kv_hbm, row_ref, *refs):
    part_refs, sems = list(refs[:-1]), refs[-1]
    keys, width = kv_hbm.shape[0], kv_hbm.shape[1] // 2
    copies = []
    for (first, heads), count in zip(spans, PIECES):
        wide, height = heads * size, keys // count
        for number in range(count):
            ref = part_refs.pop(0)
            for half in range(2):
                start = half * width + first * size
                source = kv_hbm.at[number * height : (number + 1) * height, start : start + wide]
                target = ref.at[:, half * wide : (half + 1) * wide]
                copies.append(pltpu.make_async_copy(source, target, sems.at[len(copies)]))
    for copy in copies:
        copy.start()
    row = slot_row(owner_ref[...], columns, capacity)
    row_ref[...] = jnp.broadcast_to(row, row_ref.shape).astype(jnp.int32)
    for copy in copies:
        copy.wait()


def prepare(owner_row, kv, spans, size, columns, capacity):
    shapes = []
    for (_, heads), count in zip(spans, PIECES):
        shape = (kv.shape[0] // count, 2 * heads * size)
        shapes += [jax.ShapeDtypeStruct(shape, BF16)] * count
    row, *parts = pl.pallas_call(
        functools.partial(prepare_kernel, columns, capacity, spans, size),
        in_specs=whole() + [pl.BlockSpec(memory_space=pl.ANY)],
        out_specs=whole(1 + len(shapes)),
        out_shape=[jax.ShapeDtypeStruct((8, owner_row.shape[1]), jnp.int32)] + shapes,
        scratch_shapes=[pltpu.SemaphoreType.DMA((2 * len(shapes),))],
        compiler_params=params(KERNEL_MIB),
        cost_estimate=cost(SLOTS_COST * 1e9, 0),
        name="prepare",
    )(owner_row, kv)
    return row, [[parts.pop(0) for _ in range(count)] for count in PIECES]


def wait_kernel(*refs):
    refs[-1][...] = jnp.zeros_like(refs[-1])


def wait_for(arrays):
    return pl.pallas_call(
        wait_kernel,
        in_specs=unread(arrays),
        out_specs=whole()[0],
        out_shape=TOKEN,
        compiler_params=params(KERNEL_MIB),
        cost_estimate=cost(WAIT_COST * 1e9, 0),
        name="wait_for",
    )(*arrays)


def column_kernel(columns, capacity, owner_ref, *refs):
    column_ref, token_ref = refs[-2:]
    token_ref[...] = jnp.zeros_like(token_ref)
    row = slot_row(owner_ref[...], columns, capacity)
    column_ref[...] = jnp.broadcast_to(row, (BLK, row.shape[1])).T.astype(jnp.int32)


def slot_column(owner_row, columns, capacity, after):
    rows = owner_row.shape[1]
    return pl.pallas_call(
        functools.partial(column_kernel, columns, capacity),
        in_specs=whole() + unread(after),
        out_specs=whole(2),
        out_shape=[jax.ShapeDtypeStruct((rows, BLK), jnp.int32), TOKEN],
        compiler_params=params(KERNEL_MIB),
        cost_estimate=cost(WAIT_COST * 1e9, 4 * rows * BLK),
        name="slot_column",
    )(owner_row, *after)


def attend_kernel(size, heads, first, starts, behind, has_base, capacity, length_ref, *refs):
    refs = refs[behind:]
    rows_ref, refs = refs[0], refs[1:]
    count = len(starts)
    parts = []
    for _, _, _, pieces in starts:
        parts.append(refs[:pieces])
        refs = refs[pieces:]
    base_ref = refs[0] if has_base else None
    outs = 3 if capacity else 1
    out_refs, shown = refs[int(has_base) : int(has_base) + outs], refs[int(has_base) + outs]
    result = out_refs[0] if outs == 1 else refs[-1]
    me = lax.axis_index("cand")
    places = [lax.axis_index("user") ^ start[0] for start in starts]
    slots = rows_ref.shape[0]
    columns_of = slots // capacity if capacity else 1
    keys = sum(piece.shape[0] for piece in parts[0])
    blocks = keys // BLK
    seen = rows_ref[:, HEADS * size :].astype(F32)
    for number in range(count):
        for block in range(blocks):
            start = (places[number] * blocks + block).astype(F32)
            shown[number * blocks + block] = (start < seen).astype(F32).astype(BF16)
    row = lax.broadcasted_iota(jnp.int32, (keys, size), 0)
    tile = min(512, slots)

    def columns(start):
        return slice(start, start + size)

    def read(part, start):
        return jnp.concatenate([piece[:, columns(start)] for piece in part], axis=0)

    def one_head(head):
        values = []
        for number, part in enumerate(parts):
            inside = row + places[number] * keys < length_ref[0]
            value = read(part, (starts[number][2] + head) * size).astype(F32)
            values.append(jnp.where(inside, value, 0.0).astype(BF16))
        values = jnp.concatenate(values, axis=0)
        for start in range(0, slots, tile):
            span = slice(start, start + tile)
            queries = rows_ref[span, columns((first + head) * size)]
            weights = []
            for number, part in enumerate(parts):
                scores = lax.dot_general(
                    queries,
                    read(part, (starts[number][1] + head) * size),
                    (((1,), (1,)), ((), ())),
                    preferred_element_type=F32,
                )
                for block in range(blocks):
                    half = scores[:, block * BLK : (block + 1) * BLK] * (0.5 / math.sqrt(size))
                    half = half.astype(BF16) * shown[number * blocks + block, span, :]
                    weights.append(half * jnp.tanh(half) + half)
            total = jnp.dot(
                jnp.concatenate(weights, axis=1), values, preferred_element_type=F32
            )
            if has_base:
                total = total + base_ref[span, columns(head * size)]
            result[span, columns(head * size)] = total.astype(result.dtype)

    for head in range(heads):
        one_head(head)
    if outs > 1:
        numbers = list(range(0, columns_of, 2)) + list(range(1, columns_of, 2))
        for ref in out_refs:
            for start in range(0, ref.shape[0], capacity):
                block = me ^ numbers.pop(0)
                source = pl.ds(pl.multiple_of(block * capacity, capacity), capacity)
                ref[start : start + capacity, :] = result[source, :]


def attend(length, after, rows, segments, base, first, heads, size, capacity, dtype, share):
    slots = rows.shape[0]
    keys = sum(piece.shape[0] for piece in segments[0][1])
    count = len(segments)
    starts = [(place, key, value, len(pieces)) for place, pieces, key, value in segments]
    pieces = [piece for _, pieces, _, _ in segments for piece in pieces]
    heights = [slots // 2, slots // 4, slots // 4] if capacity else [slots]
    outs = len(heights)
    extra = [] if base is None else [base]
    scratch = [pltpu.VMEM((count * (keys // BLK), slots, BLK), BF16)]
    if outs > 1:
        scratch.append(pltpu.VMEM((slots, heads * size), BF16))
    return pl.pallas_call(
        functools.partial(
            attend_kernel, size, heads, first, starts, len(after), base is not None, capacity
        ),
        in_specs=[pl.BlockSpec(memory_space=pltpu.SMEM)]
        + unread(after)
        + whole(1 + len(pieces) + len(extra)),
        out_specs=whole(outs),
        out_shape=[jax.ShapeDtypeStruct((height, heads * size), dtype) for height in heights],
        scratch_shapes=scratch,
        compiler_params=params(KERNEL_MIB),
        cost_estimate=cost(
            share * 4 * slots * keys * count * heads * size,
            2 * (2 * slots + count * keys * 2) * heads * size,
            slots * keys * count * heads,
        ),
        name="attend",
    )(length, *after, rows, *pieces, *extra)


def placement(slot, slots):
    lane = lax.broadcasted_iota(jnp.int32, (1, BLK), 1)
    return jnp.concatenate(
        [(lane + start == slot).astype(BF16) for start in range(0, slots, BLK)], axis=1
    )


def in_slots(parts, capacity):
    return jnp.concatenate(
        [part[:capacity, :] for part in parts[:2]] + [part[...] for part in parts[2:]], axis=0
    )


def collect_kernel(capacity, slots, slot_ref, *refs):
    rows = in_slots(refs[:-1], capacity)
    place = placement(slot_ref[...], slots)
    refs[-1][...] = jnp.dot(place, rows, preferred_element_type=F32).astype(BF16)


def collect(slot, parts, capacity, slots):
    rows, width = slot.shape[0], parts[0].shape[1]
    return pl.pallas_call(
        functools.partial(collect_kernel, capacity, slots),
        in_specs=whole(1 + len(parts)),
        out_specs=whole()[0],
        out_shape=jax.ShapeDtypeStruct((rows, width), BF16),
        compiler_params=params(KERNEL_MIB),
        cost_estimate=cost(COLLECT_COST * 1e9, 2 * (rows + slots) * width),
        name="collect",
    )(slot, *parts)


def finish_kernel(groups, capacity, slots, slot_ref, gain_ref, gate_ref, x_ref, w_ref, *refs):
    early, parts, (out_hbm, out_ref, sems) = refs[:groups], refs[groups:-3], refs[-3:]
    rows = x_ref.shape[0]
    place = placement(slot_ref[...], slots)
    late = jnp.dot(place, in_slots(parts, capacity), preferred_element_type=F32)
    tile = rows // 2
    stores = []
    for half in range(2):
        span = slice(half * tile, (half + 1) * tile)
        attn = jnp.concatenate([part[span, :].astype(F32) for part in early] + [late[span, :]], axis=1)
        centered = attn - jnp.mean(attn, axis=1, keepdims=True)
        variance = jnp.mean(centered * centered, axis=1, keepdims=True)
        normed = (centered * lax.rsqrt(variance + norm_eps) * gain_ref[...]).astype(BF16)
        mixed = (normed.astype(F32) * gate_ref[span, :].astype(F32)).astype(BF16)
        projected = jnp.dot(mixed, w_ref[...], preferred_element_type=F32)
        out_ref[span, :] = (x_ref[span, :].astype(F32) + projected).astype(BF16)
        store = pltpu.make_async_copy(out_ref.at[span, :], out_hbm.at[span, :], sems.at[half])
        store.start()
        stores.append(store)
    for store in stores:
        store.wait()


def finish(slot, early, gate, cand_x, ln_gain, w_out, parts, capacity, slots):
    rows, width = cand_x.shape
    return pl.pallas_call(
        functools.partial(finish_kernel, len(early), capacity, slots),
        in_specs=whole(5 + len(early) + len(parts)),
        out_specs=pl.BlockSpec(memory_space=pl.ANY),
        out_shape=jax.ShapeDtypeStruct((rows, width), BF16),
        scratch_shapes=[pltpu.VMEM((rows, width), BF16), pltpu.SemaphoreType.DMA((2,))],
        compiler_params=params(KERNEL_MIB),
        cost_estimate=cost(
            2 * rows * width * (width + slots), 2 * (3 * rows * width + width * width + slots * width)
        ),
        name="finish",
    )(slot, ln_gain.reshape(1, width), gate, cand_x, w_out, *early, *parts)


def swap(array, axis, bits, count):
    return lax.ppermute(array, axis, [(i, i ^ bits) for i in range(count)])


def tied(arrays, behind):
    return lax.optimization_barrier((arrays, behind))[0]


def neighbours(pieces, count):
    back = []
    for piece in pieces:
        back.append(swap(tied(piece, back[-1]) if back else piece, "user", 1, count))
    return back


def exchange_cores(even, odds, capacity, count, behind):
    others = [swap(odd, "cand", 1, count) for odd in odds]
    if behind is not None:
        (even, others), _ = lax.optimization_barrier(((even, others), behind))
    pairs = []
    for d in range(1, count // 2):
        first, second = d * capacity, (d * capacity) % odds[0].shape[0]
        other = others[first // odds[0].shape[0]]
        pairs.append(
            jnp.concatenate(
                [even[first : first + capacity], other[second : second + capacity]], axis=0
            )
        )
    return [even, others[0]], pairs


def exchange_chips(pairs, count):
    return [swap(pair, "cand", 2 * d, count) for d, pair in enumerate(pairs, 1)]


def per_device(cand_x, cand_user, visible, hist_len, kv_cache, w_in, w_out, ln_gain):
    rows, width = cand_x.shape
    columns = lax.axis_size("cand")
    count = lax.axis_size("user")
    size = width // HEADS
    capacity = 2 * rows // columns
    slots = columns * capacity
    me = lax.axis_index("cand").astype(jnp.int32)
    owner_row = cand_user.reshape(1, rows)
    visible_row = visible.reshape(1, rows)
    spans = [(sum(GROUPS[:number]), heads) for number, heads in enumerate(GROUPS)]

    gate, gated = project_gate(cand_x, w_in)
    row, parts = prepare(owner_row, kv_cache[0], spans, size, columns, capacity)
    send = project_queries(row, visible_row, cand_x, w_in, slots)
    far = []
    for number, pieces in enumerate(parts):
        if far:
            pieces = tied(pieces, (far[-1], gated, send))
        held = {0: pieces}
        bit = count // 2
        while bit > 1:
            for key in sorted(held):
                held[key | bit] = [swap(piece, "user", bit, count) for piece in held[key]]
            bit //= 2
        far.append(held)
    evens = sorted(far[0])
    near = []
    for number, pieces in enumerate(parts):
        if number:
            pieces = tied(pieces, [far[number][key] for key in evens[1:]])
        near.append(neighbours(pieces, count))

    got = lax.all_to_all(
        send.reshape(columns, capacity, -1), "cand", split_axis=0, concat_axis=0, tiled=True
    ).reshape(slots, -1)
    arrived = [gated] + near[0]
    for key in evens[1:]:
        arrived += far[0][key]
    slot, started = slot_column(owner_row ^ me, columns, capacity, arrived)
    early = []
    after = [started]
    behind = None
    for number, (first, heads) in enumerate(spans):
        held = far[number]
        close = (1, near[number], 0, heads)
        segments = [(key, held[key], 0, heads) for key in evens] + [close] * (number == 0)
        cuts = [(key | 1, neighbours(held[key], count), 0, heads) for key in evens[1:]]
        cuts += [close] * (number > 0)
        base = attend(
            hist_len, after, got, segments, None, first, heads, size, None, F32, 0.0
        )[0]
        attn = attend(
            hist_len,
            [],
            got,
            cuts,
            base,
            first,
            heads,
            size,
            capacity,
            BF16,
            LATE_SHARE * (number > 0),
        )
        here, pairs = exchange_cores(attn[0], attn[1:], capacity, columns, behind)
        away = exchange_chips(pairs, columns)
        if number + 1 < len(spans):
            token = wait_for(
                [attn[0]] + [piece for key in evens[1:] for piece in far[number + 1][key]]
            )
            after = [token] + pairs
            early.append(collect(slot, here + away, capacity, slots))
            behind = early[-1]
    return finish(slot, early, gate, cand_x, ln_gain, w_out, here + away, capacity, slots)


def solution(mesh):
    in_specs = (
        P(("user", "cand"), None),
        P(("user", "cand"), None),
        P(("user", "cand")),
        P("cand"),
        P("cand", "user", None),
        P(),
        P(),
        P(),
    )
    out_specs = P(("user", "cand"), None)
    return jax.shard_map(
        per_device, mesh=mesh, in_specs=in_specs, out_specs=out_specs, check_vma=False
    )
```

```python
import functools
import math

import jax
import jax.numpy as jnp
from jax import lax
from jax.experimental import pallas as pl
from jax.experimental.pallas import tpu as pltpu
from jax.sharding import PartitionSpec as P

HEADS = 8
BLK = 128
GROUPS = (4, 4)
norm_eps = 1e-06
F32 = jnp.float32
BF16 = jnp.bfloat16
MIB = 1024 * 1024
TOKEN = jax.ShapeDtypeStruct((8, BLK), jnp.int32)
WAIT_COST = 20.0
LATE_SHARE = 20.0
COLLECT_COST = 20.0
SLOTS_COST = 6.0
KERNEL_MIB = 24


def params(mib):
    return pltpu.CompilerParams(vmem_limit_bytes=mib * MIB)


def cost(flops, nbytes, transcendentals=0):
    return pl.CostEstimate(
        flops=int(flops), bytes_accessed=int(nbytes), transcendentals=int(transcendentals)
    )


def silu(v):
    half = 0.5 * v
    return half * jnp.tanh(half) + half


def earlier_mask(rows):
    first = lax.broadcasted_iota(jnp.int32, (rows, rows), 0)
    second = lax.broadcasted_iota(jnp.int32, (rows, rows), 1)
    return (first < second).astype(BF16)


def slot_row(owner_row, columns, capacity):
    rows = owner_row.shape[1]
    users = lax.broadcasted_iota(jnp.int32, (columns, rows), 0)
    mine = users == owner_row
    before = jnp.dot(mine.astype(BF16), earlier_mask(rows), preferred_element_type=F32)
    rank = jnp.sum(jnp.where(mine, before, 0.0), axis=0, keepdims=True)
    return owner_row.astype(F32) * capacity + rank


def whole(count=1):
    return [pl.BlockSpec(memory_space=pltpu.VMEM)] * count


def unread(arrays):
    return [pl.BlockSpec(memory_space=pl.ANY)] * len(arrays)


def query_kernel(slot_ref, visible_ref, x_ref, w_ref, send_ref):
    rows, width = x_ref.shape
    slots = send_ref.shape[0]
    index = lax.broadcasted_iota(jnp.int32, (slots, rows), 0)
    place = (index == slot_ref[:1, :]).astype(BF16)
    seen = jnp.broadcast_to(visible_ref[...].astype(F32), (BLK, rows)).T.astype(BF16)
    send_ref[:, width:] = jnp.dot(place, seen, preferred_element_type=F32).astype(BF16)
    tile = min(256, width)
    for start in range(0, width, tile):
        span = slice(start, start + tile)
        hidden = jnp.dot(x_ref[...], w_ref[:, span], preferred_element_type=F32)
        moved = jnp.dot(place, silu(hidden).astype(BF16), preferred_element_type=F32)
        send_ref[:, span] = moved.astype(BF16)


def project_queries(slot, visible_row, cand_x, w_in, slots):
    rows, width = cand_x.shape
    return pl.pallas_call(
        query_kernel,
        in_specs=whole(4),
        out_specs=whole()[0],
        out_shape=jax.ShapeDtypeStruct((slots, width + BLK), BF16),
        compiler_params=params(KERNEL_MIB),
        cost_estimate=cost(
            2 * rows * width * width + 2 * slots * rows * width,
            2 * (rows * width + width * width + slots * width),
            rows * width,
        ),
        name="project_queries",
    )(slot, visible_row, cand_x, w_in)


def gate_kernel(x_ref, w_ref, gate_ref, token_ref):
    token_ref[...] = jnp.zeros_like(token_ref)
    width = x_ref.shape[1]
    tile = min(256, width)
    for start in range(0, width, tile):
        columns = w_ref[:, width + start : width + start + tile]
        hidden = jnp.dot(x_ref[...], columns, preferred_element_type=F32)
        gate_ref[:, start : start + tile] = silu(hidden).astype(BF16)


def project_gate(cand_x, w_in):
    rows, width = cand_x.shape
    return pl.pallas_call(
        gate_kernel,
        in_specs=whole(2),
        out_specs=whole(2),
        out_shape=[jax.ShapeDtypeStruct((rows, width), BF16), TOKEN],
        compiler_params=params(KERNEL_MIB),
        cost_estimate=cost(
            2 * rows * width * width, 2 * (2 * rows * width + width * width), rows * width
        ),
        name="project_gate",
    )(cand_x, w_in)


def prepare_kernel(columns, capacity, spans, size, owner_ref, kv_hbm, row_ref, *refs):
    part_refs, sems = refs[:-1], refs[-1]
    width = kv_hbm.shape[1] // 2
    copies = []
    for (first, heads), ref in zip(spans, part_refs):
        wide = heads * size
        for start in (0, width):
            source = kv_hbm.at[:, start + first * size : start + first * size + wide]
            target = ref.at[:, wide * (start > 0) : wide * (start > 0) + wide]
            copies.append(pltpu.make_async_copy(source, target, sems.at[len(copies)]))
    for copy in copies:
        copy.start()
    row = slot_row(owner_ref[...], columns, capacity)
    row_ref[...] = jnp.broadcast_to(row, row_ref.shape).astype(jnp.int32)
    for copy in copies:
        copy.wait()


def prepare(owner_row, kv, spans, size, columns, capacity):
    rows = kv.shape[0]
    return pl.pallas_call(
        functools.partial(prepare_kernel, columns, capacity, spans, size),
        in_specs=whole() + [pl.BlockSpec(memory_space=pl.ANY)],
        out_specs=whole(1 + len(spans)),
        out_shape=[jax.ShapeDtypeStruct((8, owner_row.shape[1]), jnp.int32)]
        + [jax.ShapeDtypeStruct((rows, 2 * heads * size), BF16) for _, heads in spans],
        scratch_shapes=[pltpu.SemaphoreType.DMA((2 * len(spans),))],
        compiler_params=params(KERNEL_MIB),
        cost_estimate=cost(SLOTS_COST * 1e9, 0),
        name="prepare",
    )(owner_row, kv)


def wait_kernel(*refs):
    refs[-1][...] = jnp.zeros_like(refs[-1])


def wait_for(arrays):
    return pl.pallas_call(
        wait_kernel,
        in_specs=unread(arrays),
        out_specs=whole()[0],
        out_shape=TOKEN,
        compiler_params=params(KERNEL_MIB),
        cost_estimate=cost(WAIT_COST * 1e9, 0),
        name="wait_for",
    )(*arrays)


def column_kernel(columns, capacity, owner_ref, *refs):
    column_ref, token_ref = refs[-2:]
    token_ref[...] = jnp.zeros_like(token_ref)
    row = slot_row(owner_ref[...], columns, capacity)
    column_ref[...] = jnp.broadcast_to(row, (BLK, row.shape[1])).T.astype(jnp.int32)


def slot_column(owner_row, columns, capacity, after):
    rows = owner_row.shape[1]
    return pl.pallas_call(
        functools.partial(column_kernel, columns, capacity),
        in_specs=whole() + unread(after),
        out_specs=whole(2),
        out_shape=[jax.ShapeDtypeStruct((rows, BLK), jnp.int32), TOKEN],
        compiler_params=params(KERNEL_MIB),
        cost_estimate=cost(WAIT_COST * 1e9, 4 * rows * BLK),
        name="slot_column",
    )(owner_row, *after)


def attend_kernel(size, heads, first, starts, behind, has_base, capacity, length_ref, *refs):
    refs = refs[behind:]
    rows_ref, refs = refs[0], refs[1:]
    count = len(starts)
    parts = []
    for _, _, _, pieces in starts:
        parts.append(refs[:pieces])
        refs = refs[pieces:]
    base_ref = refs[0] if has_base else None
    outs = 3 if capacity else 1
    out_refs, shown = refs[int(has_base) : int(has_base) + outs], refs[int(has_base) + outs]
    result = out_refs[0] if outs == 1 else refs[-1]
    me = lax.axis_index("cand")
    places = [lax.axis_index("user") ^ start[0] for start in starts]
    slots = rows_ref.shape[0]
    columns_of = slots // capacity if capacity else 1
    keys = sum(piece.shape[0] for piece in parts[0])
    blocks = keys // BLK
    seen = rows_ref[:, HEADS * size :].astype(F32)
    for number in range(count):
        for block in range(blocks):
            start = (places[number] * blocks + block).astype(F32)
            shown[number * blocks + block] = (start < seen).astype(F32).astype(BF16)
    row = lax.broadcasted_iota(jnp.int32, (keys, size), 0)
    tile = min(512, slots)

    def columns(start):
        return slice(start, start + size)

    def read(part, start):
        return jnp.concatenate([piece[:, columns(start)] for piece in part], axis=0)

    def one_head(head):
        values = []
        for number, part in enumerate(parts):
            inside = row + places[number] * keys < length_ref[0]
            value = read(part, (starts[number][2] + head) * size).astype(F32)
            values.append(jnp.where(inside, value, 0.0).astype(BF16))
        values = jnp.concatenate(values, axis=0)
        for start in range(0, slots, tile):
            span = slice(start, start + tile)
            queries = rows_ref[span, columns((first + head) * size)]
            weights = []
            for number, part in enumerate(parts):
                scores = lax.dot_general(
                    queries,
                    read(part, (starts[number][1] + head) * size),
                    (((1,), (1,)), ((), ())),
                    preferred_element_type=F32,
                )
                for block in range(blocks):
                    half = scores[:, block * BLK : (block + 1) * BLK] * (0.5 / math.sqrt(size))
                    half = half.astype(BF16) * shown[number * blocks + block, span, :]
                    weights.append(half * jnp.tanh(half) + half)
            total = jnp.dot(
                jnp.concatenate(weights, axis=1), values, preferred_element_type=F32
            )
            if has_base:
                total = total + base_ref[span, columns(head * size)]
            result[span, columns(head * size)] = total.astype(result.dtype)

    for head in range(heads):
        one_head(head)
    if outs > 1:
        numbers = list(range(0, columns_of, 2)) + list(range(1, columns_of, 2))
        for ref in out_refs:
            for start in range(0, ref.shape[0], capacity):
                block = me ^ numbers.pop(0)
                source = pl.ds(pl.multiple_of(block * capacity, capacity), capacity)
                ref[start : start + capacity, :] = result[source, :]


def attend(length, after, rows, segments, base, first, heads, size, capacity, dtype, share):
    slots = rows.shape[0]
    keys = sum(piece.shape[0] for piece in segments[0][1])
    count = len(segments)
    starts = [(place, key, value, len(pieces)) for place, pieces, key, value in segments]
    pieces = [piece for _, pieces, _, _ in segments for piece in pieces]
    heights = [slots // 2, slots // 4, slots // 4] if capacity else [slots]
    outs = len(heights)
    extra = [] if base is None else [base]
    scratch = [pltpu.VMEM((count * (keys // BLK), slots, BLK), BF16)]
    if outs > 1:
        scratch.append(pltpu.VMEM((slots, heads * size), BF16))
    return pl.pallas_call(
        functools.partial(
            attend_kernel, size, heads, first, starts, len(after), base is not None, capacity
        ),
        in_specs=[pl.BlockSpec(memory_space=pltpu.SMEM)]
        + unread(after)
        + whole(1 + len(pieces) + len(extra)),
        out_specs=whole(outs),
        out_shape=[jax.ShapeDtypeStruct((height, heads * size), dtype) for height in heights],
        scratch_shapes=scratch,
        compiler_params=params(KERNEL_MIB),
        cost_estimate=cost(
            share * 4 * slots * keys * count * heads * size,
            2 * (2 * slots + count * keys * 2) * heads * size,
            slots * keys * count * heads,
        ),
        name="attend",
    )(length, *after, rows, *pieces, *extra)


def placement(slot, slots):
    lane = lax.broadcasted_iota(jnp.int32, (1, BLK), 1)
    return jnp.concatenate(
        [(lane + start == slot).astype(BF16) for start in range(0, slots, BLK)], axis=1
    )


def in_slots(parts, capacity):
    return jnp.concatenate(
        [part[:capacity, :] for part in parts[:2]] + [part[...] for part in parts[2:]], axis=0
    )


def collect_kernel(capacity, slots, slot_ref, *refs):
    rows = in_slots(refs[:-1], capacity)
    place = placement(slot_ref[...], slots)
    refs[-1][...] = jnp.dot(place, rows, preferred_element_type=F32).astype(BF16)


def collect(slot, parts, capacity, slots):
    rows, width = slot.shape[0], parts[0].shape[1]
    return pl.pallas_call(
        functools.partial(collect_kernel, capacity, slots),
        in_specs=whole(1 + len(parts)),
        out_specs=whole()[0],
        out_shape=jax.ShapeDtypeStruct((rows, width), BF16),
        compiler_params=params(KERNEL_MIB),
        cost_estimate=cost(COLLECT_COST * 1e9, 2 * (rows + slots) * width),
        name="collect",
    )(slot, *parts)


def finish_kernel(groups, capacity, slots, slot_ref, gain_ref, gate_ref, x_ref, w_ref, *refs):
    early, parts, (out_hbm, out_ref, sems) = refs[:groups], refs[groups:-3], refs[-3:]
    rows = x_ref.shape[0]
    place = placement(slot_ref[...], slots)
    late = jnp.dot(place, in_slots(parts, capacity), preferred_element_type=F32)
    tile = rows // 2
    stores = []
    for half in range(2):
        span = slice(half * tile, (half + 1) * tile)
        attn = jnp.concatenate([part[span, :].astype(F32) for part in early] + [late[span, :]], axis=1)
        centered = attn - jnp.mean(attn, axis=1, keepdims=True)
        variance = jnp.mean(centered * centered, axis=1, keepdims=True)
        normed = (centered * lax.rsqrt(variance + norm_eps) * gain_ref[...]).astype(BF16)
        mixed = (normed.astype(F32) * gate_ref[span, :].astype(F32)).astype(BF16)
        projected = jnp.dot(mixed, w_ref[...], preferred_element_type=F32)
        out_ref[span, :] = (x_ref[span, :].astype(F32) + projected).astype(BF16)
        store = pltpu.make_async_copy(out_ref.at[span, :], out_hbm.at[span, :], sems.at[half])
        store.start()
        stores.append(store)
    for store in stores:
        store.wait()


def finish(slot, early, gate, cand_x, ln_gain, w_out, parts, capacity, slots):
    rows, width = cand_x.shape
    return pl.pallas_call(
        functools.partial(finish_kernel, len(early), capacity, slots),
        in_specs=whole(5 + len(early) + len(parts)),
        out_specs=pl.BlockSpec(memory_space=pl.ANY),
        out_shape=jax.ShapeDtypeStruct((rows, width), BF16),
        scratch_shapes=[pltpu.VMEM((rows, width), BF16), pltpu.SemaphoreType.DMA((2,))],
        compiler_params=params(KERNEL_MIB),
        cost_estimate=cost(
            2 * rows * width * (width + slots), 2 * (3 * rows * width + width * width + slots * width)
        ),
        name="finish",
    )(slot, ln_gain.reshape(1, width), gate, cand_x, w_out, *early, *parts)


def swap(array, axis, bits, count):
    return lax.ppermute(array, axis, [(i, i ^ bits) for i in range(count)])


def exchange_cores(even, odds, capacity, count, behind):
    others = [swap(odd, "cand", 1, count) for odd in odds]
    if behind is not None:
        (even, others), _ = lax.optimization_barrier(((even, others), behind))
    pairs = []
    for d in range(1, count // 2):
        first, second = d * capacity, (d * capacity) % odds[0].shape[0]
        other = others[first // odds[0].shape[0]]
        pairs.append(
            jnp.concatenate(
                [even[first : first + capacity], other[second : second + capacity]], axis=0
            )
        )
    return [even, others[0]], pairs


def exchange_chips(pairs, count):
    return [swap(pair, "cand", 2 * d, count) for d, pair in enumerate(pairs, 1)]


def per_device(cand_x, cand_user, visible, hist_len, kv_cache, w_in, w_out, ln_gain):
    rows, width = cand_x.shape
    columns = lax.axis_size("cand")
    count = lax.axis_size("user")
    size = width // HEADS
    capacity = 2 * rows // columns
    slots = columns * capacity
    me = lax.axis_index("cand").astype(jnp.int32)
    owner_row = cand_user.reshape(1, rows)
    visible_row = visible.reshape(1, rows)
    spans = [(sum(GROUPS[:number]), heads) for number, heads in enumerate(GROUPS)]

    gate, gated = project_gate(cand_x, w_in)
    row, *parts = prepare(owner_row, kv_cache[0], spans, size, columns, capacity)
    send = project_queries(row, visible_row, cand_x, w_in, slots)
    near = None
    far = []
    for part in parts:
        if far:
            part, _ = lax.optimization_barrier((part, send))
        held = {0: part}
        bit = count // 2
        while bit > 1:
            for key in sorted(held):
                held[key | bit] = swap(held[key], "user", bit, count)
            bit //= 2
        if near is None:
            own, _ = lax.optimization_barrier((kv_cache[0], row))
            near = swap(own, "user", 1, count)
        far.append(held)
    evens = sorted(far[0])

    got = lax.all_to_all(
        send.reshape(columns, capacity, -1), "cand", split_axis=0, concat_axis=0, tiled=True
    ).reshape(slots, -1)
    arrived = [gated, near] + [held[key] for held in far for key in evens[1:]]
    slot, started = slot_column(owner_row ^ me, columns, capacity, arrived)
    early = []
    after = [started]
    behind = None
    for number, (first, heads) in enumerate(spans):
        held = far[number]
        cuts = [(key | 1, [swap(held[key], "user", 1, count)], 0, heads) for key in evens[1:]]
        segments = [(key, [held[key]], 0, heads) for key in evens]
        segments.append((1, [near], first, HEADS + first))
        base = attend(
            hist_len, after, got, segments, None, first, heads, size, None, F32, 0.0
        )[0]
        attn = attend(
            hist_len,
            [],
            got,
            cuts,
            base,
            first,
            heads,
            size,
            capacity,
            BF16,
            LATE_SHARE * (number > 0),
        )
        here, pairs = exchange_cores(attn[0], attn[1:], capacity, columns, behind)
        away = exchange_chips(pairs, columns)
        if number + 1 < len(spans):
            token = wait_for([attn[0]] + [far[number + 1][key] for key in evens[1:]])
            after = [token] + pairs
            early.append(collect(slot, here + away, capacity, slots))
            behind = early[-1]
    return finish(slot, early, gate, cand_x, ln_gain, w_out, here + away, capacity, slots)


def solution(mesh):
    in_specs = (
        P(("user", "cand"), None),
        P(("user", "cand"), None),
        P(("user", "cand")),
        P("cand"),
        P("cand", "user", None),
        P(),
        P(),
        P(),
    )
    out_specs = P(("user", "cand"), None)
    return jax.shard_map(
        per_device, mesh=mesh, in_specs=in_specs, out_specs=out_specs, check_vma=False
    )
```

```python
import functools
import math

import jax
import jax.numpy as jnp
from jax import lax
from jax.experimental import pallas as pl
from jax.experimental.pallas import tpu as pltpu
from jax.sharding import PartitionSpec as P

HEADS = 8
BLK = 128
GROUPS = (4, 4)
PIECES = (1, 1)
norm_eps = 1e-06
F32 = jnp.float32
BF16 = jnp.bfloat16
MIB = 1024 * 1024
TOKEN = jax.ShapeDtypeStruct((8, BLK), jnp.int32)
WAIT_COST = 20.0
LATE_SHARE = 20.0
COLLECT_COST = 20.0
SLOTS_COST = 6.0
KERNEL_MIB = 24


def params(mib):
    return pltpu.CompilerParams(vmem_limit_bytes=mib * MIB)


def cost(flops, nbytes, transcendentals=0):
    return pl.CostEstimate(
        flops=int(flops), bytes_accessed=int(nbytes), transcendentals=int(transcendentals)
    )


def silu(v):
    half = 0.5 * v
    return half * jnp.tanh(half) + half


def earlier_mask(rows):
    first = lax.broadcasted_iota(jnp.int32, (rows, rows), 0)
    second = lax.broadcasted_iota(jnp.int32, (rows, rows), 1)
    return (first < second).astype(BF16)


def slot_row(owner_row, columns, capacity):
    rows = owner_row.shape[1]
    users = lax.broadcasted_iota(jnp.int32, (columns, rows), 0)
    mine = users == owner_row
    before = jnp.dot(mine.astype(BF16), earlier_mask(rows), preferred_element_type=F32)
    rank = jnp.sum(jnp.where(mine, before, 0.0), axis=0, keepdims=True)
    return owner_row.astype(F32) * capacity + rank


def whole(count=1):
    return [pl.BlockSpec(memory_space=pltpu.VMEM)] * count


def unread(arrays):
    return [pl.BlockSpec(memory_space=pl.ANY)] * len(arrays)


def query_kernel(slot_ref, visible_ref, x_ref, w_ref, send_ref):
    rows, width = x_ref.shape
    slots = send_ref.shape[0]
    index = lax.broadcasted_iota(jnp.int32, (slots, rows), 0)
    place = (index == slot_ref[:1, :]).astype(BF16)
    seen = jnp.broadcast_to(visible_ref[...].astype(F32), (BLK, rows)).T.astype(BF16)
    send_ref[:, width:] = jnp.dot(place, seen, preferred_element_type=F32).astype(BF16)
    tile = min(256, width)
    for start in range(0, width, tile):
        span = slice(start, start + tile)
        hidden = jnp.dot(x_ref[...], w_ref[:, span], preferred_element_type=F32)
        moved = jnp.dot(place, silu(hidden).astype(BF16), preferred_element_type=F32)
        send_ref[:, span] = moved.astype(BF16)


def project_queries(slot, visible_row, cand_x, w_in, slots):
    rows, width = cand_x.shape
    return pl.pallas_call(
        query_kernel,
        in_specs=whole(4),
        out_specs=whole()[0],
        out_shape=jax.ShapeDtypeStruct((slots, width + BLK), BF16),
        compiler_params=params(KERNEL_MIB),
        cost_estimate=cost(
            2 * rows * width * width + 2 * slots * rows * width,
            2 * (rows * width + width * width + slots * width),
            rows * width,
        ),
        name="project_queries",
    )(slot, visible_row, cand_x, w_in)


def gate_kernel(x_ref, w_ref, gate_ref, token_ref):
    token_ref[...] = jnp.zeros_like(token_ref)
    width = x_ref.shape[1]
    tile = min(256, width)
    for start in range(0, width, tile):
        columns = w_ref[:, width + start : width + start + tile]
        hidden = jnp.dot(x_ref[...], columns, preferred_element_type=F32)
        gate_ref[:, start : start + tile] = silu(hidden).astype(BF16)


def project_gate(cand_x, w_in):
    rows, width = cand_x.shape
    return pl.pallas_call(
        gate_kernel,
        in_specs=whole(2),
        out_specs=whole(2),
        out_shape=[jax.ShapeDtypeStruct((rows, width), BF16), TOKEN],
        compiler_params=params(KERNEL_MIB),
        cost_estimate=cost(
            2 * rows * width * width, 2 * (2 * rows * width + width * width), rows * width
        ),
        name="project_gate",
    )(cand_x, w_in)


def prepare_kernel(columns, capacity, spans, size, owner_ref, kv_hbm, row_ref, *refs):
    part_refs, sems = list(refs[:-1]), refs[-1]
    keys, width = kv_hbm.shape[0], kv_hbm.shape[1] // 2
    copies = []
    for (first, heads), count in zip(spans, PIECES):
        wide, height = heads * size, keys // count
        for number in range(count):
            ref = part_refs.pop(0)
            for half in range(2):
                start = half * width + first * size
                source = kv_hbm.at[number * height : (number + 1) * height, start : start + wide]
                target = ref.at[:, half * wide : (half + 1) * wide]
                copies.append(pltpu.make_async_copy(source, target, sems.at[len(copies)]))
    for copy in copies:
        copy.start()
    row = slot_row(owner_ref[...], columns, capacity)
    row_ref[...] = jnp.broadcast_to(row, row_ref.shape).astype(jnp.int32)
    for copy in copies:
        copy.wait()


def prepare(owner_row, kv, spans, size, columns, capacity):
    shapes = []
    for (_, heads), count in zip(spans, PIECES):
        shape = (kv.shape[0] // count, 2 * heads * size)
        shapes += [jax.ShapeDtypeStruct(shape, BF16)] * count
    row, *parts = pl.pallas_call(
        functools.partial(prepare_kernel, columns, capacity, spans, size),
        in_specs=whole() + [pl.BlockSpec(memory_space=pl.ANY)],
        out_specs=whole(1 + len(shapes)),
        out_shape=[jax.ShapeDtypeStruct((8, owner_row.shape[1]), jnp.int32)] + shapes,
        scratch_shapes=[pltpu.SemaphoreType.DMA((2 * len(shapes),))],
        compiler_params=params(KERNEL_MIB),
        cost_estimate=cost(SLOTS_COST * 1e9, 0),
        name="prepare",
    )(owner_row, kv)
    return row, [[parts.pop(0) for _ in range(count)] for count in PIECES]


def wait_kernel(*refs):
    refs[-1][...] = jnp.zeros_like(refs[-1])


def wait_for(arrays):
    return pl.pallas_call(
        wait_kernel,
        in_specs=unread(arrays),
        out_specs=whole()[0],
        out_shape=TOKEN,
        compiler_params=params(KERNEL_MIB),
        cost_estimate=cost(WAIT_COST * 1e9, 0),
        name="wait_for",
    )(*arrays)


def column_kernel(columns, capacity, owner_ref, *refs):
    column_ref, token_ref = refs[-2:]
    token_ref[...] = jnp.zeros_like(token_ref)
    row = slot_row(owner_ref[...], columns, capacity)
    column_ref[...] = jnp.broadcast_to(row, (BLK, row.shape[1])).T.astype(jnp.int32)


def slot_column(owner_row, columns, capacity, after):
    rows = owner_row.shape[1]
    return pl.pallas_call(
        functools.partial(column_kernel, columns, capacity),
        in_specs=whole() + unread(after),
        out_specs=whole(2),
        out_shape=[jax.ShapeDtypeStruct((rows, BLK), jnp.int32), TOKEN],
        compiler_params=params(KERNEL_MIB),
        cost_estimate=cost(WAIT_COST * 1e9, 4 * rows * BLK),
        name="slot_column",
    )(owner_row, *after)


def attend_kernel(size, heads, first, starts, behind, has_base, capacity, length_ref, *refs):
    refs = refs[behind:]
    rows_ref, refs = refs[0], refs[1:]
    count = len(starts)
    parts = []
    for _, _, _, pieces in starts:
        parts.append(refs[:pieces])
        refs = refs[pieces:]
    base_ref = refs[0] if has_base else None
    outs = 3 if capacity else 1
    out_refs, shown = refs[int(has_base) : int(has_base) + outs], refs[int(has_base) + outs]
    result = out_refs[0] if outs == 1 else refs[-1]
    me = lax.axis_index("cand")
    places = [lax.axis_index("user") ^ start[0] for start in starts]
    slots = rows_ref.shape[0]
    columns_of = slots // capacity if capacity else 1
    keys = sum(piece.shape[0] for piece in parts[0])
    blocks = keys // BLK
    seen = rows_ref[:, HEADS * size :].astype(F32)
    for number in range(count):
        for block in range(blocks):
            start = (places[number] * blocks + block).astype(F32)
            shown[number * blocks + block] = (start < seen).astype(F32).astype(BF16)
    row = lax.broadcasted_iota(jnp.int32, (keys, size), 0)
    tile = min(512, slots)

    def columns(start):
        return slice(start, start + size)

    def read(part, start):
        return jnp.concatenate([piece[:, columns(start)] for piece in part], axis=0)

    def one_head(head):
        values = []
        for number, part in enumerate(parts):
            inside = row + places[number] * keys < length_ref[0]
            value = read(part, (starts[number][2] + head) * size).astype(F32)
            values.append(jnp.where(inside, value, 0.0).astype(BF16))
        values = jnp.concatenate(values, axis=0)
        for start in range(0, slots, tile):
            span = slice(start, start + tile)
            queries = rows_ref[span, columns((first + head) * size)]
            weights = []
            for number, part in enumerate(parts):
                scores = lax.dot_general(
                    queries,
                    read(part, (starts[number][1] + head) * size),
                    (((1,), (1,)), ((), ())),
                    preferred_element_type=F32,
                )
                for block in range(blocks):
                    half = scores[:, block * BLK : (block + 1) * BLK] * (0.5 / math.sqrt(size))
                    half = half.astype(BF16) * shown[number * blocks + block, span, :]
                    weights.append(half * jnp.tanh(half) + half)
            total = jnp.dot(
                jnp.concatenate(weights, axis=1), values, preferred_element_type=F32
            )
            if has_base:
                total = total + base_ref[span, columns(head * size)]
            result[span, columns(head * size)] = total.astype(result.dtype)

    for head in range(heads):
        one_head(head)
    if outs > 1:
        numbers = list(range(0, columns_of, 2)) + list(range(1, columns_of, 2))
        for ref in out_refs:
            for start in range(0, ref.shape[0], capacity):
                block = me ^ numbers.pop(0)
                source = pl.ds(pl.multiple_of(block * capacity, capacity), capacity)
                ref[start : start + capacity, :] = result[source, :]


def attend(length, after, rows, segments, base, first, heads, size, capacity, dtype, share):
    slots = rows.shape[0]
    keys = sum(piece.shape[0] for piece in segments[0][1])
    count = len(segments)
    starts = [(place, key, value, len(pieces)) for place, pieces, key, value in segments]
    pieces = [piece for _, pieces, _, _ in segments for piece in pieces]
    heights = [slots // 2, slots // 4, slots // 4] if capacity else [slots]
    outs = len(heights)
    extra = [] if base is None else [base]
    scratch = [pltpu.VMEM((count * (keys // BLK), slots, BLK), BF16)]
    if outs > 1:
        scratch.append(pltpu.VMEM((slots, heads * size), BF16))
    return pl.pallas_call(
        functools.partial(
            attend_kernel, size, heads, first, starts, len(after), base is not None, capacity
        ),
        in_specs=[pl.BlockSpec(memory_space=pltpu.SMEM)]
        + unread(after)
        + whole(1 + len(pieces) + len(extra)),
        out_specs=whole(outs),
        out_shape=[jax.ShapeDtypeStruct((height, heads * size), dtype) for height in heights],
        scratch_shapes=scratch,
        compiler_params=params(KERNEL_MIB),
        cost_estimate=cost(
            share * 4 * slots * keys * count * heads * size,
            2 * (2 * slots + count * keys * 2) * heads * size,
            slots * keys * count * heads,
        ),
        name="attend",
    )(length, *after, rows, *pieces, *extra)


def placement(slot, slots):
    lane = lax.broadcasted_iota(jnp.int32, (1, BLK), 1)
    return jnp.concatenate(
        [(lane + start == slot).astype(BF16) for start in range(0, slots, BLK)], axis=1
    )


def in_slots(parts, capacity):
    return jnp.concatenate(
        [part[:capacity, :] for part in parts[:2]] + [part[...] for part in parts[2:]], axis=0
    )


def collect_kernel(capacity, slots, slot_ref, *refs):
    rows = in_slots(refs[:-1], capacity)
    place = placement(slot_ref[...], slots)
    refs[-1][...] = jnp.dot(place, rows, preferred_element_type=F32).astype(BF16)


def collect(slot, parts, capacity, slots):
    rows, width = slot.shape[0], parts[0].shape[1]
    return pl.pallas_call(
        functools.partial(collect_kernel, capacity, slots),
        in_specs=whole(1 + len(parts)),
        out_specs=whole()[0],
        out_shape=jax.ShapeDtypeStruct((rows, width), BF16),
        compiler_params=params(KERNEL_MIB),
        cost_estimate=cost(COLLECT_COST * 1e9, 2 * (rows + slots) * width),
        name="collect",
    )(slot, *parts)


def finish_kernel(groups, capacity, slots, slot_ref, gain_ref, gate_ref, x_ref, w_ref, *refs):
    early, parts, (out_hbm, out_ref, sems) = refs[:groups], refs[groups:-3], refs[-3:]
    rows = x_ref.shape[0]
    place = placement(slot_ref[...], slots)
    late = jnp.dot(place, in_slots(parts, capacity), preferred_element_type=F32)
    tile = rows // 2
    stores = []
    for half in range(2):
        span = slice(half * tile, (half + 1) * tile)
        attn = jnp.concatenate([part[span, :].astype(F32) for part in early] + [late[span, :]], axis=1)
        centered = attn - jnp.mean(attn, axis=1, keepdims=True)
        variance = jnp.mean(centered * centered, axis=1, keepdims=True)
        normed = (centered * lax.rsqrt(variance + norm_eps) * gain_ref[...]).astype(BF16)
        mixed = (normed.astype(F32) * gate_ref[span, :].astype(F32)).astype(BF16)
        projected = jnp.dot(mixed, w_ref[...], preferred_element_type=F32)
        out_ref[span, :] = (x_ref[span, :].astype(F32) + projected).astype(BF16)
        store = pltpu.make_async_copy(out_ref.at[span, :], out_hbm.at[span, :], sems.at[half])
        store.start()
        stores.append(store)
    for store in stores:
        store.wait()


def finish(slot, early, gate, cand_x, ln_gain, w_out, parts, capacity, slots):
    rows, width = cand_x.shape
    return pl.pallas_call(
        functools.partial(finish_kernel, len(early), capacity, slots),
        in_specs=whole(5 + len(early) + len(parts)),
        out_specs=pl.BlockSpec(memory_space=pl.ANY),
        out_shape=jax.ShapeDtypeStruct((rows, width), BF16),
        scratch_shapes=[pltpu.VMEM((rows, width), BF16), pltpu.SemaphoreType.DMA((2,))],
        compiler_params=params(KERNEL_MIB),
        cost_estimate=cost(
            2 * rows * width * (width + slots), 2 * (3 * rows * width + width * width + slots * width)
        ),
        name="finish",
    )(slot, ln_gain.reshape(1, width), gate, cand_x, w_out, *early, *parts)


def swap(array, axis, bits, count):
    return lax.ppermute(array, axis, [(i, i ^ bits) for i in range(count)])


def tied(arrays, behind):
    return lax.optimization_barrier((arrays, behind))[0]


def neighbours(pieces, count):
    back = []
    for piece in pieces:
        back.append(swap(tied(piece, back[-1]) if back else piece, "user", 1, count))
    return back


def exchange_cores(even, odds, capacity, count, behind):
    others = [swap(odd, "cand", 1, count) for odd in odds]
    if behind is not None:
        (even, others), _ = lax.optimization_barrier(((even, others), behind))
    pairs = []
    for d in range(1, count // 2):
        first, second = d * capacity, (d * capacity) % odds[0].shape[0]
        other = others[first // odds[0].shape[0]]
        pairs.append(
            jnp.concatenate(
                [even[first : first + capacity], other[second : second + capacity]], axis=0
            )
        )
    return [even, others[0]], pairs


def exchange_chips(pairs, count):
    return [swap(pair, "cand", 2 * d, count) for d, pair in enumerate(pairs, 1)]


def per_device(cand_x, cand_user, visible, hist_len, kv_cache, w_in, w_out, ln_gain):
    rows, width = cand_x.shape
    columns = lax.axis_size("cand")
    count = lax.axis_size("user")
    size = width // HEADS
    capacity = 2 * rows // columns
    slots = columns * capacity
    me = lax.axis_index("cand").astype(jnp.int32)
    owner_row = cand_user.reshape(1, rows)
    visible_row = visible.reshape(1, rows)
    spans = [(sum(GROUPS[:number]), heads) for number, heads in enumerate(GROUPS)]

    gate, gated = project_gate(cand_x, w_in)
    row, parts = prepare(owner_row, kv_cache[0], spans, size, columns, capacity)
    send = project_queries(row, visible_row, cand_x, w_in, slots)
    far = []
    for number, pieces in enumerate(parts):
        if far:
            pieces = tied(pieces, send)
        held = {0: pieces}
        bit = count // 2
        while bit > 1:
            for key in sorted(held):
                held[key | bit] = [swap(piece, "user", bit, count) for piece in held[key]]
            bit //= 2
        far.append(held)
    evens = sorted(far[0])
    near, passed = [], []
    for number, pieces in enumerate(parts):
        onward = [far[number][key] for key in evens[1:]]
        if number:
            pieces, onward = tied((pieces, onward), (onward, passed[-1]))
        passed.append([neighbours(held, count) for held in onward])
        near.append(neighbours(pieces, count))

    got = lax.all_to_all(
        send.reshape(columns, capacity, -1), "cand", split_axis=0, concat_axis=0, tiled=True
    ).reshape(slots, -1)
    arrived = [gated] + near[0]
    for held in far:
        for key in evens[1:]:
            arrived += held[key]
    slot, started = slot_column(owner_row ^ me, columns, capacity, arrived)
    early = []
    after = [started]
    behind = None
    for number, (first, heads) in enumerate(spans):
        held = far[number]
        close = (1, near[number], 0, heads)
        segments = [(key, held[key], 0, heads) for key in evens] + [close] * (number == 0)
        cuts = [(key | 1, cut, 0, heads) for key, cut in zip(evens[1:], passed[number])]
        cuts += [close] * (number > 0)
        base = attend(
            hist_len, after, got, segments, None, first, heads, size, None, F32, 0.0
        )[0]
        attn = attend(
            hist_len,
            [],
            got,
            cuts,
            base,
            first,
            heads,
            size,
            capacity,
            BF16,
            LATE_SHARE * (number > 0),
        )
        here, pairs = exchange_cores(attn[0], attn[1:], capacity, columns, behind)
        away = exchange_chips(pairs, columns)
        if number + 1 < len(spans):
            token = wait_for(
                [attn[0]] + [piece for key in evens[1:] for piece in far[number + 1][key]]
            )
            after = [token] + pairs
            early.append(collect(slot, here + away, capacity, slots))
            behind = early[-1]
    return finish(slot, early, gate, cand_x, ln_gain, w_out, here + away, capacity, slots)


def solution(mesh):
    in_specs = (
        P(("user", "cand"), None),
        P(("user", "cand"), None),
        P(("user", "cand")),
        P("cand"),
        P("cand", "user", None),
        P(),
        P(),
        P(),
    )
    out_specs = P(("user", "cand"), None)
    return jax.shard_map(
        per_device, mesh=mesh, in_specs=in_specs, out_specs=out_specs, check_vma=False
    )
```

```python
import functools
import math

import jax
import jax.numpy as jnp
from jax import lax
from jax.experimental import pallas as pl
from jax.experimental.pallas import tpu as pltpu
from jax.sharding import PartitionSpec as P

HEADS = 8
BLK = 128
GROUPS = (3, 3, 2)
norm_eps = 1e-06
F32 = jnp.float32
BF16 = jnp.bfloat16
MIB = 1024 * 1024
TOKEN = jax.ShapeDtypeStruct((8, BLK), jnp.int32)
WAIT_COST = 20.0
LATE_SHARE = 20.0
COLLECT_COST = 20.0
SLOTS_COST = 6.0
KERNEL_MIB = 24


def params(mib):
    return pltpu.CompilerParams(vmem_limit_bytes=mib * MIB)


def cost(flops, nbytes, transcendentals=0):
    return pl.CostEstimate(
        flops=int(flops), bytes_accessed=int(nbytes), transcendentals=int(transcendentals)
    )


def silu(v):
    half = 0.5 * v
    return half * jnp.tanh(half) + half


def earlier_mask(rows):
    first = lax.broadcasted_iota(jnp.int32, (rows, rows), 0)
    second = lax.broadcasted_iota(jnp.int32, (rows, rows), 1)
    return (first < second).astype(BF16)


def slot_row(owner_row, columns, capacity):
    rows = owner_row.shape[1]
    users = lax.broadcasted_iota(jnp.int32, (columns, rows), 0)
    mine = users == owner_row
    before = jnp.dot(mine.astype(BF16), earlier_mask(rows), preferred_element_type=F32)
    rank = jnp.sum(jnp.where(mine, before, 0.0), axis=0, keepdims=True)
    return owner_row.astype(F32) * capacity + rank


def whole(count=1):
    return [pl.BlockSpec(memory_space=pltpu.VMEM)] * count


def unread(arrays):
    return [pl.BlockSpec(memory_space=pl.ANY)] * len(arrays)


def query_kernel(slot_ref, visible_ref, x_ref, w_ref, send_ref):
    rows, width = x_ref.shape
    slots = send_ref.shape[0]
    index = lax.broadcasted_iota(jnp.int32, (slots, rows), 0)
    place = (index == slot_ref[:1, :]).astype(BF16)
    seen = jnp.broadcast_to(visible_ref[...].astype(F32), (BLK, rows)).T.astype(BF16)
    send_ref[:, width:] = jnp.dot(place, seen, preferred_element_type=F32).astype(BF16)
    tile = min(256, width)
    for start in range(0, width, tile):
        span = slice(start, start + tile)
        hidden = jnp.dot(x_ref[...], w_ref[:, span], preferred_element_type=F32)
        moved = jnp.dot(place, silu(hidden).astype(BF16), preferred_element_type=F32)
        send_ref[:, span] = moved.astype(BF16)


def project_queries(slot, visible_row, cand_x, w_in, slots):
    rows, width = cand_x.shape
    return pl.pallas_call(
        query_kernel,
        in_specs=whole(4),
        out_specs=whole()[0],
        out_shape=jax.ShapeDtypeStruct((slots, width + BLK), BF16),
        compiler_params=params(KERNEL_MIB),
        cost_estimate=cost(
            2 * rows * width * width + 2 * slots * rows * width,
            2 * (rows * width + width * width + slots * width),
            rows * width,
        ),
        name="project_queries",
    )(slot, visible_row, cand_x, w_in)


def gate_kernel(x_ref, w_ref, gate_ref, token_ref):
    token_ref[...] = jnp.zeros_like(token_ref)
    width = x_ref.shape[1]
    tile = min(256, width)
    for start in range(0, width, tile):
        columns = w_ref[:, width + start : width + start + tile]
        hidden = jnp.dot(x_ref[...], columns, preferred_element_type=F32)
        gate_ref[:, start : start + tile] = silu(hidden).astype(BF16)


def project_gate(cand_x, w_in):
    rows, width = cand_x.shape
    return pl.pallas_call(
        gate_kernel,
        in_specs=whole(2),
        out_specs=whole(2),
        out_shape=[jax.ShapeDtypeStruct((rows, width), BF16), TOKEN],
        compiler_params=params(KERNEL_MIB),
        cost_estimate=cost(
            2 * rows * width * width, 2 * (2 * rows * width + width * width), rows * width
        ),
        name="project_gate",
    )(cand_x, w_in)


def prepare_kernel(columns, capacity, spans, size, owner_ref, kv_hbm, row_ref, *refs):
    part_refs, sems = refs[:-1], refs[-1]
    width = kv_hbm.shape[1] // 2
    copies = []
    for (first, heads), ref in zip(spans, part_refs):
        wide = heads * size
        for start in (0, width):
            source = kv_hbm.at[:, start + first * size : start + first * size + wide]
            target = ref.at[:, wide * (start > 0) : wide * (start > 0) + wide]
            copies.append(pltpu.make_async_copy(source, target, sems.at[len(copies)]))
    for copy in copies:
        copy.start()
    row = slot_row(owner_ref[...], columns, capacity)
    row_ref[...] = jnp.broadcast_to(row, row_ref.shape).astype(jnp.int32)
    for copy in copies:
        copy.wait()


def prepare(owner_row, kv, spans, size, columns, capacity):
    rows = kv.shape[0]
    return pl.pallas_call(
        functools.partial(prepare_kernel, columns, capacity, spans, size),
        in_specs=whole() + [pl.BlockSpec(memory_space=pl.ANY)],
        out_specs=whole(1 + len(spans)),
        out_shape=[jax.ShapeDtypeStruct((8, owner_row.shape[1]), jnp.int32)]
        + [jax.ShapeDtypeStruct((rows, 2 * heads * size), BF16) for _, heads in spans],
        scratch_shapes=[pltpu.SemaphoreType.DMA((2 * len(spans),))],
        compiler_params=params(KERNEL_MIB),
        cost_estimate=cost(SLOTS_COST * 1e9, 0),
        name="prepare",
    )(owner_row, kv)


def wait_kernel(*refs):
    refs[-1][...] = jnp.zeros_like(refs[-1])


def wait_for(arrays):
    return pl.pallas_call(
        wait_kernel,
        in_specs=unread(arrays),
        out_specs=whole()[0],
        out_shape=TOKEN,
        compiler_params=params(KERNEL_MIB),
        cost_estimate=cost(WAIT_COST * 1e9, 0),
        name="wait_for",
    )(*arrays)


def column_kernel(columns, capacity, owner_ref, *refs):
    column_ref, token_ref = refs[-2:]
    token_ref[...] = jnp.zeros_like(token_ref)
    row = slot_row(owner_ref[...], columns, capacity)
    column_ref[...] = jnp.broadcast_to(row, (BLK, row.shape[1])).T.astype(jnp.int32)


def slot_column(owner_row, columns, capacity, after):
    rows = owner_row.shape[1]
    return pl.pallas_call(
        functools.partial(column_kernel, columns, capacity),
        in_specs=whole() + unread(after),
        out_specs=whole(2),
        out_shape=[jax.ShapeDtypeStruct((rows, BLK), jnp.int32), TOKEN],
        compiler_params=params(KERNEL_MIB),
        cost_estimate=cost(WAIT_COST * 1e9, 4 * rows * BLK),
        name="slot_column",
    )(owner_row, *after)


def attend_kernel(size, heads, first, starts, behind, has_base, capacity, length_ref, *refs):
    refs = refs[behind:]
    rows_ref, refs = refs[0], refs[1:]
    count = len(starts)
    parts = []
    for _, _, _, pieces in starts:
        parts.append(refs[:pieces])
        refs = refs[pieces:]
    base_ref = refs[0] if has_base else None
    outs = 3 if capacity else 1
    out_refs, shown = refs[int(has_base) : int(has_base) + outs], refs[int(has_base) + outs]
    result = out_refs[0] if outs == 1 else refs[-1]
    me = lax.axis_index("cand")
    places = [lax.axis_index("user") ^ start[0] for start in starts]
    slots = rows_ref.shape[0]
    columns_of = slots // capacity if capacity else 1
    keys = sum(piece.shape[0] for piece in parts[0])
    blocks = keys // BLK
    seen = rows_ref[:, HEADS * size :].astype(F32)
    for number in range(count):
        for block in range(blocks):
            start = (places[number] * blocks + block).astype(F32)
            shown[number * blocks + block] = (start < seen).astype(F32).astype(BF16)
    row = lax.broadcasted_iota(jnp.int32, (keys, size), 0)
    tile = min(512, slots)

    def columns(start):
        return slice(start, start + size)

    def read(part, start):
        return jnp.concatenate([piece[:, columns(start)] for piece in part], axis=0)

    def one_head(head):
        values = []
        for number, part in enumerate(parts):
            inside = row + places[number] * keys < length_ref[0]
            value = read(part, (starts[number][2] + head) * size).astype(F32)
            values.append(jnp.where(inside, value, 0.0).astype(BF16))
        values = jnp.concatenate(values, axis=0)
        for start in range(0, slots, tile):
            span = slice(start, start + tile)
            queries = rows_ref[span, columns((first + head) * size)]
            weights = []
            for number, part in enumerate(parts):
                scores = lax.dot_general(
                    queries,
                    read(part, (starts[number][1] + head) * size),
                    (((1,), (1,)), ((), ())),
                    preferred_element_type=F32,
                )
                for block in range(blocks):
                    half = scores[:, block * BLK : (block + 1) * BLK] * (0.5 / math.sqrt(size))
                    half = half.astype(BF16) * shown[number * blocks + block, span, :]
                    weights.append(half * jnp.tanh(half) + half)
            total = jnp.dot(
                jnp.concatenate(weights, axis=1), values, preferred_element_type=F32
            )
            if has_base:
                total = total + base_ref[span, columns(head * size)]
            result[span, columns(head * size)] = total.astype(result.dtype)

    for head in range(heads):
        one_head(head)
    if outs > 1:
        numbers = list(range(0, columns_of, 2)) + list(range(1, columns_of, 2))
        for ref in out_refs:
            for start in range(0, ref.shape[0], capacity):
                block = me ^ numbers.pop(0)
                source = pl.ds(pl.multiple_of(block * capacity, capacity), capacity)
                ref[start : start + capacity, :] = result[source, :]


def attend(length, after, rows, segments, base, first, heads, size, capacity, dtype, share):
    slots = rows.shape[0]
    keys = sum(piece.shape[0] for piece in segments[0][1])
    count = len(segments)
    starts = [(place, key, value, len(pieces)) for place, pieces, key, value in segments]
    pieces = [piece for _, pieces, _, _ in segments for piece in pieces]
    heights = [slots // 2, slots // 4, slots // 4] if capacity else [slots]
    outs = len(heights)
    extra = [] if base is None else [base]
    scratch = [pltpu.VMEM((count * (keys // BLK), slots, BLK), BF16)]
    if outs > 1:
        scratch.append(pltpu.VMEM((slots, heads * size), BF16))
    return pl.pallas_call(
        functools.partial(
            attend_kernel, size, heads, first, starts, len(after), base is not None, capacity
        ),
        in_specs=[pl.BlockSpec(memory_space=pltpu.SMEM)]
        + unread(after)
        + whole(1 + len(pieces) + len(extra)),
        out_specs=whole(outs),
        out_shape=[jax.ShapeDtypeStruct((height, heads * size), dtype) for height in heights],
        scratch_shapes=scratch,
        compiler_params=params(KERNEL_MIB),
        cost_estimate=cost(
            share * 4 * slots * keys * count * heads * size,
            2 * (2 * slots + count * keys * 2) * heads * size,
            slots * keys * count * heads,
        ),
        name="attend",
    )(length, *after, rows, *pieces, *extra)


def placement(slot, slots):
    lane = lax.broadcasted_iota(jnp.int32, (1, BLK), 1)
    return jnp.concatenate(
        [(lane + start == slot).astype(BF16) for start in range(0, slots, BLK)], axis=1
    )


def in_slots(parts, capacity):
    return jnp.concatenate(
        [part[:capacity, :] for part in parts[:2]] + [part[...] for part in parts[2:]], axis=0
    )


def collect_kernel(capacity, slots, slot_ref, *refs):
    rows = in_slots(refs[:-1], capacity)
    place = placement(slot_ref[...], slots)
    refs[-1][...] = jnp.dot(place, rows, preferred_element_type=F32).astype(BF16)


def collect(slot, parts, capacity, slots):
    rows, width = slot.shape[0], parts[0].shape[1]
    return pl.pallas_call(
        functools.partial(collect_kernel, capacity, slots),
        in_specs=whole(1 + len(parts)),
        out_specs=whole()[0],
        out_shape=jax.ShapeDtypeStruct((rows, width), BF16),
        compiler_params=params(KERNEL_MIB),
        cost_estimate=cost(COLLECT_COST * 1e9, 2 * (rows + slots) * width),
        name="collect",
    )(slot, *parts)


def finish_kernel(groups, capacity, slots, slot_ref, gain_ref, gate_ref, x_ref, w_ref, *refs):
    early, parts, (out_hbm, out_ref, sems) = refs[:groups], refs[groups:-3], refs[-3:]
    rows = x_ref.shape[0]
    place = placement(slot_ref[...], slots)
    late = jnp.dot(place, in_slots(parts, capacity), preferred_element_type=F32)
    tile = rows // 2
    stores = []
    for half in range(2):
        span = slice(half * tile, (half + 1) * tile)
        attn = jnp.concatenate([part[span, :].astype(F32) for part in early] + [late[span, :]], axis=1)
        centered = attn - jnp.mean(attn, axis=1, keepdims=True)
        variance = jnp.mean(centered * centered, axis=1, keepdims=True)
        normed = (centered * lax.rsqrt(variance + norm_eps) * gain_ref[...]).astype(BF16)
        mixed = (normed.astype(F32) * gate_ref[span, :].astype(F32)).astype(BF16)
        projected = jnp.dot(mixed, w_ref[...], preferred_element_type=F32)
        out_ref[span, :] = (x_ref[span, :].astype(F32) + projected).astype(BF16)
        store = pltpu.make_async_copy(out_ref.at[span, :], out_hbm.at[span, :], sems.at[half])
        store.start()
        stores.append(store)
    for store in stores:
        store.wait()


def finish(slot, early, gate, cand_x, ln_gain, w_out, parts, capacity, slots):
    rows, width = cand_x.shape
    return pl.pallas_call(
        functools.partial(finish_kernel, len(early), capacity, slots),
        in_specs=whole(5 + len(early) + len(parts)),
        out_specs=pl.BlockSpec(memory_space=pl.ANY),
        out_shape=jax.ShapeDtypeStruct((rows, width), BF16),
        scratch_shapes=[pltpu.VMEM((rows, width), BF16), pltpu.SemaphoreType.DMA((2,))],
        compiler_params=params(KERNEL_MIB),
        cost_estimate=cost(
            2 * rows * width * (width + slots), 2 * (3 * rows * width + width * width + slots * width)
        ),
        name="finish",
    )(slot, ln_gain.reshape(1, width), gate, cand_x, w_out, *early, *parts)


def swap(array, axis, bits, count):
    return lax.ppermute(array, axis, [(i, i ^ bits) for i in range(count)])


def exchange_cores(even, odds, capacity, count, behind):
    others = [swap(odd, "cand", 1, count) for odd in odds]
    if behind is not None:
        (even, others), _ = lax.optimization_barrier(((even, others), behind))
    pairs = []
    for d in range(1, count // 2):
        first, second = d * capacity, (d * capacity) % odds[0].shape[0]
        other = others[first // odds[0].shape[0]]
        pairs.append(
            jnp.concatenate(
                [even[first : first + capacity], other[second : second + capacity]], axis=0
            )
        )
    return [even, others[0]], pairs


def exchange_chips(pairs, count):
    return [swap(pair, "cand", 2 * d, count) for d, pair in enumerate(pairs, 1)]


def per_device(cand_x, cand_user, visible, hist_len, kv_cache, w_in, w_out, ln_gain):
    rows, width = cand_x.shape
    columns = lax.axis_size("cand")
    count = lax.axis_size("user")
    size = width // HEADS
    capacity = 2 * rows // columns
    slots = columns * capacity
    me = lax.axis_index("cand").astype(jnp.int32)
    owner_row = cand_user.reshape(1, rows)
    visible_row = visible.reshape(1, rows)
    spans = [(sum(GROUPS[:number]), heads) for number, heads in enumerate(GROUPS)]

    gate, gated = project_gate(cand_x, w_in)
    row, *parts = prepare(owner_row, kv_cache[0], spans, size, columns, capacity)
    send = project_queries(row, visible_row, cand_x, w_in, slots)
    near = None
    far = []
    for part in parts:
        if far:
            part, _ = lax.optimization_barrier((part, send))
        held = {0: part}
        bit = count // 2
        while bit > 1:
            for key in sorted(held):
                held[key | bit] = swap(held[key], "user", bit, count)
            bit //= 2
        if near is None:
            own, _ = lax.optimization_barrier((kv_cache[0], row))
            near = swap(own, "user", 1, count)
        far.append(held)
    evens = sorted(far[0])

    got = lax.all_to_all(
        send.reshape(columns, capacity, -1), "cand", split_axis=0, concat_axis=0, tiled=True
    ).reshape(slots, -1)
    arrived = [gated, near] + [held[key] for held in far for key in evens[1:]]
    slot, started = slot_column(owner_row ^ me, columns, capacity, arrived)
    early = []
    bases = []
    after = [started]
    behind = None
    for number, (first, heads) in enumerate(spans):
        held = far[number]
        passed = [held[key] for key in evens[1:]]
        if number > 1:
            passed, _ = lax.optimization_barrier((passed, bases[0]))
        passed = [[swap(part, "user", 1, count)] for part in passed]
        cuts = [(key | 1, cut, 0, heads) for key, cut in zip(evens[1:], passed)]
        segments = [(key, [held[key]], 0, heads) for key in evens]
        segments.append((1, [near], first, HEADS + first))
        base = attend(
            hist_len, after, got, segments, None, first, heads, size, None, F32, 0.0
        )[0]
        bases.append(base)
        attn = attend(
            hist_len,
            [],
            got,
            cuts,
            base,
            first,
            heads,
            size,
            capacity,
            BF16,
            LATE_SHARE * (number > 0),
        )
        here, pairs = exchange_cores(attn[0], attn[1:], capacity, columns, behind)
        away = exchange_chips(pairs, columns)
        if number + 1 < len(spans):
            token = wait_for([attn[0]] + [far[number + 1][key] for key in evens[1:]])
            after = [token] + pairs
            early.append(collect(slot, here + away, capacity, slots))
            behind = early[-1]
    return finish(slot, early, gate, cand_x, ln_gain, w_out, here + away, capacity, slots)


def solution(mesh):
    in_specs = (
        P(("user", "cand"), None),
        P(("user", "cand"), None),
        P(("user", "cand")),
        P("cand"),
        P("cand", "user", None),
        P(),
        P(),
        P(),
    )
    out_specs = P(("user", "cand"), None)
    return jax.shard_map(
        per_device, mesh=mesh, in_specs=in_specs, out_specs=out_specs, check_vma=False
    )
```

```python
import functools
import math

import jax
import jax.numpy as jnp
from jax import lax
from jax.experimental import pallas as pl
from jax.experimental.pallas import tpu as pltpu
from jax.sharding import PartitionSpec as P

HEADS = 8
BLK = 128
GROUPS = (4, 4)
norm_eps = 1e-06
F32 = jnp.float32
BF16 = jnp.bfloat16
MIB = 1024 * 1024
TOKEN = jax.ShapeDtypeStruct((8, BLK), jnp.int32)
WAIT_COST = 20.0
LATE_SHARE = 20.0
COLLECT_COST = 20.0
SLOTS_COST = 6.0
KERNEL_MIB = 24


def params(mib):
    return pltpu.CompilerParams(vmem_limit_bytes=mib * MIB)


def cost(flops, nbytes, transcendentals=0):
    return pl.CostEstimate(
        flops=int(flops), bytes_accessed=int(nbytes), transcendentals=int(transcendentals)
    )


def silu(v):
    half = 0.5 * v
    return half * jnp.tanh(half) + half


def earlier_mask(rows):
    first = lax.broadcasted_iota(jnp.int32, (rows, rows), 0)
    second = lax.broadcasted_iota(jnp.int32, (rows, rows), 1)
    return (first < second).astype(BF16)


def slot_row(owner_row, columns, capacity):
    rows = owner_row.shape[1]
    users = lax.broadcasted_iota(jnp.int32, (columns, rows), 0)
    mine = users == owner_row
    before = jnp.dot(mine.astype(BF16), earlier_mask(rows), preferred_element_type=F32)
    rank = jnp.sum(jnp.where(mine, before, 0.0), axis=0, keepdims=True)
    return owner_row.astype(F32) * capacity + rank


def whole(count=1):
    return [pl.BlockSpec(memory_space=pltpu.VMEM)] * count


def unread(arrays):
    return [pl.BlockSpec(memory_space=pl.ANY)] * len(arrays)


def query_kernel(slot_ref, visible_ref, x_ref, w_ref, send_ref):
    rows, width = x_ref.shape
    slots = send_ref.shape[0]
    index = lax.broadcasted_iota(jnp.int32, (slots, rows), 0)
    place = (index == slot_ref[:1, :]).astype(BF16)
    seen = jnp.broadcast_to(visible_ref[...].astype(F32), (BLK, rows)).T.astype(BF16)
    send_ref[:, width:] = jnp.dot(place, seen, preferred_element_type=F32).astype(BF16)
    tile = min(256, width)
    for start in range(0, width, tile):
        span = slice(start, start + tile)
        hidden = jnp.dot(x_ref[...], w_ref[:, span], preferred_element_type=F32)
        moved = jnp.dot(place, silu(hidden).astype(BF16), preferred_element_type=F32)
        send_ref[:, span] = moved.astype(BF16)


def project_queries(slot, visible_row, cand_x, w_in, slots):
    rows, width = cand_x.shape
    return pl.pallas_call(
        query_kernel,
        in_specs=whole(4),
        out_specs=whole()[0],
        out_shape=jax.ShapeDtypeStruct((slots, width + BLK), BF16),
        compiler_params=params(KERNEL_MIB),
        cost_estimate=cost(
            2 * rows * width * width + 2 * slots * rows * width,
            2 * (rows * width + width * width + slots * width),
            rows * width,
        ),
        name="project_queries",
    )(slot, visible_row, cand_x, w_in)


def gate_kernel(x_ref, w_ref, gate_ref, token_ref):
    token_ref[...] = jnp.zeros_like(token_ref)
    width = x_ref.shape[1]
    tile = min(256, width)
    for start in range(0, width, tile):
        columns = w_ref[:, width + start : width + start + tile]
        hidden = jnp.dot(x_ref[...], columns, preferred_element_type=F32)
        gate_ref[:, start : start + tile] = silu(hidden).astype(BF16)


def project_gate(cand_x, w_in):
    rows, width = cand_x.shape
    return pl.pallas_call(
        gate_kernel,
        in_specs=whole(2),
        out_specs=whole(2),
        out_shape=[jax.ShapeDtypeStruct((rows, width), BF16), TOKEN],
        compiler_params=params(KERNEL_MIB),
        cost_estimate=cost(
            2 * rows * width * width, 2 * (2 * rows * width + width * width), rows * width
        ),
        name="project_gate",
    )(cand_x, w_in)


def prepare_kernel(columns, capacity, spans, size, owner_ref, kv_hbm, row_ref, *refs):
    part_refs, sems = refs[:-1], refs[-1]
    width = kv_hbm.shape[1] // 2
    copies = []
    for (first, heads), ref in zip(spans, part_refs):
        wide = heads * size
        for start in (0, width):
            source = kv_hbm.at[:, start + first * size : start + first * size + wide]
            target = ref.at[:, wide * (start > 0) : wide * (start > 0) + wide]
            copies.append(pltpu.make_async_copy(source, target, sems.at[len(copies)]))
    for copy in copies:
        copy.start()
    row = slot_row(owner_ref[...], columns, capacity)
    row_ref[...] = jnp.broadcast_to(row, row_ref.shape).astype(jnp.int32)
    for copy in copies:
        copy.wait()


def prepare(owner_row, kv, spans, size, columns, capacity):
    rows = kv.shape[0]
    return pl.pallas_call(
        functools.partial(prepare_kernel, columns, capacity, spans, size),
        in_specs=whole() + [pl.BlockSpec(memory_space=pl.ANY)],
        out_specs=whole(1 + len(spans)),
        out_shape=[jax.ShapeDtypeStruct((8, owner_row.shape[1]), jnp.int32)]
        + [jax.ShapeDtypeStruct((rows, 2 * heads * size), BF16) for _, heads in spans],
        scratch_shapes=[pltpu.SemaphoreType.DMA((2 * len(spans),))],
        compiler_params=params(KERNEL_MIB),
        cost_estimate=cost(SLOTS_COST * 1e9, 0),
        name="prepare",
    )(owner_row, kv)


def wait_kernel(*refs):
    refs[-1][...] = jnp.zeros_like(refs[-1])


def wait_for(arrays):
    return pl.pallas_call(
        wait_kernel,
        in_specs=unread(arrays),
        out_specs=whole()[0],
        out_shape=TOKEN,
        compiler_params=params(KERNEL_MIB),
        cost_estimate=cost(WAIT_COST * 1e9, 0),
        name="wait_for",
    )(*arrays)


def column_kernel(columns, capacity, owner_ref, *refs):
    column_ref, token_ref = refs[-2:]
    token_ref[...] = jnp.zeros_like(token_ref)
    row = slot_row(owner_ref[...], columns, capacity)
    column_ref[...] = jnp.broadcast_to(row, (BLK, row.shape[1])).T.astype(jnp.int32)


def slot_column(owner_row, columns, capacity, after):
    rows = owner_row.shape[1]
    return pl.pallas_call(
        functools.partial(column_kernel, columns, capacity),
        in_specs=whole() + unread(after),
        out_specs=whole(2),
        out_shape=[jax.ShapeDtypeStruct((rows, BLK), jnp.int32), TOKEN],
        compiler_params=params(KERNEL_MIB),
        cost_estimate=cost(WAIT_COST * 1e9, 4 * rows * BLK),
        name="slot_column",
    )(owner_row, *after)


def attend_kernel(size, heads, first, starts, behind, has_base, capacity, length_ref, *refs):
    refs = refs[behind:]
    rows_ref, refs = refs[0], refs[1:]
    count = len(starts)
    parts = []
    for _, _, _, pieces in starts:
        parts.append(refs[:pieces])
        refs = refs[pieces:]
    base_ref = refs[0] if has_base else None
    outs = 3 if capacity else 1
    out_refs, shown = refs[int(has_base) : int(has_base) + outs], refs[int(has_base) + outs]
    result = out_refs[0] if outs == 1 else refs[-1]
    me = lax.axis_index("cand")
    places = [lax.axis_index("user") ^ start[0] for start in starts]
    slots = rows_ref.shape[0]
    columns_of = slots // capacity if capacity else 1
    keys = sum(piece.shape[0] for piece in parts[0])
    blocks = keys // BLK
    seen = rows_ref[:, HEADS * size :].astype(F32)
    for number in range(count):
        for block in range(blocks):
            start = (places[number] * blocks + block).astype(F32)
            shown[number * blocks + block] = (start < seen).astype(F32).astype(BF16)
    row = lax.broadcasted_iota(jnp.int32, (keys, size), 0)
    tile = min(512, slots)

    def columns(start):
        return slice(start, start + size)

    def read(part, start):
        return jnp.concatenate([piece[:, columns(start)] for piece in part], axis=0)

    def one_head(head):
        values = []
        for number, part in enumerate(parts):
            inside = row + places[number] * keys < length_ref[0]
            value = read(part, (starts[number][2] + head) * size).astype(F32)
            values.append(jnp.where(inside, value, 0.0).astype(BF16))
        values = jnp.concatenate(values, axis=0)
        for start in range(0, slots, tile):
            span = slice(start, start + tile)
            queries = rows_ref[span, columns((first + head) * size)]
            weights = []
            for number, part in enumerate(parts):
                scores = lax.dot_general(
                    queries,
                    read(part, (starts[number][1] + head) * size),
                    (((1,), (1,)), ((), ())),
                    preferred_element_type=F32,
                )
                for block in range(blocks):
                    half = scores[:, block * BLK : (block + 1) * BLK] * (0.5 / math.sqrt(size))
                    half = half.astype(BF16) * shown[number * blocks + block, span, :]
                    weights.append(half * jnp.tanh(half) + half)
            total = jnp.dot(
                jnp.concatenate(weights, axis=1), values, preferred_element_type=F32
            )
            if has_base:
                total = total + base_ref[span, columns(head * size)]
            result[span, columns(head * size)] = total.astype(result.dtype)

    for head in range(heads):
        one_head(head)
    if outs > 1:
        numbers = list(range(0, columns_of, 2)) + list(range(1, columns_of, 2))
        for ref in out_refs:
            for start in range(0, ref.shape[0], capacity):
                block = me ^ numbers.pop(0)
                source = pl.ds(pl.multiple_of(block * capacity, capacity), capacity)
                ref[start : start + capacity, :] = result[source, :]


def attend(length, after, rows, segments, base, first, heads, size, capacity, dtype, share):
    slots = rows.shape[0]
    keys = sum(piece.shape[0] for piece in segments[0][1])
    count = len(segments)
    starts = [(place, key, value, len(pieces)) for place, pieces, key, value in segments]
    pieces = [piece for _, pieces, _, _ in segments for piece in pieces]
    heights = [slots // 2, slots // 4, slots // 4] if capacity else [slots]
    outs = len(heights)
    extra = [] if base is None else [base]
    scratch = [pltpu.VMEM((count * (keys // BLK), slots, BLK), BF16)]
    if outs > 1:
        scratch.append(pltpu.VMEM((slots, heads * size), BF16))
    return pl.pallas_call(
        functools.partial(
            attend_kernel, size, heads, first, starts, len(after), base is not None, capacity
        ),
        in_specs=[pl.BlockSpec(memory_space=pltpu.SMEM)]
        + unread(after)
        + whole(1 + len(pieces) + len(extra)),
        out_specs=whole(outs),
        out_shape=[jax.ShapeDtypeStruct((height, heads * size), dtype) for height in heights],
        scratch_shapes=scratch,
        compiler_params=params(KERNEL_MIB),
        cost_estimate=cost(
            share * 4 * slots * keys * count * heads * size,
            2 * (2 * slots + count * keys * 2) * heads * size,
            slots * keys * count * heads,
        ),
        name="attend",
    )(length, *after, rows, *pieces, *extra)


def placement(slot, slots):
    lane = lax.broadcasted_iota(jnp.int32, (1, BLK), 1)
    return jnp.concatenate(
        [(lane + start == slot).astype(BF16) for start in range(0, slots, BLK)], axis=1
    )


def in_slots(parts, capacity):
    return jnp.concatenate(
        [part[:capacity, :] for part in parts[:2]] + [part[...] for part in parts[2:]], axis=0
    )


def collect_kernel(capacity, slots, slot_ref, *refs):
    rows = in_slots(refs[:-1], capacity)
    place = placement(slot_ref[...], slots)
    refs[-1][...] = jnp.dot(place, rows, preferred_element_type=F32).astype(BF16)


def collect(slot, parts, capacity, slots):
    rows, width = slot.shape[0], parts[0].shape[1]
    return pl.pallas_call(
        functools.partial(collect_kernel, capacity, slots),
        in_specs=whole(1 + len(parts)),
        out_specs=whole()[0],
        out_shape=jax.ShapeDtypeStruct((rows, width), BF16),
        compiler_params=params(KERNEL_MIB),
        cost_estimate=cost(COLLECT_COST * 1e9, 2 * (rows + slots) * width),
        name="collect",
    )(slot, *parts)


def finish_kernel(groups, capacity, slots, slot_ref, gain_ref, gate_ref, x_ref, w_ref, *refs):
    early, parts, (out_hbm, out_ref, sems) = refs[:groups], refs[groups:-3], refs[-3:]
    rows = x_ref.shape[0]
    place = placement(slot_ref[...], slots)
    late = jnp.dot(place, in_slots(parts, capacity), preferred_element_type=F32)
    tile = rows // 2
    stores = []
    for half in range(2):
        span = slice(half * tile, (half + 1) * tile)
        attn = jnp.concatenate([part[span, :].astype(F32) for part in early] + [late[span, :]], axis=1)
        centered = attn - jnp.mean(attn, axis=1, keepdims=True)
        variance = jnp.mean(centered * centered, axis=1, keepdims=True)
        normed = (centered * lax.rsqrt(variance + norm_eps) * gain_ref[...]).astype(BF16)
        mixed = (normed.astype(F32) * gate_ref[span, :].astype(F32)).astype(BF16)
        projected = jnp.dot(mixed, w_ref[...], preferred_element_type=F32)
        out_ref[span, :] = (x_ref[span, :].astype(F32) + projected).astype(BF16)
        store = pltpu.make_async_copy(out_ref.at[span, :], out_hbm.at[span, :], sems.at[half])
        store.start()
        stores.append(store)
    for store in stores:
        store.wait()


def finish(slot, early, gate, cand_x, ln_gain, w_out, parts, capacity, slots):
    rows, width = cand_x.shape
    return pl.pallas_call(
        functools.partial(finish_kernel, len(early), capacity, slots),
        in_specs=whole(5 + len(early) + len(parts)),
        out_specs=pl.BlockSpec(memory_space=pl.ANY),
        out_shape=jax.ShapeDtypeStruct((rows, width), BF16),
        scratch_shapes=[pltpu.VMEM((rows, width), BF16), pltpu.SemaphoreType.DMA((2,))],
        compiler_params=params(KERNEL_MIB),
        cost_estimate=cost(
            2 * rows * width * (width + slots), 2 * (3 * rows * width + width * width + slots * width)
        ),
        name="finish",
    )(slot, ln_gain.reshape(1, width), gate, cand_x, w_out, *early, *parts)


def swap(array, axis, bits, count):
    return lax.ppermute(array, axis, [(i, i ^ bits) for i in range(count)])


def exchange_cores(even, odds, capacity, count, behind):
    others = [swap(odd, "cand", 1, count) for odd in odds]
    if behind is not None:
        (even, others), _ = lax.optimization_barrier(((even, others), behind))
    pairs = []
    for d in range(1, count // 2):
        first, second = d * capacity, (d * capacity) % odds[0].shape[0]
        other = others[first // odds[0].shape[0]]
        pairs.append(
            jnp.concatenate(
                [even[first : first + capacity], other[second : second + capacity]], axis=0
            )
        )
    return [even, others[0]], pairs


def exchange_chips(pairs, count):
    return [swap(pair, "cand", 2 * d, count) for d, pair in enumerate(pairs, 1)]


def per_device(cand_x, cand_user, visible, hist_len, kv_cache, w_in, w_out, ln_gain):
    rows, width = cand_x.shape
    columns = lax.axis_size("cand")
    count = lax.axis_size("user")
    size = width // HEADS
    capacity = 2 * rows // columns
    slots = columns * capacity
    me = lax.axis_index("cand").astype(jnp.int32)
    owner_row = cand_user.reshape(1, rows)
    visible_row = visible.reshape(1, rows)
    spans = [(sum(GROUPS[:number]), heads) for number, heads in enumerate(GROUPS)]

    gate, gated = project_gate(cand_x, w_in)
    row, *parts = prepare(owner_row, kv_cache[0], spans, size, columns, capacity)
    send = project_queries(row, visible_row, cand_x, w_in, slots)
    near = []
    far = []
    for part in parts:
        if far:
            part, _ = lax.optimization_barrier((part, send))
        held = {0: part}
        bit = count // 2
        while bit > 1:
            for key in sorted(held):
                held[key | bit] = swap(held[key], "user", bit, count)
            bit //= 2
        near.append(swap(part, "user", 1, count))
        far.append(held)
    evens = sorted(far[0])

    got = lax.all_to_all(
        send.reshape(columns, capacity, -1), "cand", split_axis=0, concat_axis=0, tiled=True
    ).reshape(slots, -1)
    arrived = [gated] + near + [held[key] for held in far for key in evens[1:]]
    slot, started = slot_column(owner_row ^ me, columns, capacity, arrived)
    early = []
    after = [started]
    behind = None
    for number, (first, heads) in enumerate(spans):
        held = far[number]
        cuts = [(key | 1, [swap(held[key], "user", 1, count)], 0, heads) for key in evens[1:]]
        segments = [(key, [held[key]], 0, heads) for key in evens]
        segments.append((1, [near[number]], 0, heads))
        base = attend(
            hist_len, after, got, segments, None, first, heads, size, None, F32, 0.0
        )[0]
        attn = attend(
            hist_len,
            [],
            got,
            cuts,
            base,
            first,
            heads,
            size,
            capacity,
            BF16,
            LATE_SHARE * (number > 0),
        )
        here, pairs = exchange_cores(attn[0], attn[1:], capacity, columns, behind)
        away = exchange_chips(pairs, columns)
        if number + 1 < len(spans):
            token = wait_for([attn[0]] + [far[number + 1][key] for key in evens[1:]])
            after = [token] + pairs
            early.append(collect(slot, here + away, capacity, slots))
            behind = early[-1]
    return finish(slot, early, gate, cand_x, ln_gain, w_out, here + away, capacity, slots)


def solution(mesh):
    in_specs = (
        P(("user", "cand"), None),
        P(("user", "cand"), None),
        P(("user", "cand")),
        P("cand"),
        P("cand", "user", None),
        P(),
        P(),
        P(),
    )
    out_specs = P(("user", "cand"), None)
    return jax.shard_map(
        per_device, mesh=mesh, in_specs=in_specs, out_specs=out_specs, check_vma=False
    )
```

```python
import functools
import math

import jax
import jax.numpy as jnp
from jax import lax
from jax.experimental import pallas as pl
from jax.experimental.pallas import tpu as pltpu
from jax.sharding import PartitionSpec as P

HEADS = 8
BLK = 128
GROUPS = (4, 4)
norm_eps = 1e-06
F32 = jnp.float32
BF16 = jnp.bfloat16
MIB = 1024 * 1024
TOKEN = jax.ShapeDtypeStruct((8, BLK), jnp.int32)
WAIT_COST = 20.0
LATE_SHARE = 20.0
SLOTS_COST = 6.0
KERNEL_MIB = 24


def params(mib):
    return pltpu.CompilerParams(vmem_limit_bytes=mib * MIB)


def cost(flops, nbytes, transcendentals=0):
    return pl.CostEstimate(
        flops=int(flops), bytes_accessed=int(nbytes), transcendentals=int(transcendentals)
    )


def silu(v):
    half = 0.5 * v
    return half * jnp.tanh(half) + half


def earlier_mask(rows):
    first = lax.broadcasted_iota(jnp.int32, (rows, rows), 0)
    second = lax.broadcasted_iota(jnp.int32, (rows, rows), 1)
    return (first < second).astype(BF16)


def slot_row(owner_row, columns, capacity):
    rows = owner_row.shape[1]
    users = lax.broadcasted_iota(jnp.int32, (columns, rows), 0)
    mine = users == owner_row
    before = jnp.dot(mine.astype(BF16), earlier_mask(rows), preferred_element_type=F32)
    rank = jnp.sum(jnp.where(mine, before, 0.0), axis=0, keepdims=True)
    return owner_row.astype(F32) * capacity + rank


def whole(count=1):
    return [pl.BlockSpec(memory_space=pltpu.VMEM)] * count


def unread(arrays):
    return [pl.BlockSpec(memory_space=pl.ANY)] * len(arrays)


def query_kernel(slot_ref, visible_ref, x_ref, w_ref, send_ref):
    rows, width = x_ref.shape
    slots = send_ref.shape[0]
    index = lax.broadcasted_iota(jnp.int32, (slots, rows), 0)
    place = (index == slot_ref[:1, :]).astype(BF16)
    seen = jnp.broadcast_to(visible_ref[...].astype(F32), (BLK, rows)).T.astype(BF16)
    send_ref[:, width:] = jnp.dot(place, seen, preferred_element_type=F32).astype(BF16)
    tile = min(256, width)
    for start in range(0, width, tile):
        span = slice(start, start + tile)
        hidden = jnp.dot(x_ref[...], w_ref[:, span], preferred_element_type=F32)
        moved = jnp.dot(place, silu(hidden).astype(BF16), preferred_element_type=F32)
        send_ref[:, span] = moved.astype(BF16)


def project_queries(slot, visible_row, cand_x, w_in, slots):
    rows, width = cand_x.shape
    return pl.pallas_call(
        query_kernel,
        in_specs=whole(4),
        out_specs=whole()[0],
        out_shape=jax.ShapeDtypeStruct((slots, width + BLK), BF16),
        compiler_params=params(KERNEL_MIB),
        cost_estimate=cost(
            2 * rows * width * width + 2 * slots * rows * width,
            2 * (rows * width + width * width + slots * width),
            rows * width,
        ),
        name="project_queries",
    )(slot, visible_row, cand_x, w_in)


def gate_kernel(x_ref, w_ref, gate_ref, token_ref):
    token_ref[...] = jnp.zeros_like(token_ref)
    width = x_ref.shape[1]
    tile = min(256, width)
    for start in range(0, width, tile):
        columns = w_ref[:, width + start : width + start + tile]
        hidden = jnp.dot(x_ref[...], columns, preferred_element_type=F32)
        gate_ref[:, start : start + tile] = silu(hidden).astype(BF16)


def project_gate(cand_x, w_in):
    rows, width = cand_x.shape
    return pl.pallas_call(
        gate_kernel,
        in_specs=whole(2),
        out_specs=whole(2),
        out_shape=[jax.ShapeDtypeStruct((rows, width), BF16), TOKEN],
        compiler_params=params(KERNEL_MIB),
        cost_estimate=cost(
            2 * rows * width * width, 2 * (2 * rows * width + width * width), rows * width
        ),
        name="project_gate",
    )(cand_x, w_in)


def prepare_kernel(columns, capacity, spans, size, owner_ref, kv_hbm, row_ref, *refs):
    part_refs, sems = refs[:-1], refs[-1]
    width = kv_hbm.shape[1] // 2
    copies = []
    for (first, heads), ref in zip(spans, part_refs):
        wide = heads * size
        for start in (0, width):
            source = kv_hbm.at[:, start + first * size : start + first * size + wide]
            target = ref.at[:, wide * (start > 0) : wide * (start > 0) + wide]
            copies.append(pltpu.make_async_copy(source, target, sems.at[len(copies)]))
    for copy in copies:
        copy.start()
    row = slot_row(owner_ref[...], columns, capacity)
    row_ref[...] = jnp.broadcast_to(row, row_ref.shape).astype(jnp.int32)
    for copy in copies:
        copy.wait()


def prepare(owner_row, kv, spans, size, columns, capacity):
    rows = kv.shape[0]
    return pl.pallas_call(
        functools.partial(prepare_kernel, columns, capacity, spans, size),
        in_specs=whole() + [pl.BlockSpec(memory_space=pl.ANY)],
        out_specs=whole(1 + len(spans)),
        out_shape=[jax.ShapeDtypeStruct((8, owner_row.shape[1]), jnp.int32)]
        + [jax.ShapeDtypeStruct((rows, 2 * heads * size), BF16) for _, heads in spans],
        scratch_shapes=[pltpu.SemaphoreType.DMA((2 * len(spans),))],
        compiler_params=params(KERNEL_MIB),
        cost_estimate=cost(SLOTS_COST * 1e9, 0),
        name="prepare",
    )(owner_row, kv)


def wait_kernel(*refs):
    refs[-1][...] = jnp.zeros_like(refs[-1])


def wait_for(arrays):
    return pl.pallas_call(
        wait_kernel,
        in_specs=unread(arrays),
        out_specs=whole()[0],
        out_shape=TOKEN,
        compiler_params=params(KERNEL_MIB),
        cost_estimate=cost(WAIT_COST * 1e9, 0),
        name="wait_for",
    )(*arrays)


def column_kernel(columns, capacity, owner_ref, *refs):
    column_ref, token_ref = refs[-2:]
    token_ref[...] = jnp.zeros_like(token_ref)
    row = slot_row(owner_ref[...], columns, capacity)
    column_ref[...] = jnp.broadcast_to(row, (BLK, row.shape[1])).T.astype(jnp.int32)


def slot_column(owner_row, columns, capacity, after):
    rows = owner_row.shape[1]
    return pl.pallas_call(
        functools.partial(column_kernel, columns, capacity),
        in_specs=whole() + unread(after),
        out_specs=whole(2),
        out_shape=[jax.ShapeDtypeStruct((rows, BLK), jnp.int32), TOKEN],
        compiler_params=params(KERNEL_MIB),
        cost_estimate=cost(WAIT_COST * 1e9, 4 * rows * BLK),
        name="slot_column",
    )(owner_row, *after)


def attend_kernel(size, heads, first, starts, behind, has_base, capacity, length_ref, *refs):
    refs = refs[behind:]
    rows_ref, refs = refs[0], refs[1:]
    count = len(starts)
    parts = []
    for _, _, _, pieces in starts:
        parts.append(refs[:pieces])
        refs = refs[pieces:]
    base_ref = refs[0] if has_base else None
    outs = 3 if capacity else 1
    out_refs, shown = refs[int(has_base) : int(has_base) + outs], refs[int(has_base) + outs]
    result = out_refs[0] if outs == 1 else refs[-1]
    me = lax.axis_index("cand")
    places = [lax.axis_index("user") ^ start[0] for start in starts]
    slots = rows_ref.shape[0]
    columns_of = slots // capacity if capacity else 1
    keys = sum(piece.shape[0] for piece in parts[0])
    blocks = keys // BLK
    seen = rows_ref[:, HEADS * size :].astype(F32)
    for number in range(count):
        for block in range(blocks):
            start = (places[number] * blocks + block).astype(F32)
            shown[number * blocks + block] = (start < seen).astype(F32).astype(BF16)
    row = lax.broadcasted_iota(jnp.int32, (keys, size), 0)
    tile = min(512, slots)

    def columns(start):
        return slice(start, start + size)

    def read(part, start):
        return jnp.concatenate([piece[:, columns(start)] for piece in part], axis=0)

    def one_head(head):
        values = []
        for number, part in enumerate(parts):
            inside = row + places[number] * keys < length_ref[0]
            value = read(part, (starts[number][2] + head) * size).astype(F32)
            values.append(jnp.where(inside, value, 0.0).astype(BF16))
        values = jnp.concatenate(values, axis=0)
        for start in range(0, slots, tile):
            span = slice(start, start + tile)
            queries = rows_ref[span, columns((first + head) * size)]
            weights = []
            for number, part in enumerate(parts):
                scores = lax.dot_general(
                    queries,
                    read(part, (starts[number][1] + head) * size),
                    (((1,), (1,)), ((), ())),
                    preferred_element_type=F32,
                )
                for block in range(blocks):
                    half = scores[:, block * BLK : (block + 1) * BLK] * (0.5 / math.sqrt(size))
                    half = half.astype(BF16) * shown[number * blocks + block, span, :]
                    weights.append(half * jnp.tanh(half) + half)
            total = jnp.dot(
                jnp.concatenate(weights, axis=1), values, preferred_element_type=F32
            )
            if has_base:
                total = total + base_ref[span, columns(head * size)]
            result[span, columns(head * size)] = total.astype(result.dtype)

    for head in range(heads):
        one_head(head)
    if outs > 1:
        numbers = list(range(0, columns_of, 2)) + list(range(1, columns_of, 2))
        for ref in out_refs:
            for start in range(0, ref.shape[0], capacity):
                block = me ^ numbers.pop(0)
                source = pl.ds(pl.multiple_of(block * capacity, capacity), capacity)
                ref[start : start + capacity, :] = result[source, :]


def attend(length, after, rows, segments, base, first, heads, size, capacity, dtype, share):
    slots = rows.shape[0]
    keys = sum(piece.shape[0] for piece in segments[0][1])
    count = len(segments)
    starts = [(place, key, value, len(pieces)) for place, pieces, key, value in segments]
    pieces = [piece for _, pieces, _, _ in segments for piece in pieces]
    heights = [slots // 2, slots // 4, slots // 4] if capacity else [slots]
    outs = len(heights)
    extra = [] if base is None else [base]
    scratch = [pltpu.VMEM((count * (keys // BLK), slots, BLK), BF16)]
    if outs > 1:
        scratch.append(pltpu.VMEM((slots, heads * size), BF16))
    return pl.pallas_call(
        functools.partial(
            attend_kernel, size, heads, first, starts, len(after), base is not None, capacity
        ),
        in_specs=[pl.BlockSpec(memory_space=pltpu.SMEM)]
        + unread(after)
        + whole(1 + len(pieces) + len(extra)),
        out_specs=whole(outs),
        out_shape=[jax.ShapeDtypeStruct((height, heads * size), dtype) for height in heights],
        scratch_shapes=scratch,
        compiler_params=params(KERNEL_MIB),
        cost_estimate=cost(
            share * 4 * slots * keys * count * heads * size,
            2 * (2 * slots + count * keys * 2) * heads * size,
            slots * keys * count * heads,
        ),
        name="attend",
    )(length, *after, rows, *pieces, *extra)


def placement(slot, slots):
    lane = lax.broadcasted_iota(jnp.int32, (1, BLK), 1)
    return jnp.concatenate(
        [(lane + start == slot).astype(BF16) for start in range(0, slots, BLK)], axis=1
    )


def in_slots(parts, capacity):
    return jnp.concatenate(
        [part[:capacity, :] for part in parts[:2]] + [part[...] for part in parts[2:]], axis=0
    )


def collect_kernel(capacity, slots, slot_ref, *refs):
    rows = in_slots(refs[:-2], capacity)
    place = placement(slot_ref[...], slots)
    refs[-1][...] = jnp.dot(place, rows, preferred_element_type=F32).astype(BF16)


def collect(slot, parts, after, capacity, slots):
    rows, width = slot.shape[0], parts[0].shape[1]
    return pl.pallas_call(
        functools.partial(collect_kernel, capacity, slots),
        in_specs=whole(1 + len(parts)) + unread([after]),
        out_specs=whole()[0],
        out_shape=jax.ShapeDtypeStruct((rows, width), BF16),
        compiler_params=params(KERNEL_MIB),
        cost_estimate=cost(2 * rows * slots * width, 2 * (rows + slots) * width),
        name="collect",
    )(slot, *parts, after)


def finish_kernel(groups, capacity, slots, slot_ref, gain_ref, gate_ref, x_ref, w_ref, *refs):
    early, parts, (out_hbm, out_ref, sems) = refs[:groups], refs[groups:-3], refs[-3:]
    rows = x_ref.shape[0]
    place = placement(slot_ref[...], slots)
    late = jnp.dot(place, in_slots(parts, capacity), preferred_element_type=F32)
    tile = rows // 2
    stores = []
    for half in range(2):
        span = slice(half * tile, (half + 1) * tile)
        attn = jnp.concatenate([part[span, :].astype(F32) for part in early] + [late[span, :]], axis=1)
        centered = attn - jnp.mean(attn, axis=1, keepdims=True)
        variance = jnp.mean(centered * centered, axis=1, keepdims=True)
        normed = (centered * lax.rsqrt(variance + norm_eps) * gain_ref[...]).astype(BF16)
        mixed = (normed.astype(F32) * gate_ref[span, :].astype(F32)).astype(BF16)
        projected = jnp.dot(mixed, w_ref[...], preferred_element_type=F32)
        out_ref[span, :] = (x_ref[span, :].astype(F32) + projected).astype(BF16)
        store = pltpu.make_async_copy(out_ref.at[span, :], out_hbm.at[span, :], sems.at[half])
        store.start()
        stores.append(store)
    for store in stores:
        store.wait()


def finish(slot, early, gate, cand_x, ln_gain, w_out, parts, capacity, slots):
    rows, width = cand_x.shape
    return pl.pallas_call(
        functools.partial(finish_kernel, len(early), capacity, slots),
        in_specs=whole(5 + len(early) + len(parts)),
        out_specs=pl.BlockSpec(memory_space=pl.ANY),
        out_shape=jax.ShapeDtypeStruct((rows, width), BF16),
        scratch_shapes=[pltpu.VMEM((rows, width), BF16), pltpu.SemaphoreType.DMA((2,))],
        compiler_params=params(KERNEL_MIB),
        cost_estimate=cost(
            2 * rows * width * (width + slots), 2 * (3 * rows * width + width * width + slots * width)
        ),
        name="finish",
    )(slot, ln_gain.reshape(1, width), gate, cand_x, w_out, *early, *parts)


def swap(array, axis, bits, count):
    return lax.ppermute(array, axis, [(i, i ^ bits) for i in range(count)])


def exchange_cores(even, odds, capacity, count, behind):
    others = [swap(odd, "cand", 1, count) for odd in odds]
    if behind is not None:
        (even, others), _ = lax.optimization_barrier(((even, others), behind))
    pairs = []
    for d in range(1, count // 2):
        first, second = d * capacity, (d * capacity) % odds[0].shape[0]
        other = others[first // odds[0].shape[0]]
        pairs.append(
            jnp.concatenate(
                [even[first : first + capacity], other[second : second + capacity]], axis=0
            )
        )
    return [even, others[0]], pairs


def exchange_chips(pairs, count):
    return [swap(pair, "cand", 2 * d, count) for d, pair in enumerate(pairs, 1)]


def per_device(cand_x, cand_user, visible, hist_len, kv_cache, w_in, w_out, ln_gain):
    rows, width = cand_x.shape
    columns = lax.axis_size("cand")
    count = lax.axis_size("user")
    size = width // HEADS
    capacity = 2 * rows // columns
    slots = columns * capacity
    me = lax.axis_index("cand").astype(jnp.int32)
    owner_row = cand_user.reshape(1, rows)
    visible_row = visible.reshape(1, rows)
    spans = [(sum(GROUPS[:number]), heads) for number, heads in enumerate(GROUPS)]

    gate, gated = project_gate(cand_x, w_in)
    row, *parts = prepare(owner_row, kv_cache[0], spans, size, columns, capacity)
    send = project_queries(row, visible_row, cand_x, w_in, slots)
    near = None
    far = []
    for part in parts:
        if far:
            part, _ = lax.optimization_barrier((part, send))
        held = {0: part}
        bit = count // 2
        while bit > 1:
            for key in sorted(held):
                held[key | bit] = swap(held[key], "user", bit, count)
            bit //= 2
        if near is None:
            own, _ = lax.optimization_barrier((kv_cache[0], row))
            near = swap(own, "user", 1, count)
        far.append(held)
    evens = sorted(far[0])

    got = lax.all_to_all(
        send.reshape(columns, capacity, -1), "cand", split_axis=0, concat_axis=0, tiled=True
    ).reshape(slots, -1)
    arrived = [gated, near] + [held[key] for held in far for key in evens[1:]]
    slot, started = slot_column(owner_row ^ me, columns, capacity, arrived)
    early = []
    after = [started]
    behind = None
    for number, (first, heads) in enumerate(spans):
        held = far[number]
        cuts = [(key | 1, [swap(held[key], "user", 1, count)], 0, heads) for key in evens[1:]]
        segments = [(key, [held[key]], 0, heads) for key in evens]
        segments.append((1, [near], first, HEADS + first))
        base = attend(
            hist_len, after, got, segments, None, first, heads, size, None, F32, 0.0
        )[0]
        attn = attend(
            hist_len,
            [],
            got,
            cuts,
            base,
            first,
            heads,
            size,
            capacity,
            BF16,
            LATE_SHARE * (number > 0),
        )
        here, pairs = exchange_cores(attn[0], attn[1:], capacity, columns, behind)
        away = exchange_chips(pairs, columns)
        if number + 1 < len(spans):
            token = wait_for([attn[0]] + [far[number + 1][key] for key in evens[1:]])
            after = [token] + pairs
            behind = wait_for(away)
            early.append(collect(slot, here + away, behind, capacity, slots))
    return finish(slot, early, gate, cand_x, ln_gain, w_out, here + away, capacity, slots)


def solution(mesh):
    in_specs = (
        P(("user", "cand"), None),
        P(("user", "cand"), None),
        P(("user", "cand")),
        P("cand"),
        P("cand", "user", None),
        P(),
        P(),
        P(),
    )
    out_specs = P(("user", "cand"), None)
    return jax.shard_map(
        per_device, mesh=mesh, in_specs=in_specs, out_specs=out_specs, check_vma=False
    )
```

```python
import functools
import math

import jax
import jax.numpy as jnp
from jax import lax
from jax.experimental import pallas as pl
from jax.experimental.pallas import tpu as pltpu
from jax.sharding import PartitionSpec as P

HEADS = 8
BLK = 128
GROUPS = (4, 4)
norm_eps = 1e-06
F32 = jnp.float32
BF16 = jnp.bfloat16
MIB = 1024 * 1024
TOKEN = jax.ShapeDtypeStruct((8, BLK), jnp.int32)
WAIT_COST = 20.0
LATE_SHARE = 20.0
SLOTS_COST = 6.0
KERNEL_MIB = 24


def params(mib):
    return pltpu.CompilerParams(vmem_limit_bytes=mib * MIB)


def cost(flops, nbytes, transcendentals=0):
    return pl.CostEstimate(
        flops=int(flops), bytes_accessed=int(nbytes), transcendentals=int(transcendentals)
    )


def silu(v):
    half = 0.5 * v
    return half * jnp.tanh(half) + half


def earlier_mask(rows):
    first = lax.broadcasted_iota(jnp.int32, (rows, rows), 0)
    second = lax.broadcasted_iota(jnp.int32, (rows, rows), 1)
    return (first < second).astype(BF16)


def slot_row(owner_row, columns, capacity):
    rows = owner_row.shape[1]
    users = lax.broadcasted_iota(jnp.int32, (columns, rows), 0)
    mine = users == owner_row
    before = jnp.dot(mine.astype(BF16), earlier_mask(rows), preferred_element_type=F32)
    rank = jnp.sum(jnp.where(mine, before, 0.0), axis=0, keepdims=True)
    return owner_row.astype(F32) * capacity + rank


def whole(count=1):
    return [pl.BlockSpec(memory_space=pltpu.VMEM)] * count


def unread(arrays):
    return [pl.BlockSpec(memory_space=pl.ANY)] * len(arrays)


def query_kernel(slot_ref, visible_ref, x_ref, w_ref, send_ref):
    rows, width = x_ref.shape
    slots = send_ref.shape[0]
    index = lax.broadcasted_iota(jnp.int32, (slots, rows), 0)
    place = (index == slot_ref[:1, :]).astype(BF16)
    seen = jnp.broadcast_to(visible_ref[...].astype(F32), (BLK, rows)).T.astype(BF16)
    send_ref[:, width:] = jnp.dot(place, seen, preferred_element_type=F32).astype(BF16)
    tile = min(256, width)
    for start in range(0, width, tile):
        span = slice(start, start + tile)
        hidden = jnp.dot(x_ref[...], w_ref[:, span], preferred_element_type=F32)
        moved = jnp.dot(place, silu(hidden).astype(BF16), preferred_element_type=F32)
        send_ref[:, span] = moved.astype(BF16)


def project_queries(slot, visible_row, cand_x, w_in, slots):
    rows, width = cand_x.shape
    return pl.pallas_call(
        query_kernel,
        in_specs=whole(4),
        out_specs=whole()[0],
        out_shape=jax.ShapeDtypeStruct((slots, width + BLK), BF16),
        compiler_params=params(KERNEL_MIB),
        cost_estimate=cost(
            2 * rows * width * width + 2 * slots * rows * width,
            2 * (rows * width + width * width + slots * width),
            rows * width,
        ),
        name="project_queries",
    )(slot, visible_row, cand_x, w_in)


def gate_kernel(x_ref, w_ref, gate_ref, token_ref):
    token_ref[...] = jnp.zeros_like(token_ref)
    width = x_ref.shape[1]
    tile = min(256, width)
    for start in range(0, width, tile):
        columns = w_ref[:, width + start : width + start + tile]
        hidden = jnp.dot(x_ref[...], columns, preferred_element_type=F32)
        gate_ref[:, start : start + tile] = silu(hidden).astype(BF16)


def project_gate(cand_x, w_in):
    rows, width = cand_x.shape
    return pl.pallas_call(
        gate_kernel,
        in_specs=whole(2),
        out_specs=whole(2),
        out_shape=[jax.ShapeDtypeStruct((rows, width), BF16), TOKEN],
        compiler_params=params(KERNEL_MIB),
        cost_estimate=cost(
            2 * rows * width * width, 2 * (2 * rows * width + width * width), rows * width
        ),
        name="project_gate",
    )(cand_x, w_in)


def prepare_kernel(columns, capacity, spans, size, owner_ref, kv_hbm, row_ref, *refs):
    part_refs, sems = refs[:-1], refs[-1]
    width = kv_hbm.shape[1] // 2
    copies = []
    for (first, heads), ref in zip(spans, part_refs):
        wide = heads * size
        for start in (0, width):
            source = kv_hbm.at[:, start + first * size : start + first * size + wide]
            target = ref.at[:, wide * (start > 0) : wide * (start > 0) + wide]
            copies.append(pltpu.make_async_copy(source, target, sems.at[len(copies)]))
    for copy in copies:
        copy.start()
    row = slot_row(owner_ref[...], columns, capacity)
    row_ref[...] = jnp.broadcast_to(row, row_ref.shape).astype(jnp.int32)
    for copy in copies:
        copy.wait()


def prepare(owner_row, kv, spans, size, columns, capacity):
    rows = kv.shape[0]
    return pl.pallas_call(
        functools.partial(prepare_kernel, columns, capacity, spans, size),
        in_specs=whole() + [pl.BlockSpec(memory_space=pl.ANY)],
        out_specs=whole(1 + len(spans)),
        out_shape=[jax.ShapeDtypeStruct((8, owner_row.shape[1]), jnp.int32)]
        + [jax.ShapeDtypeStruct((rows, 2 * heads * size), BF16) for _, heads in spans],
        scratch_shapes=[pltpu.SemaphoreType.DMA((2 * len(spans),))],
        compiler_params=params(KERNEL_MIB),
        cost_estimate=cost(SLOTS_COST * 1e9, 0),
        name="prepare",
    )(owner_row, kv)


def wait_kernel(*refs):
    refs[-1][...] = jnp.zeros_like(refs[-1])


def wait_for(arrays):
    return pl.pallas_call(
        wait_kernel,
        in_specs=unread(arrays),
        out_specs=whole()[0],
        out_shape=TOKEN,
        compiler_params=params(KERNEL_MIB),
        cost_estimate=cost(WAIT_COST * 1e9, 0),
        name="wait_for",
    )(*arrays)


def column_kernel(columns, capacity, owner_ref, *refs):
    column_ref, token_ref = refs[-2:]
    token_ref[...] = jnp.zeros_like(token_ref)
    row = slot_row(owner_ref[...], columns, capacity)
    column_ref[...] = jnp.broadcast_to(row, (BLK, row.shape[1])).T.astype(jnp.int32)


def slot_column(owner_row, columns, capacity, after):
    rows = owner_row.shape[1]
    return pl.pallas_call(
        functools.partial(column_kernel, columns, capacity),
        in_specs=whole() + unread(after),
        out_specs=whole(2),
        out_shape=[jax.ShapeDtypeStruct((rows, BLK), jnp.int32), TOKEN],
        compiler_params=params(KERNEL_MIB),
        cost_estimate=cost(WAIT_COST * 1e9, 4 * rows * BLK),
        name="slot_column",
    )(owner_row, *after)


def attend_kernel(size, heads, first, starts, behind, has_base, capacity, length_ref, *refs):
    refs = refs[behind:]
    rows_ref, refs = refs[0], refs[1:]
    count = len(starts)
    parts = []
    for _, _, _, pieces in starts:
        parts.append(refs[:pieces])
        refs = refs[pieces:]
    base_ref = refs[0] if has_base else None
    outs = 3 if capacity else 1
    out_refs, shown = refs[int(has_base) : int(has_base) + outs], refs[int(has_base) + outs]
    result = out_refs[0] if outs == 1 else refs[-1]
    me = lax.axis_index("cand")
    places = [lax.axis_index("user") ^ start[0] for start in starts]
    slots = rows_ref.shape[0]
    columns_of = slots // capacity if capacity else 1
    keys = sum(piece.shape[0] for piece in parts[0])
    blocks = keys // BLK
    seen = rows_ref[:, HEADS * size :].astype(F32)
    for number in range(count):
        for block in range(blocks):
            start = (places[number] * blocks + block).astype(F32)
            shown[number * blocks + block] = (start < seen).astype(F32).astype(BF16)
    row = lax.broadcasted_iota(jnp.int32, (keys, size), 0)
    tile = min(512, slots)

    def columns(start):
        return slice(start, start + size)

    def read(part, start):
        return jnp.concatenate([piece[:, columns(start)] for piece in part], axis=0)

    def one_head(head):
        values = []
        for number, part in enumerate(parts):
            inside = row + places[number] * keys < length_ref[0]
            value = read(part, (starts[number][2] + head) * size).astype(F32)
            values.append(jnp.where(inside, value, 0.0).astype(BF16))
        values = jnp.concatenate(values, axis=0)
        for start in range(0, slots, tile):
            span = slice(start, start + tile)
            queries = rows_ref[span, columns((first + head) * size)]
            weights = []
            for number, part in enumerate(parts):
                scores = lax.dot_general(
                    queries,
                    read(part, (starts[number][1] + head) * size),
                    (((1,), (1,)), ((), ())),
                    preferred_element_type=F32,
                )
                for block in range(blocks):
                    half = scores[:, block * BLK : (block + 1) * BLK] * (0.5 / math.sqrt(size))
                    half = half.astype(BF16) * shown[number * blocks + block, span, :]
                    weights.append(half * jnp.tanh(half) + half)
            total = jnp.dot(
                jnp.concatenate(weights, axis=1), values, preferred_element_type=F32
            )
            if has_base:
                total = total + base_ref[span, columns(head * size)]
            result[span, columns(head * size)] = total.astype(result.dtype)

    for head in range(heads):
        one_head(head)
    if outs > 1:
        numbers = list(range(0, columns_of, 2)) + list(range(1, columns_of, 2))
        for ref in out_refs:
            for start in range(0, ref.shape[0], capacity):
                block = me ^ numbers.pop(0)
                source = pl.ds(pl.multiple_of(block * capacity, capacity), capacity)
                ref[start : start + capacity, :] = result[source, :]


def attend(length, after, rows, segments, base, first, heads, size, capacity, dtype, share):
    slots = rows.shape[0]
    keys = sum(piece.shape[0] for piece in segments[0][1])
    count = len(segments)
    starts = [(place, key, value, len(pieces)) for place, pieces, key, value in segments]
    pieces = [piece for _, pieces, _, _ in segments for piece in pieces]
    heights = [slots // 2, slots // 4, slots // 4] if capacity else [slots]
    outs = len(heights)
    extra = [] if base is None else [base]
    scratch = [pltpu.VMEM((count * (keys // BLK), slots, BLK), BF16)]
    if outs > 1:
        scratch.append(pltpu.VMEM((slots, heads * size), BF16))
    return pl.pallas_call(
        functools.partial(
            attend_kernel, size, heads, first, starts, len(after), base is not None, capacity
        ),
        in_specs=[pl.BlockSpec(memory_space=pltpu.SMEM)]
        + unread(after)
        + whole(1 + len(pieces) + len(extra)),
        out_specs=whole(outs),
        out_shape=[jax.ShapeDtypeStruct((height, heads * size), dtype) for height in heights],
        scratch_shapes=scratch,
        compiler_params=params(KERNEL_MIB),
        cost_estimate=cost(
            share * 4 * slots * keys * count * heads * size,
            2 * (2 * slots + count * keys * 2) * heads * size,
            slots * keys * count * heads,
        ),
        name="attend",
    )(length, *after, rows, *pieces, *extra)


def placement(slot, slots):
    lane = lax.broadcasted_iota(jnp.int32, (1, BLK), 1)
    return jnp.concatenate(
        [(lane + start == slot).astype(BF16) for start in range(0, slots, BLK)], axis=1
    )


def in_slots(parts, capacity):
    return jnp.concatenate(
        [part[:capacity, :] for part in parts[:2]] + [part[...] for part in parts[2:]], axis=0
    )


def collect_kernel(capacity, slots, slot_ref, *refs):
    rows = in_slots(refs[:-2], capacity)
    place = placement(slot_ref[...], slots)
    refs[-1][...] = jnp.dot(place, rows, preferred_element_type=F32).astype(BF16)


def collect(slot, parts, after, capacity, slots):
    rows, width = slot.shape[0], parts[0].shape[1]
    return pl.pallas_call(
        functools.partial(collect_kernel, capacity, slots),
        in_specs=whole(1 + len(parts)) + unread([after]),
        out_specs=whole()[0],
        out_shape=jax.ShapeDtypeStruct((rows, width), BF16),
        compiler_params=params(KERNEL_MIB),
        cost_estimate=cost(2 * rows * slots * width, 2 * (rows + slots) * width),
        name="collect",
    )(slot, *parts, after)


def finish_kernel(groups, capacity, slots, slot_ref, gain_ref, gate_ref, x_ref, w_ref, *refs):
    early, parts, (out_hbm, out_ref, sems) = refs[:groups], refs[groups:-3], refs[-3:]
    rows = x_ref.shape[0]
    place = placement(slot_ref[...], slots)
    late = jnp.dot(place, in_slots(parts, capacity), preferred_element_type=F32)
    tile = rows // 2
    stores = []
    for half in range(2):
        span = slice(half * tile, (half + 1) * tile)
        attn = jnp.concatenate([part[span, :].astype(F32) for part in early] + [late[span, :]], axis=1)
        centered = attn - jnp.mean(attn, axis=1, keepdims=True)
        variance = jnp.mean(centered * centered, axis=1, keepdims=True)
        normed = (centered * lax.rsqrt(variance + norm_eps) * gain_ref[...]).astype(BF16)
        mixed = (normed.astype(F32) * gate_ref[span, :].astype(F32)).astype(BF16)
        projected = jnp.dot(mixed, w_ref[...], preferred_element_type=F32)
        out_ref[span, :] = (x_ref[span, :].astype(F32) + projected).astype(BF16)
        store = pltpu.make_async_copy(out_ref.at[span, :], out_hbm.at[span, :], sems.at[half])
        store.start()
        stores.append(store)
    for store in stores:
        store.wait()


def finish(slot, early, gate, cand_x, ln_gain, w_out, parts, capacity, slots):
    rows, width = cand_x.shape
    return pl.pallas_call(
        functools.partial(finish_kernel, len(early), capacity, slots),
        in_specs=whole(5 + len(early) + len(parts)),
        out_specs=pl.BlockSpec(memory_space=pl.ANY),
        out_shape=jax.ShapeDtypeStruct((rows, width), BF16),
        scratch_shapes=[pltpu.VMEM((rows, width), BF16), pltpu.SemaphoreType.DMA((2,))],
        compiler_params=params(KERNEL_MIB),
        cost_estimate=cost(
            2 * rows * width * (width + slots), 2 * (3 * rows * width + width * width + slots * width)
        ),
        name="finish",
    )(slot, ln_gain.reshape(1, width), gate, cand_x, w_out, *early, *parts)


def swap(array, axis, bits, count):
    return lax.ppermute(array, axis, [(i, i ^ bits) for i in range(count)])


def exchange_cores(even, odds, capacity, count, behind):
    others = [swap(odd, "cand", 1, count) for odd in odds]
    if behind is not None:
        (even, others), _ = lax.optimization_barrier(((even, others), behind))
    pairs = []
    for d in range(1, count // 2):
        first, second = d * capacity, (d * capacity) % odds[0].shape[0]
        other = others[first // odds[0].shape[0]]
        pairs.append(
            jnp.concatenate(
                [even[first : first + capacity], other[second : second + capacity]], axis=0
            )
        )
    return [even, others[0]], pairs


def exchange_chips(pairs, count):
    return [swap(pair, "cand", 2 * d, count) for d, pair in enumerate(pairs, 1)]


def per_device(cand_x, cand_user, visible, hist_len, kv_cache, w_in, w_out, ln_gain):
    rows, width = cand_x.shape
    columns = lax.axis_size("cand")
    count = lax.axis_size("user")
    size = width // HEADS
    capacity = 2 * rows // columns
    slots = columns * capacity
    me = lax.axis_index("cand").astype(jnp.int32)
    owner_row = cand_user.reshape(1, rows)
    visible_row = visible.reshape(1, rows)
    spans = [(sum(GROUPS[:number]), heads) for number, heads in enumerate(GROUPS)]

    gate, gated = project_gate(cand_x, w_in)
    row, *parts = prepare(owner_row, kv_cache[0], spans, size, columns, capacity)
    send = project_queries(row, visible_row, cand_x, w_in, slots)
    near = None
    far = []
    for part in parts:
        if far:
            part, _ = lax.optimization_barrier((part, send))
        held = {0: part}
        bit = count // 2
        while bit > 1:
            for key in sorted(held):
                held[key | bit] = swap(held[key], "user", bit, count)
            bit //= 2
        if near is None:
            own, _ = lax.optimization_barrier((kv_cache[0], row))
            near = swap(own, "user", 1, count)
        far.append(held)
    evens = sorted(far[0])

    got = lax.all_to_all(
        send.reshape(columns, capacity, -1), "cand", split_axis=0, concat_axis=0, tiled=True
    ).reshape(slots, -1)
    arrived = [gated, near] + [held[key] for held in far for key in evens[1:]]
    slot, started = slot_column(owner_row ^ me, columns, capacity, arrived)
    early = []
    after = [started]
    behind = None
    for number, (first, heads) in enumerate(spans):
        held = far[number]
        passed = [held[key] for key in evens[1:]]
        if number:
            passed, _ = lax.optimization_barrier((passed, attn[0]))
        cuts = [
            (key | 1, [swap(part, "user", 1, count)], 0, heads)
            for key, part in zip(evens[1:], passed)
        ]
        segments = [(key, [held[key]], 0, heads) for key in evens]
        segments.append((1, [near], first, HEADS + first))
        base = attend(
            hist_len, after, got, segments, None, first, heads, size, None, F32, 0.0
        )[0]
        attn = attend(
            hist_len,
            [],
            got,
            cuts,
            base,
            first,
            heads,
            size,
            capacity,
            BF16,
            LATE_SHARE * (number > 0),
        )
        here, pairs = exchange_cores(attn[0], attn[1:], capacity, columns, behind)
        away = exchange_chips(pairs, columns)
        if number + 1 < len(spans):
            token = wait_for([attn[0]] + [far[number + 1][key] for key in evens[1:]])
            after = [token] + pairs
            behind = wait_for(away)
            early.append(collect(slot, here + away, behind, capacity, slots))
    return finish(slot, early, gate, cand_x, ln_gain, w_out, here + away, capacity, slots)


def solution(mesh):
    in_specs = (
        P(("user", "cand"), None),
        P(("user", "cand"), None),
        P(("user", "cand")),
        P("cand"),
        P("cand", "user", None),
        P(),
        P(),
        P(),
    )
    out_specs = P(("user", "cand"), None)
    return jax.shard_map(
        per_device, mesh=mesh, in_specs=in_specs, out_specs=out_specs, check_vma=False
    )
```
